128 devices in a mesh: section: 2 (over y_hi), fsdp: 64 (over x, y_lo, z, core).
Axes of the slice: x: 4, y: 4 (y_hi: 2, y_lo: 2; y = y_hi * 2 + y_lo), z: 4, core: 2. Of those that a mesh axis runs over, the one named last changes fastest.
Arguments:
- tokens_in: bfloat16 [2, 64, 128, 896], P(None, 'fsdp'), may hold values from -6 to 6
- out_grad: bfloat16 [2, 64, 128, 896], P(None, 'fsdp'), may hold values from -6 to 6
- segments: int32 [2, 64, 128], P(None, 'fsdp'), may hold values from 0 to 3, never falling along the last dimension, each value on 1 to 64 neighbouring positions
- norm1_gain: bfloat16 [2, 896], P('section', 'fsdp'), may hold values from 0.099609375 to 1.8984375
- qkv_weight: bfloat16 [2, 896, 1152], P('section', 'fsdp'), may hold values from -0.1875 to 0.1875
- qkv_bias: bfloat16 [2, 1152], P('section', 'fsdp'), may hold values from -3 to 3
- out_weight: bfloat16 [2, 896, 896], P('section', 'fsdp'), may hold values from -0.75 to 0.75
- norm2_gain: bfloat16 [2, 896], P('section', 'fsdp'), may hold values from 0.099609375 to 1.8984375
- gate_weight: bfloat16 [2, 896, 4864], P('section', 'fsdp'), may hold values from -0.1875 to 0.1875
- up_weight: bfloat16 [2, 896, 4864], P('section', 'fsdp'), may hold values from -0.1875 to 0.1875
- down_weight: bfloat16 [2, 4864, 896], P('section', 'fsdp'), may hold values from -0.078125 to 0.078125
Outputs:
- section_out: bfloat16 [2, 2, 64, 128, 896], P('section', None, 'fsdp')
- section_in_grad: bfloat16 [2, 2, 64, 128, 896], P('section', None, 'fsdp')
- norm1_gain_grad: float32 [2, 896], P('section', 'fsdp')
- qkv_weight_grad: float32 [2, 896, 1152], P('section', 'fsdp')
- qkv_bias_grad: float32 [2, 1152], P('section', 'fsdp')
- out_weight_grad: float32 [2, 896, 896], P('section', 'fsdp')
- norm2_gain_grad: float32 [2, 896], P('section', 'fsdp')
- gate_weight_grad: float32 [2, 896, 4864], P('section', 'fsdp')
- up_weight_grad: float32 [2, 896, 4864], P('section', 'fsdp')
- down_weight_grad: float32 [2, 4864, 896], P('section', 'fsdp')
The draws below stay inside these ranges and needn't reach their ends.
Inputs may be any that keep to these rules, and one draw needn't show every extreme that they name: `segments`: along each sequence the segment numbers never fall; a document covers at most 64 tokens of its sequence, and some document covers exactly that many.
All inputs are finite; a program needn't handle non-finite values.
Results may differ from the reference program's by a relative error of at most 0.023.
Values may be sent and summed in bfloat16 or wider, within the bound.
A program may use at most 192 MiB of HBM per device.

```python
import math
import jax
import jax.numpy as jnp
import numpy as np
from jax import lax

D = 896
HEADS = 14
KV_HEADS = 2
HEAD_DIM = 64
FF = 4864
QKV = 1152
SEQ_LEN = 128
MICRO = 2
SEQS = 64
SECTIONS = 2


def block_levels(rng, dims, cuts, low, largest):
    level = 1.0
    for dim, shards_of in cuts:
        heights = jax.random.uniform(jax.random.fold_in(jax.random.fold_in(rng, 6), dim), (shards_of,), jnp.float32, low / len(cuts), largest / len(cuts))
        level = level * jnp.repeat(jnp.exp(heights), dims[dim] // shards_of).reshape((-1,) + (1,) * (len(dims) - 1 - dim))
    return level


def length_profile(number_of, total, most, skew):
    loads = [(1 << 20) // math.isqrt(grade ** skew) + 1 for grade in range(2, number_of + 1)]
    rest, holding = total - most - (number_of - 1), [1] * (number_of - 1)
    while rest > 0:
        free = [i for i in range(number_of - 1) if holding[i] < most]
        pool, budget = sum([loads[i] for i in free]), rest
        for i in free:
            extra = min(most - holding[i], max(1, budget * loads[i] // pool), rest)
            holding[i] = holding[i] + extra
            rest = rest - extra
    return np.array([most] + holding)


def ragged(rng, number_of, total, bound, skew):
    if number_of == 2:
        one = jax.random.randint(rng, (), max(1, total - bound), min(bound, total - 1) + 1)
        return jnp.stack([one, total - one])
    lengths = jnp.asarray(length_profile(number_of, total, bound, skew), jnp.int32)
    twos = (number_of - 1) // 2
    source_of, receiver = lengths[1:1 + 2 * twos:2], lengths[2:2 + 2 * twos:2]
    slack = jnp.minimum(source_of - 1, bound - receiver)
    passed = jax.random.randint(jax.random.fold_in(rng, 1), (twos,), 0, 1 << 20) % (slack + 1)
    lengths = lengths.at[1:1 + 2 * twos:2].set(source_of - passed).at[2:2 + 2 * twos:2].set(receiver + passed)
    return lengths[jax.random.permutation(jax.random.fold_in(rng, 2), number_of)]


def scatter_about(own_key, extent, spread, most, cuts=(), kind=jnp.bfloat16):
    array = spread * jax.random.normal(own_key, extent, jnp.float32)
    if cuts:
        array = array * block_levels(own_key, extent, cuts, -0.22, 0.18)
    return jnp.clip(array, -most, most).astype(kind)


def setup_inputs(seed: int = 0) -> dict:
    seeds = jax.random.split(jax.random.key(seed), 12)
    return {
        "tokens_in": scatter_about(seeds[0], (MICRO, SEQS, SEQ_LEN, D), 1.0, 6.0, ((1, 64),)),
        "out_grad": scatter_about(seeds[1], (MICRO, SEQS, SEQ_LEN, D), 1.0, 6.0, ((1, 64),)),
        "segments": jax.vmap(lambda own: jnp.searchsorted(jnp.cumsum(ragged(own, 4, SEQ_LEN, SEQ_LEN // 2, 1)), jnp.arange(SEQ_LEN), side="right"))(jax.random.split(seeds[2], MICRO * SEQS)).reshape((MICRO, SEQS, SEQ_LEN)).astype(jnp.int32),
        "norm1_gain": jnp.clip(1.0 + 0.18 * jax.random.normal(seeds[3], (SECTIONS, D), jnp.float32), 0.099609375, 1.8984375).astype(jnp.bfloat16),
        "qkv_weight": scatter_about(seeds[4], (SECTIONS, D, QKV), D ** -0.5, 0.1875, ((0, 2), (1, 64))),
        "qkv_bias": scatter_about(seeds[5], (SECTIONS, QKV), 0.5, 3.0, ((0, 2), (1, 64))),
        "out_weight": scatter_about(seeds[6], (SECTIONS, D, D), (D // 16) ** -0.5, 0.75, ((0, 2), (1, 64))),
        "norm2_gain": jnp.clip(1.0 + 0.18 * jax.random.normal(seeds[7], (SECTIONS, D), jnp.float32), 0.099609375, 1.8984375).astype(jnp.bfloat16),
        "gate_weight": scatter_about(seeds[8], (SECTIONS, D, FF), D ** -0.5, 0.1875, ((0, 2), (1, 64))),
        "up_weight": scatter_about(seeds[9], (SECTIONS, D, FF), D ** -0.5, 0.1875, ((0, 2), (1, 64))),
        "down_weight": scatter_about(seeds[10], (SECTIONS, FF, D), FF ** -0.5, 0.078125, ((0, 2), (1, 64))),
    }


norm_epsilon = 1e-06
rope_base = 1000000.0

@jax.custom_vjp
def low(v):
    return lax.optimization_barrier(v.astype(jnp.bfloat16)).astype(jnp.float32)

@jax.custom_vjp
def low_back(v):
    return v

def low_keep(v):
    return (low(v), None)

def low_pass(kept, grad):
    return (grad,)

def back_keep(v):
    return (v, None)

def back_low(kept, grad):
    return (low(grad),)
low.defvjp(low_keep, low_pass)
low_back.defvjp(back_keep, back_low)

def rope_tables(segment_row, head_size):
    length = segment_row.shape[0]
    places = jnp.arange(length, dtype=jnp.int32)
    changes = jnp.concatenate([jnp.ones((1,), jnp.int32), (segment_row[1:] != segment_row[:-1]).astype(jnp.int32)])
    starts = lax.cummax(places * changes, axis=0)
    offsets = (places - starts).astype(jnp.float32)
    ladder = jnp.arange(head_size // 2, dtype=jnp.float32) * (-2.0 * math.log(rope_base) / head_size)
    angles = offsets[:, None] * jnp.exp(ladder)[None, :]
    angles = jnp.concatenate([angles, angles], axis=-1)
    return (jnp.cos(angles), jnp.sin(angles))

def rotate_half(head_block):
    half_width = head_block.shape[-1] // 2
    return jnp.concatenate([-head_block[..., half_width:], head_block[..., :half_width]], axis=-1)

def spin(head_block, cosine_table, sine_table):
    return head_block * cosine_table + rotate_half(head_block) * sine_table

def matmul(left_rows, right_rows):
    return jnp.einsum('...a,ab->...b', left_rows, right_rows, precision=lax.Precision.HIGHEST)

def visible(segment_row):
    places = jnp.arange(segment_row.shape[0], dtype=jnp.int32)
    return (segment_row[:, None] == segment_row[None, :]) & (places[None, :] <= places[:, None])

def attend_one(pieces):
    query_block, key_block, value_block, segment_row = pieces
    length = query_block.shape[0]
    groups = HEADS // KV_HEADS
    query_group = query_block.reshape(length, KV_HEADS, groups, HEAD_DIM)
    scores = jnp.einsum('qkgd,skd->kgqs', query_group, key_block, precision=lax.Precision.HIGHEST) * HEAD_DIM ** (-0.5)
    scores = low_back(jnp.where(visible(segment_row)[None, None], scores, -1e+30))
    attn_probs = low(jax.nn.softmax(scores, axis=-1))
    context = jnp.einsum('kgqs,skd->qkgd', attn_probs, value_block, precision=lax.Precision.HIGHEST)
    return context.reshape(length, HEADS * HEAD_DIM)

def layer(stream, weights, segment_rows, cosine_table, sine_table):
    gain_one, w_qkv, b_qkv, w_out, gain_two, w_gate, w_up, w_down = weights
    seq_count, length, model_width = stream.shape
    pair_width = KV_HEADS * HEAD_DIM
    cosine_heads = cosine_table[:, :, None, :]
    sine_heads = sine_table[:, :, None, :]
    scale_one = lax.rsqrt(lax.optimization_barrier(jnp.mean(stream * stream, axis=-1, keepdims=True)) + norm_epsilon)
    normed_one = low(stream * scale_one * gain_one)
    mixed_qkv = low_back(matmul(normed_one, w_qkv) + b_qkv)
    queries = spin(mixed_qkv[..., :model_width].reshape(seq_count, length, HEADS, HEAD_DIM), cosine_heads, sine_heads)
    key_rows = spin(mixed_qkv[..., model_width:model_width + pair_width].reshape(seq_count, length, KV_HEADS, HEAD_DIM), cosine_heads, sine_heads)
    value_rows = mixed_qkv[..., model_width + pair_width:].reshape(seq_count, length, KV_HEADS, HEAD_DIM)
    attended = lax.map(jax.checkpoint(attend_one), (low(queries), low(key_rows), low(value_rows), segment_rows))
    attended = low_back(low(attended))
    middle = stream + low_back(matmul(attended, w_out))
    scale_two = lax.rsqrt(lax.optimization_barrier(jnp.mean(middle * middle, axis=-1, keepdims=True)) + norm_epsilon)
    normed_two = low(middle * scale_two * gain_two)
    gate_value = low_back(matmul(normed_two, w_gate))
    up_value = low_back(matmul(normed_two, w_up))
    hidden = low(jax.nn.silu(gate_value) * up_value)
    return middle + matmul(hidden, w_down)

def reference(tokens_in, out_grad, segments, norm1_gain, qkv_weight, qkv_bias, out_weight, norm2_gain, gate_weight, up_weight, down_weight):
    seq_count = MICRO * SEQS
    segment_rows = segments.reshape(seq_count, SEQ_LEN)
    cosine_table, sine_table = jax.vmap(rope_tables, in_axes=(0, None))(segment_rows, HEAD_DIM)
    start_rows = tokens_in.reshape(seq_count, SEQ_LEN, D).astype(jnp.float32)
    cotangent = out_grad.reshape(seq_count, SEQ_LEN, D).astype(jnp.float32)
    weights = tuple((piece.astype(jnp.float32) for piece in (norm1_gain, qkv_weight, qkv_bias, out_weight, norm2_gain, gate_weight, up_weight, down_weight)))
    first_weights = tuple((piece[0] for piece in weights))
    second_weights = tuple((piece[1] for piece in weights))
    delta_rows = jnp.zeros_like(start_rows)

    def whole(start_rows, first_weights, second_weights, delta_rows):
        inner = layer(start_rows, first_weights, segment_rows, cosine_table, sine_table)
        boundary = low_back(low(inner) + delta_rows)
        return (layer(boundary, second_weights, segment_rows, cosine_table, sine_table), boundary)
    final, pullback, boundary = jax.vjp(whole, start_rows, first_weights, second_weights, delta_rows, has_aux=True)
    grad_start, grad_first, grad_second, grad_boundary = pullback(cotangent)
    full_shape = (MICRO, SEQS, SEQ_LEN, D)
    section_out = jnp.stack([boundary.reshape(full_shape), final.reshape(full_shape)]).astype(jnp.bfloat16)
    section_in_grad = jnp.stack([grad_start.reshape(full_shape), grad_boundary.reshape(full_shape)]).astype(jnp.bfloat16)
    grads = tuple((jnp.stack([first_piece, second_piece]) for first_piece, second_piece in zip(grad_first, grad_second)))
    return (section_out, section_in_grad, grads[0], grads[1], grads[2], grads[3], grads[4], grads[5], grads[6], grads[7])
```

```python
import math

import jax
import jax.numpy as jnp
from jax import lax
from jax.experimental import pallas as pl
from jax.experimental.pallas import tpu as pltpu
from jax.sharding import PartitionSpec as P

HEADS = 14
KV_HEADS = 2
HEAD_DIM = 64
MICRO = 2
SEQ = 128
D = 896
DP = 1024
QKV = 1152
norm_epsilon = 1e-06
rope_base = 1000000.0

MESH = pl.DeviceIdType.MESH
BF = jnp.bfloat16
F32 = jnp.float32


class Place:
    def __init__(self):
        f = lax.axis_index("fsdp")
        self.s = lax.axis_index("section")
        self.c = lax.rem(f, 2)
        self.z = lax.rem(f // 2, 4)
        self.y = lax.rem(f // 8, 2)
        self.x = f // 16

    def at(self, x=None, y=None, z=None, c=None):
        x = self.x if x is None else x
        y = self.y if y is None else y
        z = self.z if z is None else z
        c = self.c if c is None else c
        return (self.s, ((x * 2 + y) * 4 + z) * 2 + c)

    def step(self, axis, k):
        here = self.x if axis == "x" else self.z
        return lax.rem(here + (k + 4), 4)

    def to(self, axis, k):
        return self.at(**{axis: self.step(axis, k)})

    def across(self):
        return self.at(y=1 - self.y)

    def mate(self):
        return self.at(c=1 - self.c)


def greet(place):
    barrier = pltpu.get_barrier_semaphore()
    near = (
        place.to("x", 1), place.to("x", -1), place.to("z", 1), place.to("z", -1),
        place.across(), place.mate(),
    )
    for device in near:
        pl.semaphore_signal(barrier, inc=1, device_id=device, device_id_type=MESH)
    pl.semaphore_wait(barrier, len(near))


class Wire:
    def __init__(self, send_sems, recv_sems):
        self.send_sems, self.recv_sems, self.started = send_sems, recv_sems, []

    def send(self, src, dst, device):
        k = len(self.started)
        assert k < self.send_sems.shape[0]
        copy = pltpu.make_async_remote_copy(
            src_ref=src, dst_ref=dst, send_sem=self.send_sems.at[k],
            recv_sem=self.recv_sems.at[k], device_id=device, device_id_type=MESH,
        )
        copy.start()
        self.started.append(copy)
        return copy

    def drain(self):
        for copy in self.started:
            copy.wait_send()


def interleave(flows):
    waiting = [(next(flow), k, flow) for k, flow in enumerate(flows)]
    while waiting:
        waiting.sort(key=lambda item: item[:2])
        _, k, flow = waiting.pop(0)
        try:
            waiting.append((next(flow), k, flow))
        except StopIteration:
            pass


def gather_yab(wire, place, slot, first, last, ready, t0, unit):
    x, y, z = place.x, place.y, place.z
    yield t0
    for wait in ready:
        wait()
    cross = wire.send(slot(x, y, z), slot(x, y, z), place.across())

    def pos(a, b):
        return (b, a) if first == "z" else (a, b)

    def piece(a, b, half=None):
        px, pz = pos(a, b)
        return slot(px, half, pz)

    mine = {"x": x, "z": z}
    a0, b0 = mine[first], mine[last]
    t = t0 + unit * 1
    yield t
    cross.wait_recv()
    a_r = wire.send(piece(a0, b0), piece(a0, b0), place.to(first, 1))
    a_l = wire.send(piece(a0, b0), piece(a0, b0), place.to(first, -1))

    def last_sends(a):
        r = wire.send(piece(a, b0), piece(a, b0), place.to(last, 1))
        l = wire.send(piece(a, b0), piece(a, b0), place.to(last, -1))
        return r, l

    def last_forward(a, r, l):
        r.wait_recv()
        bm = place.step(last, -1)
        r2 = wire.send(piece(a, bm, 0), piece(a, bm, 0), place.to(last, 1))
        l.wait_recv()
        bp = place.step(last, 1)
        l2 = wire.send(piece(a, bp, 1), piece(a, bp, 1), place.to(last, -1))
        return r2, l2

    w0 = last_sends(a0)
    t += unit * 2
    yield t
    a_r.wait_recv()
    am = place.step(first, -1)
    a_r2 = wire.send(piece(am, b0, 0), piece(am, b0, 0), place.to(first, 1))
    a_l.wait_recv()
    ap = place.step(first, 1)
    a_l2 = wire.send(piece(ap, b0, 1), piece(ap, b0, 1), place.to(first, -1))
    w1 = last_sends(am)
    w2 = last_sends(ap)
    t += unit * 2
    yield t
    f0 = last_forward(a0, *w0)
    t += unit * 2
    yield t
    a_r2.wait_recv()
    a_l2.wait_recv()
    aq = place.step(first, 2)
    w3 = last_sends(aq)
    t += unit * 2
    yield t
    f1 = last_forward(am, *w1)
    t += unit * 2
    yield t
    f2 = last_forward(ap, *w2)
    t += unit * 2
    yield t
    f3 = last_forward(aq, *w3)
    t += unit * 2
    yield t
    for pair in (f0, f1, f2, f3):
        for copy in pair:
            copy.wait_recv()


def gather_aby(wire, place, slot, parts, t0, unit):
    x, y, z = place.x, place.y, place.z
    yield t0
    r = wire.send(slot(x, y, z), slot(x, y, z), place.to("x", 1))
    l = wire.send(slot(x, y, z), slot(x, y, z), place.to("x", -1))
    t = t0 + unit
    yield t
    r.wait_recv()
    xm, xp = place.step("x", -1), place.step("x", 1)
    r2 = wire.send(parts(xm, y, z, 0), parts(xm, y, z, 0), place.to("x", 1))
    l.wait_recv()
    l2 = wire.send(parts(xp, y, z, 1), parts(xp, y, z, 1), place.to("x", -1))
    t += unit
    yield t
    r2.wait_recv()
    l2.wait_recv()
    zr = wire.send(slot(None, y, z), slot(None, y, z), place.to("z", 1))
    zl = wire.send(slot(None, y, z), slot(None, y, z), place.to("z", -1))
    y0 = wire.send(slot(None, y, z), slot(None, y, z), place.across())
    t += unit * 4
    yield t
    zm, zp, zq = place.step("z", -1), place.step("z", 1), place.step("z", 2)
    zr.wait_recv()
    zr2 = wire.send(slot(0, y, zm), slot(0, y, zm), place.to("z", 1))
    y1 = wire.send(slot(None, y, zm), slot(None, y, zm), place.across())
    zl.wait_recv()
    zl2 = wire.send(slot(1, y, zp), slot(1, y, zp), place.to("z", -1))
    y2 = wire.send(slot(None, y, zp), slot(None, y, zp), place.across())
    t += unit * 4
    yield t
    zr2.wait_recv()
    zl2.wait_recv()
    y3 = wire.send(slot(None, y, zq), slot(None, y, zq), place.across())
    t += unit * 10
    yield t
    for copy in (y0, y1, y2, y3):
        copy.wait_recv()


N_AG = 104
AG_COLS = dict(G=2560, U=2560, D=896, Q=1152, O=896)
BLOCK = dict(G=(32, 2560), U=(32, 2560), D=(80, 896), Q=(32, 1152), O=(32, 896))


def gather_flows(wire, place, ins, bufs, local_sems):
    x, y, z, c = place.x, place.y, place.z, place.c
    rows = pl.ds(pl.multiple_of(c * 16, 16), 16)
    G, U, D, Q, O = bufs
    g_in, u_in, d_in, q_in, o_in = ins
    own = []
    for k, (src, dst) in enumerate((
        (g_in.at[c], G.at[x, y, z, rows]), (u_in.at[c], U.at[x, y, z, rows]),
        (d_in, D.at[x, y, z]), (q_in, Q.at[x, y, z, rows]), (o_in, O.at[x, y, z, rows]),
    )):
        copy = pltpu.make_async_copy(src, dst, local_sems.at[k])
        copy.start()
        own.append(copy)
    swap_g = wire.send(g_in.at[1 - c], G.at[x, y, z, rows], place.mate())
    swap_u = wire.send(u_in.at[1 - c], U.at[x, y, z, rows], place.mate())

    def whole(buf):
        def slot(px, half, pz):
            if half is None:
                return buf.at[px, :, pz]
            return buf.at[px, half, pz]
        return slot

    def part(buf):
        def slot(px, half, pz):
            if half is None:
                return buf.at[px, :, pz, rows]
            return buf.at[px, half, pz, rows]
        return slot

    def down_slot(px, py, pz):
        if px is None:
            return D.at[:, py, pz]
        return D.at[px, py, pz]

    def down_zslot(px, py, pz):
        if px is None:
            return D.at[:, py, pz]
        if isinstance(px, int):
            return D.at[pl.ds(2 * px, 2), py, pz]
        return D.at[px, py, pz]

    def down_parts(px, py, pz, half):
        r = pl.ds(0, 48) if half == 0 else pl.ds(48, 32)
        return D.at[px, py, pz, r]

    def attention(buf, k, t0):
        yield from gather_yab(wire, place, part(buf), "z", "x", (own[k].wait,), t0, 1.0)
        mine = buf.at[:, :, :, rows]
        swap = wire.send(mine, mine, place.mate())
        yield 100.0
        swap.wait_recv()

    def down(t0):
        yield t0
        own[2].wait()
        yield from gather_aby(wire, place, down_zslot, down_parts, t0, 2.0)

    flows = [
        attention(Q, 3, 0.0),
        attention(O, 4, 0.1),
        down(0.2),
        gather_yab(wire, place, whole(G), "z", "x", (own[0].wait, swap_g.wait_recv), 0.3, 4.0),
        gather_yab(wire, place, whole(U), "x", "z", (own[1].wait, swap_u.wait_recv), 0.4, 4.0),
    ]
    return flows


def ag_kernel(g_in, u_in, d_in, q_in, o_in, g_o, u_o, d_o, q_o, o_o, G, U, D, Q, O, ss, rs, ls):
    place = Place()
    greet(place)
    wire = Wire(ss, rs)
    interleave(gather_flows(wire, place, (g_in, u_in, d_in, q_in, o_in), (G, U, D, Q, O), ls))
    wire.drain()
    out = []
    for k, (src, dst) in enumerate(((G, g_o), (U, u_o), (D, d_o), (Q, q_o), (O, o_o))):
        copy = pltpu.make_async_copy(src, dst, ls.at[k])
        copy.start()
        out.append(copy)
    for copy in out:
        copy.wait()


def bufs_shapes():
    return [(4, 2, 4) + BLOCK[k] for k in "GUDQO"]


def all_gather_weights(g, u, d, q, o):
    shapes = bufs_shapes()
    return pl.pallas_call(
        ag_kernel,
        out_shape=[jax.ShapeDtypeStruct(s, BF) for s in shapes],
        in_specs=[pl.BlockSpec(memory_space=pltpu.VMEM)] * 5,
        out_specs=[pl.BlockSpec(memory_space=pl.ANY)] * 5,
        scratch_shapes=[pltpu.VMEM(s, BF) for s in shapes]
        + [pltpu.SemaphoreType.DMA((N_AG,)), pltpu.SemaphoreType.DMA((N_AG,)), pltpu.SemaphoreType.DMA((5,))],
        compiler_params=pltpu.CompilerParams(
            collective_id=0, has_side_effects=True, vmem_limit_bytes=60 * 2**20
        ),
        name="gather_weights",
    )(g, u, d, q, o)


def add(dst, *srcs):
    total = dst[...]
    for src in srcs:
        total = total + src[...]
    dst[...] = total


def add_each(count, dst, *srcs):
    def body(i, carry):
        add(dst(i), *[src(i) for src in srcs])
        return carry
    lax.fori_loop(0, count, body, 0)


def scatter_aby(wire, place, slot, R, first, last, ready, t0, unit):
    r1a, r1b, r2a, r2b, s1a, s1b, s2a, s2b, t_buf = R
    mine = {"x": place.x, "z": place.z}
    a0, b0 = mine[first], mine[last]

    def piece(a, b, half=None):
        return slot(b, half, a) if first == "z" else slot(a, half, b)

    def blocks(a, b):
        return lambda i: piece(a, b, i)

    ap, am, aq = place.step(first, 1), place.step(first, -1), place.step(first, 2)
    order = [place.step(last, k) for k in (2, 1, -1)] + [b0]
    t = t0
    yield t
    for wait in ready:
        wait()
    one = []
    for k, b in enumerate(order):
        one.append((
            wire.send(piece(aq, b, 0), r1a.at[k], place.to(first, 1)),
            wire.send(piece(aq, b, 1), r1b.at[k], place.to(first, -1)),
        ))
    two = []
    for k, b in enumerate(order):
        t = t0 + unit * (k + 1)
        yield t
        one[k][0].wait_recv()
        add(piece(ap, b, 0), r1a.at[k])
        right = wire.send(piece(ap, b), r2a.at[k], place.to(first, 1))
        one[k][1].wait_recv()
        add(piece(am, b, 1), r1b.at[k])
        left = wire.send(piece(am, b), r2b.at[k], place.to(first, -1))
        two.append((right, left))
    t1 = t0 + unit * 4
    bp, bm, bq = order[1], order[2], order[0]

    def settle(k):
        two[k][0].wait_recv()
        two[k][1].wait_recv()
        for i in range(2):
            add(piece(a0, order[k], i), r2a.at[k, i], r2b.at[k, i])

    yield t1 + 2 * unit
    settle(0)
    d_r = wire.send(piece(a0, bq, 0), s1a, place.to(last, 1))
    d_l = wire.send(piece(a0, bq, 1), s1b, place.to(last, -1))
    yield t1 + 4 * unit
    settle(1)
    d_r.wait_recv()
    add(piece(a0, bp, 0), s1a)
    e_r = wire.send(piece(a0, bp), s2a, place.to(last, 1))
    yield t1 + 6 * unit
    settle(2)
    d_l.wait_recv()
    add(piece(a0, bm, 1), s1b)
    e_l = wire.send(piece(a0, bm), s2b, place.to(last, -1))
    yield t1 + 8 * unit
    settle(3)
    yield t1 + 9 * unit
    e_r.wait_recv()
    e_l.wait_recv()
    for i in range(2):
        add(piece(a0, b0, i), s2a.at[i], s2b.at[i])
    other = slot(place.x, 1 - place.y, place.z)
    cross = wire.send(other, t_buf, place.across())
    yield t1 + 10 * unit
    cross.wait_recv()
    add(slot(place.x, place.y, place.z), t_buf)


def scatter_down(wire, place, D, R, ready, t0, unit):
    yb, z1a, z1b, z2a, z2b, xa, xb, x2a, x2b = R
    x, y, z = place.x, place.y, place.z
    zp, zm, zq = place.step("z", 1), place.step("z", -1), place.step("z", 2)
    xp, xm, xq = place.step("x", 1), place.step("x", -1), place.step("x", 2)
    top, low = pl.ds(0, 48), pl.ds(48, 32)
    lo, hi = pl.ds(0, 2), pl.ds(2, 2)
    order = (zq, zp, zm, z)
    yield t0
    for wait in ready:
        wait()
    crossing = [wire.send(D.at[:, 1 - y, b], yb.at[k], place.across()) for k, b in enumerate(order)]

    def settle(k):
        crossing[k].wait_recv()
        add_each(4, lambda i: D.at[i, y, order[k]], lambda i: yb.at[k, i])

    yield t0 + 3 * unit
    settle(0)
    d_r = wire.send(D.at[lo, y, zq], z1a, place.to("z", 1))
    d_l = wire.send(D.at[hi, y, zq], z1b, place.to("z", -1))
    yield t0 + 6 * unit
    settle(1)
    d_r.wait_recv()
    add_each(2, lambda i: D.at[i, y, zp], lambda i: z1a.at[i])
    e_r = wire.send(D.at[:, y, zp], z2a, place.to("z", 1))
    yield t0 + 9 * unit
    settle(2)
    d_l.wait_recv()
    add_each(2, lambda i: D.at[i + 2, y, zm], lambda i: z1b.at[i])
    e_l = wire.send(D.at[:, y, zm], z2b, place.to("z", -1))
    yield t0 + 12 * unit
    settle(3)
    yield t0 + 13 * unit
    e_r.wait_recv()
    e_l.wait_recv()
    add_each(4, lambda i: D.at[i, y, z], lambda i: z2a.at[i], lambda i: z2b.at[i])
    f_r = wire.send(D.at[xq, y, z, top], xa, place.to("x", 1))
    f_l = wire.send(D.at[xq, y, z, low], xb, place.to("x", -1))
    yield t0 + 14 * unit
    f_r.wait_recv()
    add(D.at[xp, y, z, top], xa)
    g_r = wire.send(D.at[xp, y, z], x2a, place.to("x", 1))
    f_l.wait_recv()
    add(D.at[xm, y, z, low], xb)
    g_l = wire.send(D.at[xm, y, z], x2b, place.to("x", -1))
    yield t0 + 15 * unit
    g_r.wait_recv()
    g_l.wait_recv()
    add(D.at[x, y, z], x2a, x2b)


def rs_scratch():
    def aby(rows, cols):
        shapes = [(4, rows, cols)] * 2 + [(4, 2, rows, cols)] * 2 + [(rows, cols)] * 2 + [(2, rows, cols)] * 2 + [(rows, cols)]
        return [pltpu.VMEM(s, BF) for s in shapes]
    out = []
    out += aby(32, 2560) + [pltpu.VMEM((16, 2560), BF)]
    out += aby(32, 2560) + [pltpu.VMEM((16, 2560), BF)]
    b = (80, 896)
    out += [pltpu.VMEM(s, BF) for s in (
        (4, 4) + b, (2,) + b, (2,) + b, (4,) + b, (4,) + b, (48, 896), (32, 896), b, b)]
    out += aby(16, 1152) + [pltpu.VMEM((4, 2, 4, 16, 1152), BF)]
    out += aby(16, 896) + [pltpu.VMEM((4, 2, 4, 16, 896), BF)]
    return out


N_RS_SCRATCH = 10 + 10 + 9 + 10 + 10
N_RS = 104


def scatter_flows(wire, place, bufs, R, ready, outs, times):
    x, y, z, c = place.x, place.y, place.z, place.c
    G, U, D, Q, O = bufs
    g_o, u_o, d_o, q_o, o_o = outs
    rg, ru, rd, rq, ro = R[:10], R[10:20], R[20:29], R[29:39], R[39:49]
    rows = pl.ds(pl.multiple_of(c * 16, 16), 16)
    others = pl.ds(pl.multiple_of(16 - c * 16, 16), 16)

    def whole(buf):
        def slot(px, half, pz):
            return buf.at[px, :, pz] if half is None else buf.at[px, half, pz]
        return slot

    def part(buf):
        def slot(px, half, pz):
            return buf.at[px, :, pz, rows] if half is None else buf.at[px, half, pz, rows]
        return slot

    def hidden(buf, out, r, first, last, ready, t0):
        yield from scatter_aby(wire, place, whole(buf), r[:9], first, last, ready, t0, 4.0)
        swap = wire.send(buf.at[x, y, z, others], r[9], place.mate())
        yield 200.0
        swap.wait_recv()
        out[c] = buf[x, y, z, rows].astype(F32)
        out[1 - c] = r[9][...].astype(F32)

    def attention(buf, out, r, ready, t0):
        yield t0
        for wait in ready:
            wait()
        swap = wire.send(buf.at[:, :, :, others], r[9], place.mate())
        yield t0 + 8.0
        swap.wait_recv()
        add_each(32, lambda i: buf.at[i // 8, lax.rem(i // 4, 2), lax.rem(i, 4), rows],
                 lambda i: r[9].at[i // 8, lax.rem(i // 4, 2), lax.rem(i, 4)])
        yield from scatter_aby(wire, place, part(buf), r[:9], "x", "z", (), t0 + 8.0, 1.0)
        out[...] = buf[x, y, z, rows].astype(F32)

    def down(t0):
        yield from scatter_down(wire, place, D, rd, ready[2], t0, 4.0)
        d_o[...] = D[x, y, z].astype(F32)

    return [
        down(times[2]),
        hidden(G, g_o, rg, "x", "z", ready[0], times[0]),
        hidden(U, u_o, ru, "z", "x", ready[1], times[1]),
        attention(O, o_o, ro, ready[4], times[4]),
        attention(Q, q_o, rq, ready[3], times[3]),
    ]


def rs_kernel(*refs):
    ins, outs, bufs = refs[:5], refs[5:10], refs[10:15]
    R = refs[15:15 + N_RS_SCRATCH]
    ss, rs, ls = refs[15 + N_RS_SCRATCH:]
    place = Place()
    loads = []
    for k in (2, 0, 1, 4, 3):
        copy = pltpu.make_async_copy(ins[k], bufs[k], ls.at[k])
        copy.start()
        loads.append((k, copy))
    ready = {k: (copy.wait,) for k, copy in loads}
    greet(place)
    wire = Wire(ss, rs)
    interleave(scatter_flows(wire, place, bufs, R, ready, outs, (0.1, 0.2, 0.0, 0.4, 0.3)))
    wire.drain()


def reduce_scatter_grads(g, u, d, q, o):
    shapes = bufs_shapes()
    return pl.pallas_call(
        rs_kernel,
        out_shape=[jax.ShapeDtypeStruct(s, F32) for s in ((2, 16, 2560), (2, 16, 2560), (80, 896), (16, 1152), (16, 896))],
        in_specs=[pl.BlockSpec(memory_space=pl.ANY)] * 5,
        out_specs=[pl.BlockSpec(memory_space=pltpu.VMEM)] * 5,
        scratch_shapes=[pltpu.VMEM(s, BF) for s in shapes] + rs_scratch()
        + [pltpu.SemaphoreType.DMA((N_RS,)), pltpu.SemaphoreType.DMA((N_RS,)), pltpu.SemaphoreType.DMA((5,))],
        compiler_params=pltpu.CompilerParams(
            collective_id=1, has_side_effects=True, vmem_limit_bytes=60 * 2**20
        ),
        name="scatter_grads",
    )(g, u, d, q, o)


def rope_tables(segment_row, head_size):
    length = segment_row.shape[0]
    places = jnp.arange(length, dtype=jnp.int32)
    changes = jnp.concatenate(
        [jnp.ones((1,), jnp.int32), (segment_row[1:] != segment_row[:-1]).astype(jnp.int32)]
    )
    starts = lax.cummax(places * changes, axis=0)
    offsets = (places - starts).astype(F32)
    ladder = jnp.arange(head_size // 2, dtype=F32) * (-2.0 * math.log(rope_base) / head_size)
    angles = offsets[:, None] * jnp.exp(ladder)[None, :]
    angles = jnp.concatenate([angles, angles], axis=-1)
    return (jnp.cos(angles), jnp.sin(angles))


def rotate_half(head_block):
    half_width = head_block.shape[-1] // 2
    return jnp.concatenate([-head_block[..., half_width:], head_block[..., :half_width]], axis=-1)


def spin(head_block, cosine_table, sine_table):
    return head_block * cosine_table + rotate_half(head_block) * sine_table


def spin_back(grad_rotated, cosine_table, sine_table):
    return grad_rotated * cosine_table - rotate_half(grad_rotated * sine_table)


def visible(segment_row):
    places = jnp.arange(segment_row.shape[0], dtype=jnp.int32)
    return (segment_row[:, None] == segment_row[None, :]) & (places[None, :] <= places[:, None])


def score_block(query_low, key_low, allowed):
    scores = jnp.einsum(
        "bqkgd,bskd->bkgqs", query_low, key_low, preferred_element_type=F32
    ) * HEAD_DIM ** (-0.5)
    return jnp.where(allowed[:, None, None], scores, -1e30)


def mm(a, b):
    return jnp.dot(a, b, preferred_element_type=F32)


def mm_t(a, b):
    return lax.dot_general(a, b, (((1,), (1,)), ((), ())), preferred_element_type=F32)


def t_mm(a, b):
    return lax.dot_general(a, b, (((0,), (0,)), ((), ())), preferred_element_type=F32)


def swap_mates(block):
    route = [(i, i ^ 1) for i in range(lax.axis_size("fsdp"))]
    return lax.ppermute(block, "fsdp", route)


def spread_matrix():
    d = lax.broadcasted_iota(jnp.int32, (D, DP), 0)
    p = lax.broadcasted_iota(jnp.int32, (D, DP), 1)
    return ((p // 16 == d // 14) & (p % 16 == d % 14)).astype(BF)


def layer_forward(h, weights, smalls, tables, spread):
    gate_w, up_w, down_w, qkv_w, out_w = weights
    gain_one, gain_two, bias = smalls
    cos, sin, allowed = tables
    scale_one = lax.rsqrt(jnp.mean(h * h, axis=-1, keepdims=True) + norm_epsilon)
    n1 = mm((h * scale_one * gain_one).astype(BF), spread).astype(BF)
    qkv = mm(n1, qkv_w) + bias
    qkv = qkv.reshape(MICRO, SEQ, QKV)
    q = spin(qkv[..., :D].reshape(MICRO, SEQ, HEADS, HEAD_DIM), cos[:, :, None], sin[:, :, None])
    k = spin(
        qkv[..., D : D + 128].reshape(MICRO, SEQ, KV_HEADS, HEAD_DIM), cos[:, :, None], sin[:, :, None]
    )
    v = qkv[..., D + 128 :].reshape(MICRO, SEQ, KV_HEADS, HEAD_DIM).astype(BF)
    q = q.astype(BF).reshape(MICRO, SEQ, KV_HEADS, HEADS // KV_HEADS, HEAD_DIM)
    k = k.astype(BF)
    scores = score_block(q, k, allowed)
    row_max = jnp.max(scores, axis=-1, keepdims=True)
    exponent = jnp.exp(scores - row_max)
    row_total = jnp.sum(exponent, axis=-1, keepdims=True)
    probs = (exponent / row_total).astype(BF)
    lse = row_max + jnp.log(row_total)
    ctx = jnp.einsum("bkgqs,bskd->bqkgd", probs, v, preferred_element_type=F32)
    ctx = mm(ctx.reshape(MICRO * SEQ, D).astype(BF), spread).astype(BF)
    mid = h + mm(ctx, out_w)
    scale_two = lax.rsqrt(jnp.mean(mid * mid, axis=-1, keepdims=True) + norm_epsilon)
    n2 = mm((mid * scale_two * gain_two).astype(BF), spread).astype(BF)
    n2 = jnp.concatenate([n2, swap_mates(n2)], axis=0)
    gate = mm(n2, gate_w)
    up = mm(n2, up_w)
    act = (jax.nn.silu(gate) * up).astype(BF)
    part = mm(act, down_w)
    y = mid + part[: MICRO * SEQ] + swap_mates(part[MICRO * SEQ :].astype(BF)).astype(F32)
    return y, (h, scale_one, n1, q, k, v, lse, ctx, mid, scale_two, n2, gate, up, act)


def layer_backward(dy, kept, weights, smalls, tables, spread):
    h, scale_one, n1, q, k, v, lse, ctx, mid, scale_two, n2, gate, up, act = kept
    gate_w, up_w, down_w, qkv_w, out_w = weights
    gain_one, gain_two, bias = smalls
    cos, sin, allowed = tables
    dy_all = jnp.concatenate([dy, swap_mates(dy)], axis=0)
    dact = mm_t(dy_all, down_w)
    sig = jax.nn.sigmoid(gate)
    dgate = (dact * up * sig * (1.0 + gate * (1.0 - sig))).astype(BF)
    dup = (dact * gate * sig).astype(BF)
    part = mm_t(dgate, gate_w) + mm_t(dup, up_w)
    half = MICRO * SEQ
    dn2 = part[:half] + swap_mates(part[half:].astype(BF)).astype(F32)
    dn2 = mm_t(dn2.astype(BF), spread)
    g2 = jnp.sum(dn2 * mid * scale_two, axis=0)
    scaled = dn2 * gain_two
    dmid = (
        dy.astype(F32)
        + scale_two * scaled
        - mid * scale_two**3 * jnp.mean(scaled * mid, axis=-1, keepdims=True)
    )
    dbranch = dmid.astype(BF)
    dctx = mm_t(mm_t(dbranch, out_w).astype(BF), spread).astype(BF)
    dctx = dctx.reshape(MICRO, SEQ, KV_HEADS, HEADS // KV_HEADS, HEAD_DIM)
    scores = score_block(q, k, allowed)
    full = jnp.where(allowed[:, None, None], jnp.exp(scores - lse), 0.0)
    probs = full.astype(BF)
    dv = jnp.einsum("bkgqs,bqkgd->bskd", probs, dctx, preferred_element_type=F32)
    dprobs = jnp.einsum("bqkgd,bskd->bkgqs", dctx, v, preferred_element_type=F32)
    dscores = (full * (dprobs - jnp.sum(full * dprobs, axis=-1, keepdims=True))).astype(BF)
    dq = jnp.einsum("bkgqs,bskd->bqkgd", dscores, k, preferred_element_type=F32) * 0.125
    dk = jnp.einsum("bkgqs,bqkgd->bskd", dscores, q, preferred_element_type=F32) * 0.125
    dq = spin_back(dq.reshape(MICRO, SEQ, HEADS, HEAD_DIM), cos[:, :, None], sin[:, :, None])
    dk = spin_back(dk, cos[:, :, None], sin[:, :, None])
    dqkv = jnp.concatenate(
        [dq.reshape(half, -1), dk.reshape(half, -1), dv.reshape(half, -1)], axis=1
    ).astype(BF)
    dbias = jnp.sum(dqkv, axis=0, dtype=F32)
    dn1 = mm_t(mm_t(dqkv, qkv_w).astype(BF), spread)
    g1 = jnp.sum(dn1 * h * scale_one, axis=0)
    scaled = dn1 * gain_one
    dh = (
        dmid
        + scale_one * scaled
        - h * scale_one**3 * jnp.mean(scaled * h, axis=-1, keepdims=True)
    )

    def grads():
        dq_w = t_mm(n1, dqkv).astype(BF).reshape(64, 16, QKV)
        row = jnp.zeros((64, 1, QKV), BF)
        row = row.at[:, 0, 0:14].set(g1.reshape(64, 14).astype(BF))
        row = row.at[:, 0, 32:46].set(g2.reshape(64, 14).astype(BF))
        row = row.at[:, 0, 64:82].set(dbias.reshape(64, 18).astype(BF))
        dq_w = jnp.concatenate([dq_w[:, :14], row, dq_w[:, 15:]], axis=1)
        return (
            t_mm(n2, dgate).astype(BF),
            t_mm(n2, dup).astype(BF),
            t_mm(act, dy_all).astype(BF),
            dq_w,
            t_mm(ctx, dbranch).astype(BF),
        )

    return dh, grads


def pack_hidden(w):
    w = jnp.pad(w.reshape(14, 32, 2, 76), ((0, 2), (0, 0), (0, 0), (0, 4)))
    return w.transpose(2, 0, 1, 3).reshape(2, 16, 2560)


def unpack_hidden(g):
    g = g.reshape(2, 16, 32, 80)[:, :14, :, :76]
    return g.transpose(1, 2, 0, 3).reshape(14, 4864)


def hop(block, distance):
    route = [(0, 1)] if distance == 1 else [(1, 0)]
    return lax.ppermute(block, "section", route)


def shards(
    tokens_in, out_grad, segments, norm1_gain, qkv_weight, qkv_bias, out_weight, norm2_gain,
    gate_weight, up_weight, down_weight,
):
    section = lax.axis_index("section")
    half = MICRO * SEQ
    tokens = tokens_in.reshape(half, D)
    dy_last = out_grad.reshape(half, D)
    rows = segments[:, 0]
    cos, sin = jax.vmap(rope_tables, in_axes=(0, None))(rows, HEAD_DIM)
    tables = (cos, sin, jax.vmap(visible)(rows))
    spread = spread_matrix()
    small_row = jnp.concatenate(
        [jnp.pad(norm1_gain[0], (0, 18)), jnp.pad(norm2_gain[0], (0, 18)), jnp.pad(qkv_bias[0], (0, 1152 - 82))]
    )
    g, u, d, q, o = all_gather_weights(
        pack_hidden(gate_weight[0]),
        pack_hidden(up_weight[0]),
        jnp.pad(down_weight[0], ((0, 4), (0, 0))),
        jnp.concatenate([qkv_weight[0], small_row[None], jnp.zeros((1, QKV), BF)], axis=0),
        jnp.pad(out_weight[0], ((0, 2), (0, 0))),
    )
    weights = (
        g.reshape(DP, 2560), u.reshape(DP, 2560), d.reshape(2560, D), q.reshape(DP, QKV), o.reshape(DP, D)
    )
    small = q.reshape(64, 16, QKV)[:, 14, :128].astype(F32)
    smalls = (
        small[:, 0:14].reshape(1, D), small[:, 32:46].reshape(1, D), small[:, 64:82].reshape(1, QKV)
    )
    y, _ = layer_forward(tokens.astype(F32), weights, smalls, tables, spread)
    arrived = hop(y.astype(BF), 1)
    h = jnp.where(section == 0, tokens, arrived).astype(F32)
    y, kept = layer_forward(h, weights, smalls, tables, spread)
    dh, _ = layer_backward(dy_last, kept, weights, smalls, tables, spread)
    arrived = hop(dh.astype(BF), -1)
    dy = jnp.where(section == 1, dy_last, arrived)
    dh, grads = layer_backward(dy, kept, weights, smalls, tables, spread)
    parts = grads()
    shapes = bufs_shapes()
    g, u, d, q, o = reduce_scatter_grads(*[a.reshape(s) for a, s in zip(parts, shapes)])
    shape = (1, MICRO, 1, SEQ, D)
    return (
        y.astype(BF).reshape(shape),
        dh.astype(BF).reshape(shape),
        q[14, 0:14][None],
        q[:14][None],
        q[14, 64:82][None],
        o[:14][None],
        q[14, 32:46][None],
        unpack_hidden(g)[None],
        unpack_hidden(u)[None],
        d[:76][None],
    )


def solution(mesh):
    in_specs = (
        P(None, "fsdp", None, None),
        P(None, "fsdp", None, None),
        P(None, "fsdp", None),
        P("section", "fsdp"),
        P("section", "fsdp", None),
        P("section", "fsdp"),
        P("section", "fsdp", None),
        P("section", "fsdp"),
        P("section", "fsdp", None),
        P("section", "fsdp", None),
        P("section", "fsdp", None),
    )
    out_specs = (
        P("section", None, "fsdp", None, None),
        P("section", None, "fsdp", None, None),
        P("section", "fsdp"),
        P("section", "fsdp", None),
        P("section", "fsdp"),
        P("section", "fsdp", None),
        P("section", "fsdp"),
        P("section", "fsdp", None),
        P("section", "fsdp", None),
        P("section", "fsdp", None),
    )
    return jax.shard_map(shards, mesh=mesh, in_specs=in_specs, out_specs=out_specs, check_vma=False)
```

```python
import math
from types import SimpleNamespace

import jax
import jax.numpy as jnp
from jax import lax
from jax.experimental import pallas as pl
from jax.experimental.pallas import tpu as pltpu
from jax.sharding import PartitionSpec as P
import numpy as np

HEADS = 14
KV_HEADS = 2
HEAD_DIM = 64
MICRO = 2
SEQ = 128
D = 896
DP = 1024
QKV = 1152
norm_epsilon = 1e-06
rope_base = 1000000.0

MESH = pl.DeviceIdType.MESH
BF = jnp.bfloat16
F32 = jnp.float32


class Place:
    def __init__(self):
        f = lax.axis_index("fsdp")
        self.s = lax.axis_index("section")
        self.c = lax.rem(f, 2)
        self.z = lax.rem(f // 2, 4)
        self.y = lax.rem(f // 8, 2)
        self.x = f // 16

    def at(self, x=None, y=None, z=None, c=None):
        x = self.x if x is None else x
        y = self.y if y is None else y
        z = self.z if z is None else z
        c = self.c if c is None else c
        return (self.s, ((x * 2 + y) * 4 + z) * 2 + c)

    def step(self, axis, k):
        here = self.x if axis == "x" else self.z
        return lax.rem(here + (k + 4), 4)

    def to(self, axis, k):
        return self.at(**{axis: self.step(axis, k)})

    def across(self):
        return self.at(y=1 - self.y)

    def mate(self):
        return self.at(c=1 - self.c)

    def beyond(self):
        return (1 - self.s, self.at()[1])


def greet(place):
    barrier = pltpu.get_barrier_semaphore()
    near = (
        place.to("x", 1), place.to("x", -1), place.to("z", 1), place.to("z", -1),
        place.across(), place.mate(), place.beyond(),
    )
    for device in near:
        pl.semaphore_signal(barrier, inc=1, device_id=device, device_id_type=MESH)
    pl.semaphore_wait(barrier, len(near))


class Wire:
    def __init__(self, send_sems, recv_sems):
        self.send_sems, self.recv_sems = send_sems, recv_sems
        self.count, self.started = 0, []

    def send(self, src, dst, device):
        k = self.count
        self.count += 1
        assert k < self.send_sems.shape[0]
        copy = pltpu.make_async_remote_copy(
            src_ref=src, dst_ref=dst, send_sem=self.send_sems.at[k],
            recv_sem=self.recv_sems.at[k], device_id=device, device_id_type=MESH,
        )
        copy.start()
        self.started.append(copy)
        return copy

    def drain(self):
        for copy in self.started:
            copy.wait_send()
        self.started = []


def interleave(flows):
    waiting = [(next(flow), k, flow) for k, flow in enumerate(flows)]
    while waiting:
        waiting.sort(key=lambda item: item[:2])
        _, k, flow = waiting.pop(0)
        try:
            waiting.append((next(flow), k, flow))
        except StopIteration:
            pass


def gather_yab(wire, place, slot, first, last, ready, t0, unit):
    x, y, z = place.x, place.y, place.z
    yield t0
    for wait in ready:
        wait()
    cross = wire.send(slot(x, y, z), slot(x, y, z), place.across())

    def pos(a, b):
        return (b, a) if first == "z" else (a, b)

    def piece(a, b, half=None):
        px, pz = pos(a, b)
        return slot(px, half, pz)

    mine = {"x": x, "z": z}
    a0, b0 = mine[first], mine[last]
    t = t0 + unit * 1
    yield t
    cross.wait_recv()
    a_r = wire.send(piece(a0, b0), piece(a0, b0), place.to(first, 1))
    a_l = wire.send(piece(a0, b0), piece(a0, b0), place.to(first, -1))

    def last_sends(a):
        r = wire.send(piece(a, b0), piece(a, b0), place.to(last, 1))
        l = wire.send(piece(a, b0), piece(a, b0), place.to(last, -1))
        return r, l

    def last_forward(a, r, l):
        r.wait_recv()
        bm = place.step(last, -1)
        r2 = wire.send(piece(a, bm, 0), piece(a, bm, 0), place.to(last, 1))
        l.wait_recv()
        bp = place.step(last, 1)
        l2 = wire.send(piece(a, bp, 1), piece(a, bp, 1), place.to(last, -1))
        return r2, l2

    w0 = last_sends(a0)
    t += unit * 2
    yield t
    a_r.wait_recv()
    am = place.step(first, -1)
    a_r2 = wire.send(piece(am, b0, 0), piece(am, b0, 0), place.to(first, 1))
    a_l.wait_recv()
    ap = place.step(first, 1)
    a_l2 = wire.send(piece(ap, b0, 1), piece(ap, b0, 1), place.to(first, -1))
    w1 = last_sends(am)
    w2 = last_sends(ap)
    t += unit * 2
    yield t
    f0 = last_forward(a0, *w0)
    t += unit * 2
    yield t
    a_r2.wait_recv()
    a_l2.wait_recv()
    aq = place.step(first, 2)
    w3 = last_sends(aq)
    t += unit * 2
    yield t
    f1 = last_forward(am, *w1)
    t += unit * 2
    yield t
    f2 = last_forward(ap, *w2)
    t += unit * 2
    yield t
    f3 = last_forward(aq, *w3)
    t += unit * 2
    yield t
    for pair in (f0, f1, f2, f3):
        for copy in pair:
            copy.wait_recv()


def gather_aby(wire, place, slot, parts, t0, unit):
    x, y, z = place.x, place.y, place.z
    yield t0
    r = wire.send(slot(x, y, z), slot(x, y, z), place.to("x", 1))
    l = wire.send(slot(x, y, z), slot(x, y, z), place.to("x", -1))
    t = t0 + unit
    yield t
    r.wait_recv()
    xm, xp = place.step("x", -1), place.step("x", 1)
    r2 = wire.send(parts(xm, y, z, 0), parts(xm, y, z, 0), place.to("x", 1))
    l.wait_recv()
    l2 = wire.send(parts(xp, y, z, 1), parts(xp, y, z, 1), place.to("x", -1))
    t += unit
    yield t
    r2.wait_recv()
    l2.wait_recv()
    zr = wire.send(slot(None, y, z), slot(None, y, z), place.to("z", 1))
    zl = wire.send(slot(None, y, z), slot(None, y, z), place.to("z", -1))
    y0 = wire.send(slot(None, y, z), slot(None, y, z), place.across())
    t += unit * 4
    yield t
    zm, zp, zq = place.step("z", -1), place.step("z", 1), place.step("z", 2)
    zr.wait_recv()
    zr2 = wire.send(slot(0, y, zm), slot(0, y, zm), place.to("z", 1))
    y1 = wire.send(slot(None, y, zm), slot(None, y, zm), place.across())
    zl.wait_recv()
    zl2 = wire.send(slot(1, y, zp), slot(1, y, zp), place.to("z", -1))
    y2 = wire.send(slot(None, y, zp), slot(None, y, zp), place.across())
    t += unit * 4
    yield t
    zr2.wait_recv()
    zl2.wait_recv()
    y3 = wire.send(slot(None, y, zq), slot(None, y, zq), place.across())
    t += unit * 10
    yield t
    for copy in (y0, y1, y2, y3):
        copy.wait_recv()


BLOCK = dict(G=(32, 2560), U=(32, 2560), D=(80, 896), Q=(32, 1152), O=(32, 896))


def gather_flows(wire, place, ins, bufs, local_sems, done):
    x, y, z, c = place.x, place.y, place.z, place.c
    rows = pl.ds(pl.multiple_of(c * 16, 16), 16)
    G, U, D, Q, O = bufs
    g_in, u_in, d_in, q_in, o_in = ins
    own = []
    for k, (src, dst) in enumerate((
        (g_in.at[c], G.at[x, y, z, rows]), (u_in.at[c], U.at[x, y, z, rows]),
        (d_in, D.at[x, y, z]), (q_in, Q.at[x, y, z, rows]), (o_in, O.at[x, y, z, rows]),
    )):
        copy = pltpu.make_async_copy(src, dst, local_sems.at[k])
        copy.start()
        own.append(copy)
    swap_g = wire.send(g_in.at[1 - c], G.at[x, y, z, rows], place.mate())
    swap_u = wire.send(u_in.at[1 - c], U.at[x, y, z, rows], place.mate())

    def whole(buf):
        def slot(px, half, pz):
            if half is None:
                return buf.at[px, :, pz]
            return buf.at[px, half, pz]
        return slot

    def part(buf):
        def slot(px, half, pz):
            if half is None:
                return buf.at[px, :, pz, rows]
            return buf.at[px, half, pz, rows]
        return slot

    def down_slot(px, py, pz):
        if px is None:
            return D.at[:, py, pz]
        return D.at[px, py, pz]

    def down_zslot(px, py, pz):
        if px is None:
            return D.at[:, py, pz]
        if isinstance(px, int):
            return D.at[pl.ds(2 * px, 2), py, pz]
        return D.at[px, py, pz]

    def down_parts(px, py, pz, half):
        r = pl.ds(0, 48) if half == 0 else pl.ds(48, 32)
        return D.at[px, py, pz, r]

    def attention(name, buf, k, t0):
        yield from gather_yab(wire, place, part(buf), "z", "x", (own[k].wait,), t0, 1.0)
        mine = buf.at[:, :, :, rows]
        swap = wire.send(mine, mine, place.mate())
        yield t0 + 20.0
        swap.wait_recv()
        done.add(name)

    def down(t0):
        yield t0
        own[2].wait()
        yield from gather_aby(wire, place, down_zslot, down_parts, t0, 2.0)

    flows = [
        attention("Q", Q, 3, 0.0),
        attention("O", O, 4, 0.1),
        down(0.2),
        gather_yab(wire, place, whole(G), "z", "x", (own[0].wait, swap_g.wait_recv), 0.3, 4.0),
        gather_yab(wire, place, whole(U), "x", "z", (own[1].wait, swap_u.wait_recv), 0.4, 4.0),
    ]
    return flows


def bufs_shapes():
    return [(4, 2, 4) + BLOCK[k] for k in "GUDQO"]


def add(dst, *srcs):
    total = dst[...]
    for src in srcs:
        total = total + src[...]
    dst[...] = total


def add_each(count, dst, *srcs):
    def body(i, carry):
        add(dst(i), *[src(i) for src in srcs])
        return carry
    lax.fori_loop(0, count, body, 0)


def scatter_aby(wire, place, slot, R, first, last, t0, unit):
    r1a, r1b, r2a, r2b, s1a, s1b, s2a, s2b, t_buf = R
    mine = {"x": place.x, "z": place.z}
    a0, b0 = mine[first], mine[last]

    def piece(a, b, half=None):
        return slot(b, half, a) if first == "z" else slot(a, half, b)

    def blocks(a, b):
        return lambda i: piece(a, b, i)

    ap, am, aq = place.step(first, 1), place.step(first, -1), place.step(first, 2)
    order = [place.step(last, k) for k in (2, 1, -1)] + [b0]
    t = t0
    yield t
    one = []
    for k, b in enumerate(order):
        one.append((
            wire.send(piece(aq, b, 0), r1a.at[k], place.to(first, 1)),
            wire.send(piece(aq, b, 1), r1b.at[k], place.to(first, -1)),
        ))
    two = []
    for k, b in enumerate(order):
        t = t0 + unit * (k + 1)
        yield t
        one[k][0].wait_recv()
        add(piece(ap, b, 0), r1a.at[k])
        right = wire.send(piece(ap, b), r2a.at[k], place.to(first, 1))
        one[k][1].wait_recv()
        add(piece(am, b, 1), r1b.at[k])
        left = wire.send(piece(am, b), r2b.at[k], place.to(first, -1))
        two.append((right, left))
    t1 = t0 + unit * 4
    bp, bm, bq = order[1], order[2], order[0]

    def settle(k):
        two[k][0].wait_recv()
        two[k][1].wait_recv()
        for i in range(2):
            add(piece(a0, order[k], i), r2a.at[k, i], r2b.at[k, i])

    yield t1 + 2 * unit
    settle(0)
    d_r = wire.send(piece(a0, bq, 0), s1a, place.to(last, 1))
    d_l = wire.send(piece(a0, bq, 1), s1b, place.to(last, -1))
    yield t1 + 4 * unit
    settle(1)
    d_r.wait_recv()
    add(piece(a0, bp, 0), s1a)
    e_r = wire.send(piece(a0, bp), s2a, place.to(last, 1))
    yield t1 + 6 * unit
    settle(2)
    d_l.wait_recv()
    add(piece(a0, bm, 1), s1b)
    e_l = wire.send(piece(a0, bm), s2b, place.to(last, -1))
    yield t1 + 8 * unit
    settle(3)
    yield t1 + 9 * unit
    e_r.wait_recv()
    e_l.wait_recv()
    for i in range(2):
        add(piece(a0, b0, i), s2a.at[i], s2b.at[i])
    other = slot(place.x, 1 - place.y, place.z)
    cross = wire.send(other, t_buf, place.across())
    yield t1 + 10 * unit
    cross.wait_recv()
    add(slot(place.x, place.y, place.z), t_buf)


def scatter_down(wire, place, D, R, t0, unit):
    yb, z1a, z1b, z2a, z2b, xa, xb, x2a, x2b = R
    x, y, z = place.x, place.y, place.z
    zp, zm, zq = place.step("z", 1), place.step("z", -1), place.step("z", 2)
    xp, xm, xq = place.step("x", 1), place.step("x", -1), place.step("x", 2)
    top, low = pl.ds(0, 48), pl.ds(48, 32)
    lo, hi = pl.ds(0, 2), pl.ds(2, 2)
    order = (zq, zp, zm, z)
    yield t0
    crossing = [wire.send(D.at[:, 1 - y, b], yb.at[k], place.across()) for k, b in enumerate(order)]

    def settle(k):
        crossing[k].wait_recv()
        add_each(4, lambda i: D.at[i, y, order[k]], lambda i: yb.at[k, i])

    yield t0 + 3 * unit
    settle(0)
    d_r = wire.send(D.at[lo, y, zq], z1a, place.to("z", 1))
    d_l = wire.send(D.at[hi, y, zq], z1b, place.to("z", -1))
    yield t0 + 6 * unit
    settle(1)
    d_r.wait_recv()
    add_each(2, lambda i: D.at[i, y, zp], lambda i: z1a.at[i])
    e_r = wire.send(D.at[:, y, zp], z2a, place.to("z", 1))
    yield t0 + 9 * unit
    settle(2)
    d_l.wait_recv()
    add_each(2, lambda i: D.at[i + 2, y, zm], lambda i: z1b.at[i])
    e_l = wire.send(D.at[:, y, zm], z2b, place.to("z", -1))
    yield t0 + 12 * unit
    settle(3)
    yield t0 + 13 * unit
    e_r.wait_recv()
    e_l.wait_recv()
    add_each(4, lambda i: D.at[i, y, z], lambda i: z2a.at[i], lambda i: z2b.at[i])
    f_r = wire.send(D.at[xq, y, z, top], xa, place.to("x", 1))
    f_l = wire.send(D.at[xq, y, z, low], xb, place.to("x", -1))
    yield t0 + 14 * unit
    f_r.wait_recv()
    add(D.at[xp, y, z, top], xa)
    g_r = wire.send(D.at[xp, y, z], x2a, place.to("x", 1))
    f_l.wait_recv()
    add(D.at[xm, y, z, low], xb)
    g_l = wire.send(D.at[xm, y, z], x2b, place.to("x", -1))
    yield t0 + 15 * unit
    g_r.wait_recv()
    g_l.wait_recv()
    add(D.at[x, y, z], x2a, x2b)


def rs_scratch():
    def aby(rows, cols):
        shapes = [(4, rows, cols)] * 2 + [(4, 2, rows, cols)] * 2 + [(rows, cols)] * 2 + [(2, rows, cols)] * 2 + [(rows, cols)]
        return [pltpu.VMEM(s, BF) for s in shapes]
    out = []
    out += aby(32, 2560) + [pltpu.VMEM((16, 2560), BF)]
    out += aby(32, 2560) + [pltpu.VMEM((16, 2560), BF)]
    b = (80, 896)
    out += [pltpu.VMEM(s, BF) for s in (
        (4, 4) + b, (2,) + b, (2,) + b, (4,) + b, (4,) + b, (48, 896), (32, 896), b, b)]
    out += aby(16, 1152) + [pltpu.VMEM((4, 2, 4, 16, 1152), BF)]
    out += aby(16, 896) + [pltpu.VMEM((4, 2, 4, 16, 896), BF)]
    return out


N_RS_SCRATCH = 10 + 10 + 9 + 10 + 10


def scatter_flows(wire, place, bufs, R, made, outs):
    x, y, z, c = place.x, place.y, place.z, place.c
    G, U, D, Q, O = bufs
    g_o, u_o, d_o, q_o, o_o = outs
    rg, ru, rd, rq, ro = R[:10], R[10:20], R[20:29], R[29:39], R[39:49]
    rows = pl.ds(pl.multiple_of(c * 16, 16), 16)
    others = pl.ds(pl.multiple_of(16 - c * 16, 16), 16)

    def whole(buf):
        def slot(px, half, pz):
            return buf.at[px, :, pz] if half is None else buf.at[px, half, pz]
        return slot

    def part(buf):
        def slot(px, half, pz):
            return buf.at[px, :, pz, rows] if half is None else buf.at[px, half, pz, rows]
        return slot

    def made_of(name):
        t = 0.0
        while name not in made:
            yield t
            t += 0.5
        return t

    def hidden(name, buf, out, r, first, last):
        t0 = yield from made_of(name)
        yield from scatter_aby(wire, place, whole(buf), r[:9], first, last, t0, 4.0)
        swap = wire.send(buf.at[x, y, z, others], r[9], place.mate())
        yield 200.0
        swap.wait_recv()
        out[c] = buf[x, y, z, rows].astype(F32)
        out[1 - c] = r[9][...].astype(F32)

    def attention(name, buf, out, r):
        t0 = yield from made_of(name)
        swap = wire.send(buf.at[:, :, :, others], r[9], place.mate())
        yield t0 + 8.0
        swap.wait_recv()
        add_each(32, lambda i: buf.at[i // 8, lax.rem(i // 4, 2), lax.rem(i, 4), rows],
                 lambda i: r[9].at[i // 8, lax.rem(i // 4, 2), lax.rem(i, 4)])
        yield from scatter_aby(wire, place, part(buf), r[:9], "x", "z", t0 + 8.0, 1.0)
        out[...] = buf[x, y, z, rows].astype(F32)

    def down():
        t0 = yield from made_of("D")
        yield from scatter_down(wire, place, D, rd, t0, 4.0)
        d_o[...] = D[x, y, z].astype(F32)

    return [
        down(),
        hidden("G", G, g_o, rg, "x", "z"),
        hidden("U", U, u_o, ru, "z", "x"),
        attention("O", O, o_o, ro),
        attention("Q", Q, q_o, rq),
    ]


TOK = 256
FF = 2560


def mm(a, b):
    return jnp.dot(a, b, preferred_element_type=F32)


def mm_t(a, b):
    return lax.dot_general(a, b, (((1,), (1,)), ((), ())), preferred_element_type=F32)


def t_mm(a, b):
    return lax.dot_general(a, b, (((0,), (0,)), ((), ())), preferred_element_type=F32)


def constants():
    d = np.arange(D)
    spread = np.zeros((D, DP), np.float32)
    spread[d, 16 * (d // 14) + d % 14] = 1
    pick = np.zeros((64, DP), np.float32)
    pick[np.arange(64), 16 * np.arange(64) + 14] = 1
    own14 = (np.arange(64)[:, None] == d[None] // 14).astype(np.float32)
    j = np.arange(QKV)
    own18 = (np.arange(64)[:, None] == j[None] // 18).astype(np.float32)
    lane = np.arange(128)[:, None]
    e1 = (lane == d[None] % 14).astype(np.float32)
    e2 = (lane == 32 + d[None] % 14).astype(np.float32)
    eb = (lane == 64 + j[None] % 18).astype(np.float32)
    return [jnp.asarray(a, BF) for a in (spread, pick, own14, own18, e1, e2, eb)]


CONST = ("spread", "pick", "own14", "own18", "e1", "e2", "eb")


def cols(buf, start, size):
    value = buf[:, :, :, :, pl.ds(start, size)]
    return value.reshape(-1, size)


def put(ref, value):
    ref[...] = value.reshape(ref.shape)


def rotate(x, lo32):
    return jnp.where(lo32, pltpu.roll(x, 96, 1), pltpu.roll(x, 32, 1))


def lane_is(shape, width, below):
    lane = lax.broadcasted_iota(jnp.int32, shape, 1)
    return lax.rem(lane, width) < below


def gains(R):
    q = cols(R.Q, 0, 128)
    s = mm(R.pick[...], q).astype(BF)
    R.g1[...] = jnp.sum(mm(s, R.e1[...]) * R.own14[...].astype(F32), axis=0, keepdims=True)
    R.g2[...] = jnp.sum(mm(s, R.e2[...]) * R.own14[...].astype(F32), axis=0, keepdims=True)
    R.bias[...] = jnp.sum(mm(s, R.eb[...]) * R.own18[...].astype(F32), axis=0, keepdims=True)


def inverse_rms(h):
    return lax.rsqrt(jnp.sum(h * h, axis=-1, keepdims=True) * (1.0 / D) + norm_epsilon)


def project_qkv(R, source):
    h = source[...].astype(F32)
    n1 = (h * inverse_rms(h) * R.g1[...]).astype(BF)
    R.N1[...] = mm(n1, R.spread[...]).astype(BF)
    lo32 = lane_is((TOK, 128), 64, 32)
    cos, sin = R.cos[...], R.sin[...]
    for start, size in ((0, 256), (256, 256), (512, 256), (768, 256), (1024, 128)):
        out = mm(R.N1[...], cols(R.Q, start, size)) + R.bias[:, start:start + size]
        for k in range(size // 128):
            x = out[:, 128 * k:128 * k + 128]
            tile = (start + 128 * k) // 128
            if tile < 8:
                x = x * cos + rotate(x, lo32) * sin
            if tile < 7:
                R.QR[:, 128 * tile:128 * tile + 128] = x.astype(BF)
            else:
                x = x.astype(BF).astype(F32)
                swapped = pltpu.roll(x, 64, 1)
                lo = lane_is((TOK, 128), 128, 64)
                R.KV[tile - 7, 0] = jnp.where(lo, x, swapped).astype(BF)
                R.KV[tile - 7, 1] = x.astype(BF)
                R.KV[tile - 7, 2] = jnp.where(lo, swapped, x).astype(BF)


def two_heads(R, tile):
    return jnp.concatenate([tile * R.lanes[0], tile * R.lanes[1]], axis=0)


def beside(x):
    return jnp.concatenate([x[:SEQ], x[SEQ:]], axis=1)


def tile_at(t):
    return pl.ds(pl.multiple_of(t * 128, 128), 128)


def variant_of(t):
    return jnp.where(t < 3, 0, jnp.where(t > 3, 2, 1))


def probs_of(R, b, t, rows):
    q2 = two_heads(R, R.QR[rows, tile_at(t)])
    kk = R.KV[0, variant_of(t), rows]
    mask = R.mask[b]
    s = mm_t(q2, kk) * 0.125 + jnp.concatenate([mask, mask], axis=0)
    e = jnp.exp(s - jnp.max(s, axis=-1, keepdims=True))
    p = e / jnp.sum(e, axis=-1, keepdims=True)
    return q2, kk, p


def attend(R, b):
    rows = pl.ds(b * SEQ, SEQ)

    def body(t, carry):
        _, _, p = probs_of(R, b, t, rows)
        vv = two_heads(R, R.KV[1, variant_of(t), rows])
        R.DQKV[rows, tile_at(t)] = mm(beside(p.astype(BF)), vv).astype(BF)
        return carry

    lax.fori_loop(0, 7, body, 0)


def after_attention(R, source):
    R.CP[...] = mm(R.DQKV[:, :D], R.spread[...]).astype(BF)
    mid = source[...].astype(F32) + mm(R.CP[...], cols(R.O, 0, D))
    R.MID[...] = mid
    n2 = (mid * inverse_rms(mid) * R.g2[...]).astype(BF)
    R.N2[0:TOK] = mm(n2, R.spread[...]).astype(BF)


def exchange(R, k, src, dst, device):
    return pltpu.make_async_remote_copy(
        src_ref=src, dst_ref=dst, send_sem=R.xs.at[k], recv_sem=R.xr.at[k],
        device_id=device, device_id_type=MESH,
    )


def hidden(R, rows):
    def body(j, carry):
        at = pl.ds(pl.multiple_of(j * 256, 256), 256)
        n2 = R.N2[rows]
        gate = mm(n2, R.G[:, :, :, :, at].reshape(DP, 256))
        up = mm(n2, R.U[:, :, :, :, at].reshape(DP, 256))
        R.GA[rows, at] = gate.astype(BF)
        R.UP[rows, at] = up.astype(BF)
        R.ACT[rows, at] = (gate / (1.0 + jnp.exp(-gate)) * up).astype(BF)
        return carry

    lax.fori_loop(0, FF // 256, body, 0)


def feed_forward(R, place):
    own, other = pl.ds(0, TOK), pl.ds(TOK, TOK)
    n2 = exchange(R, 0, R.N2.at[own], R.N2.at[other], place.mate())
    n2.start()
    hidden(R, own)
    n2.wait_recv()
    hidden(R, other)
    down = R.D[...].reshape(FF, D)
    R.DB[...] = mm(R.ACT[other], down).astype(BF)
    part = exchange(R, 1, R.DB, R.DC, place.mate())
    part.start()
    y = R.MID[...] + mm(R.ACT[own], R.D[...].reshape(FF, D))
    part.wait_recv()
    R.y[...] = (y + R.DC[...].astype(F32)).astype(BF)
    n2.wait_send()
    part.wait_send()


def hidden_back(R, rows, acc):
    acc[...] = jnp.zeros_like(acc)

    def body(j, carry):
        at = pl.ds(pl.multiple_of(j * 640, 640), 640)
        down = R.D[j].reshape(640, D)
        for start, size in ((0, 256), (256, 256), (512, 128)):
            sub = pl.ds(pl.multiple_of(j * 640 + start, 128), size)
            dact = mm_t(R.DY[rows], down[start:start + size])
            gate = R.GA[rows, sub].astype(F32)
            up = R.UP[rows, sub].astype(F32)
            sig = 1.0 / (1.0 + jnp.exp(-gate))
            R.GA[rows, sub] = (dact * up * sig * (1.0 + gate * (1.0 - sig))).astype(BF)
            R.UP[rows, sub] = (dact * gate * sig).astype(BF)
        acc[...] += mm_t(R.GA[rows, at], R.G[:, :, :, :, at].reshape(DP, 640))
        acc[...] += mm_t(R.UP[rows, at], R.U[:, :, :, :, at].reshape(DP, 640))
        return carry

    lax.fori_loop(0, FF // 640, body, 0)


def attend_back(R, b):
    rows = pl.ds(b * SEQ, SEQ)
    R.dkv[...] = jnp.zeros_like(R.dkv)
    cos, sin = R.cos[rows], R.sin[rows]
    lo32 = lane_is((SEQ, 128), 64, 32)

    def spin_back(g):
        return g * cos + rotate(g * sin, lo32)

    def body(t, carry):
        q2, kk, p = probs_of(R, b, t, rows)
        var = variant_of(t)
        dc2 = two_heads(R, R.DC[rows, tile_at(t)])
        dp = mm_t(dc2, R.KV[1, var, rows])
        ds = (p * (dp - jnp.sum(p * dp, axis=-1, keepdims=True))).astype(BF)
        R.dkv[0, var] += t_mm(ds, q2)
        R.dkv[1, var] += t_mm(p.astype(BF), dc2)
        dq = mm(beside(ds), two_heads(R, kk)) * 0.125
        R.DQKV[rows, tile_at(t)] = spin_back(dq).astype(BF)
        return carry

    lax.fori_loop(0, 7, body, 0)
    lo = lane_is((SEQ, 128), 128, 64)

    def joined(k):
        first, mixed, last = R.dkv[k, 0], R.dkv[k, 1], R.dkv[k, 2]
        return mixed + jnp.where(
            lo, first + pltpu.roll(first, 64, 1), last + pltpu.roll(last, 64, 1)
        )

    R.DQKV[rows, 896:1024] = spin_back(joined(0) * 0.125).astype(BF)
    R.DQKV[rows, 1024:1152] = joined(1).astype(BF)


def backward(R, place):
    own, other = pl.ds(0, TOK), pl.ds(TOK, TOK)
    dy = exchange(R, 3, R.DY.at[own], R.DY.at[other], place.mate())
    dy.start()
    dy.wait_recv()
    hidden_back(R, other, R.acc)
    R.dn[...] = R.acc[...].astype(BF)
    dn = exchange(R, 4, R.dn, R.dn_in, place.mate())
    dn.start()
    hidden_back(R, own, R.acc)
    dn.wait_recv()
    dn2p = (R.acc[...] + R.dn_in[...].astype(F32)).astype(BF)
    dn2 = mm_t(dn2p, R.spread[...])
    mid = R.MID[...]
    inv2 = inverse_rms(mid)
    R.dg2[...] = jnp.sum(dn2 * mid * inv2, axis=0, keepdims=True)
    scaled = dn2 * R.g2[...]
    mean = jnp.sum(scaled * mid, axis=-1, keepdims=True) * (1.0 / D)
    dmid = R.DY[own].astype(F32) + inv2 * scaled - mid * (inv2 * inv2 * inv2 * mean)
    R.MID[...] = dmid
    R.DB[...] = dmid.astype(BF)
    dctx = mm_t(R.DB[...], cols(R.O, 0, D)).astype(BF)
    R.DC[...] = mm_t(dctx, R.spread[...]).astype(BF)
    attend_back(R, 0)
    attend_back(R, 1)
    dqkv = R.DQKV[...]
    R.dbias[...] = jnp.sum(dqkv.astype(F32), axis=0, keepdims=True)
    dn1 = mm_t(mm_t(dqkv, cols(R.Q, 0, QKV)).astype(BF), R.spread[...])
    h = R.h[...].astype(F32)
    inv1 = inverse_rms(h)
    R.dg1[...] = jnp.sum(dn1 * h * inv1, axis=0, keepdims=True)
    scaled = dn1 * R.g1[...]
    mean = jnp.sum(scaled * h, axis=-1, keepdims=True) * (1.0 / D)
    R.dh[...] = (R.MID[...] + inv1 * scaled - h * (inv1 * inv1 * inv1 * mean)).astype(BF)
    dy.wait_send()
    dn.wait_send()


def weight_grads(R, done, t):
    def down(x, carry):
        at = pl.ds(pl.multiple_of(x * 640, 640), 640)
        for start, size in ((0, 512), (512, 384)):
            grad = t_mm(R.ACT[:, at], R.DY[:, start:start + size])
            put(R.D.at[x, :, :, :, pl.ds(start, size)], grad.astype(BF))
        return carry

    yield t
    lax.fori_loop(0, 4, down, 0)
    done.add("D")
    for name, buf, grad in (("G", R.G, R.GA), ("U", R.U, R.UP)):
        def tile(x, carry):
            n2 = R.N2[:, pl.ds(pl.multiple_of(x * 256, 256), 256)]
            for start in range(0, FF, 512):
                at = pl.ds(start, 512)
                put(buf.at[x, :, :, :, at], t_mm(n2, grad[:, at]).astype(BF))
            return carry

        t += 3.0
        yield t
        lax.fori_loop(0, 4, tile, 0)
        done.add(name)
    t += 3.0
    yield t

    def out_rows(x, carry):
        rows = pl.ds(pl.multiple_of(x * 256, 256), 256)
        put(R.O.at[x], t_mm(R.CP[:, rows], R.DB[...]).astype(BF))
        return carry

    lax.fori_loop(0, 4, out_rows, 0)
    done.add("O")
    t += 1.0
    yield t
    small = (
        mm_t((R.own14[...].astype(F32) * R.dg1[...]).astype(BF), R.e1[...])
        + mm_t((R.own14[...].astype(F32) * R.dg2[...]).astype(BF), R.e2[...])
        + mm_t((R.own18[...].astype(F32) * R.dbias[...]).astype(BF), R.eb[...])
    )
    R.small[...] = small.astype(BF)

    def qkv_rows(x, carry):
        rows = pl.ds(pl.multiple_of(x * 256, 256), 256)
        n1 = R.N1[:, rows]
        for start in range(0, QKV, 384):
            g = t_mm(n1, R.DQKV[:, start:start + 384])
            if start == 0:
                g = jnp.concatenate([g[:, :128] + t_mm(R.pick[:, rows], R.small[...]), g[:, 128:]], axis=1)
            put(R.Q.at[x, :, :, :, pl.ds(start, 384)], g.astype(BF))
        return carry

    lax.fori_loop(0, 4, qkv_rows, 0)
    done.add("Q")


INS = ("g_in", "u_in", "d_in", "q_in", "o_in", "tokens", "og", "cos", "sin", "mask") + CONST
OUTS = ("y", "dh", "g_o", "u_o", "d_o", "q_o", "o_o")
LOCAL = (
    ("h", (TOK, D), BF), ("N1", (TOK, DP), BF), ("QR", (TOK, D), BF),
    ("KV", (2, 3, TOK, 128), BF), ("CP", (TOK, DP), BF),
    ("MID", (TOK, D), F32), ("N2", (2 * TOK, DP), BF), ("GA", (2 * TOK, FF), BF),
    ("UP", (2 * TOK, FF), BF), ("ACT", (2 * TOK, FF), BF), ("DY", (2 * TOK, D), BF), ("acc", (TOK, DP), F32), ("dn", (TOK, DP), BF), ("dn_in", (TOK, DP), BF),
    ("DB", (TOK, D), BF), ("DC", (TOK, D), BF), ("DQKV", (TOK, QKV), BF),
    ("dkv", (2, 3, SEQ, 128), F32), ("lanes", (2, SEQ, 128), BF),
    ("small", (64, 128), BF),
    ("g1", (1, D), F32), ("g2", (1, D), F32), ("bias", (1, QKV), F32),
    ("dg1", (1, D), F32), ("dg2", (1, D), F32), ("dbias", (1, QKV), F32),
)


def layers_kernel(*refs):
    names = INS + OUTS + tuple("GUDQO") + tuple(name for name, _, _ in LOCAL)
    R = SimpleNamespace(**dict(zip(names, refs)))
    rest = refs[len(names):]
    land = rest[:N_RS_SCRATCH]
    R.ss, R.rs, R.ls, R.xs, R.xr = rest[N_RS_SCRATCH:]
    place = Place()
    first = place.s == 0
    greet(place)
    wire = Wire(R.ss, R.rs)
    bufs = (R.G, R.U, R.D, R.Q, R.O)
    done = set()

    def early():
        lo = lane_is((SEQ, 128), 128, 64).astype(F32)
        R.lanes[0] = lo.astype(BF)
        R.lanes[1] = (1.0 - lo).astype(BF)
        t = 20.0
        while not {"Q", "O"} <= done:
            yield t
            t += 1.0
        gains(R)
        project_qkv(R, R.tokens)
        t += 5.0
        yield t
        attend(R, 0)
        t += 5.0
        yield t
        attend(R, 1)
        t += 5.0
        yield t
        after_attention(R, R.tokens)

    @pl.when(first)
    def _():
        R.h[...] = R.tokens[...]

    ins = (R.g_in, R.u_in, R.d_in, R.q_in, R.o_in)
    interleave(gather_flows(wire, place, ins, bufs, R.ls, done) + [early()])

    hop_h = exchange(R, 2, R.y, R.h, place.beyond())
    hop_dy = exchange(R, 5, R.dh, R.DY.at[pl.ds(0, TOK)], place.beyond())

    @pl.when(place.s == 1)
    def _():
        R.DY[0:TOK] = R.og[...]
        hop_h.wait_recv()
        project_qkv(R, R.h)
        attend(R, 0)
        attend(R, 1)
        after_attention(R, R.h)

    feed_forward(R, place)

    @pl.when(first)
    def _():
        hop_h.start()
        hop_dy.wait_recv()

    backward(R, place)

    @pl.when(place.s == 1)
    def _():
        hop_dy.start()

    wire.drain()
    outs = (R.g_o, R.u_o, R.d_o, R.q_o, R.o_o)
    made = set()
    flows = scatter_flows(wire, place, bufs, land, made, outs)
    interleave([weight_grads(R, made, 0.0)] + flows)
    wire.drain()

    @pl.when(first)
    def _():
        hop_h.wait_send()

    @pl.when(place.s == 1)
    def _():
        hop_dy.wait_send()


N_WIRE = 208


def run_layers(ins):
    outs = [(TOK, D), (TOK, D), (2, 16, 2560), (2, 16, 2560), (80, 896), (16, 1152), (16, 896)]
    kinds = [BF, BF] + [F32] * 5
    vmem = pl.BlockSpec(memory_space=pltpu.VMEM)
    dma = pltpu.SemaphoreType.DMA
    return pl.pallas_call(
        layers_kernel,
        out_shape=[jax.ShapeDtypeStruct(s, k) for s, k in zip(outs, kinds)],
        in_specs=[vmem] * len(INS),
        out_specs=[vmem] * len(OUTS),
        scratch_shapes=[pltpu.VMEM(s, BF) for s in bufs_shapes()]
        + [pltpu.VMEM(s, k) for _, s, k in LOCAL]
        + rs_scratch()
        + [dma((N_WIRE,)), dma((N_WIRE,)), dma((5,)), dma((6,)), dma((6,))],
        compiler_params=pltpu.CompilerParams(
            collective_id=0, has_side_effects=True, vmem_limit_bytes=63 * 2**20
        ),
        name="two_layers",
    )(*ins)


def rope_tables(segment_row, head_size):
    length = segment_row.shape[0]
    places = jnp.arange(length, dtype=jnp.int32)
    changes = jnp.concatenate(
        [jnp.ones((1,), jnp.int32), (segment_row[1:] != segment_row[:-1]).astype(jnp.int32)]
    )
    starts = lax.cummax(places * changes, axis=0)
    offsets = (places - starts).astype(F32)
    ladder = jnp.arange(head_size // 2, dtype=F32) * (-2.0 * math.log(rope_base) / head_size)
    angles = offsets[:, None] * jnp.exp(ladder)[None, :]
    cos, sin = jnp.cos(angles), jnp.sin(angles)
    return (
        jnp.concatenate([cos, cos, cos, cos], axis=-1),
        jnp.concatenate([-sin, sin, -sin, sin], axis=-1),
    )


def mask_of(segment_row):
    places = jnp.arange(segment_row.shape[0], dtype=jnp.int32)
    seen = (segment_row[:, None] == segment_row[None, :]) & (places[None, :] <= places[:, None])
    return jnp.where(seen, 0.0, -1e30).astype(F32)


def pack_hidden(w):
    w = jnp.pad(w.reshape(14, 32, 2, 76), ((0, 2), (0, 0), (0, 0), (0, 4)))
    return w.transpose(2, 0, 1, 3).reshape(2, 16, 2560)


def unpack_hidden(g):
    g = g.reshape(2, 16, 32, 80)[:, :14, :, :76]
    return g.transpose(1, 2, 0, 3).reshape(14, 4864)


def shards(
    tokens_in, out_grad, segments, norm1_gain, qkv_weight, qkv_bias, out_weight, norm2_gain,
    gate_weight, up_weight, down_weight,
):
    half = MICRO * SEQ
    rows = segments[:, 0]
    cos, sin = jax.vmap(rope_tables, in_axes=(0, None))(rows, HEAD_DIM)
    small_row = jnp.concatenate(
        [jnp.pad(norm1_gain[0], (0, 18)), jnp.pad(norm2_gain[0], (0, 18)), jnp.pad(qkv_bias[0], (0, 1152 - 82))]
    )
    y, dh, g, u, d, q, o = run_layers([
        pack_hidden(gate_weight[0]),
        pack_hidden(up_weight[0]),
        jnp.pad(down_weight[0], ((0, 4), (0, 0))),
        jnp.concatenate([qkv_weight[0], small_row[None], jnp.zeros((1, QKV), BF)], axis=0),
        jnp.pad(out_weight[0], ((0, 2), (0, 0))),
        tokens_in.reshape(half, D),
        out_grad.reshape(half, D),
        cos.reshape(half, 128),
        sin.reshape(half, 128),
        jax.vmap(mask_of)(rows),
        *constants(),
    ])
    shape = (1, MICRO, 1, SEQ, D)
    return (
        y.reshape(shape),
        dh.reshape(shape),
        q[14, 0:14][None],
        q[:14][None],
        q[14, 64:82][None],
        o[:14][None],
        q[14, 32:46][None],
        unpack_hidden(g)[None],
        unpack_hidden(u)[None],
        d[:76][None],
    )


def solution(mesh):
    in_specs = (
        P(None, "fsdp", None, None),
        P(None, "fsdp", None, None),
        P(None, "fsdp", None),
        P("section", "fsdp"),
        P("section", "fsdp", None),
        P("section", "fsdp"),
        P("section", "fsdp", None),
        P("section", "fsdp"),
        P("section", "fsdp", None),
        P("section", "fsdp", None),
        P("section", "fsdp", None),
    )
    out_specs = (
        P("section", None, "fsdp", None, None),
        P("section", None, "fsdp", None, None),
        P("section", "fsdp"),
        P("section", "fsdp", None),
        P("section", "fsdp"),
        P("section", "fsdp", None),
        P("section", "fsdp"),
        P("section", "fsdp", None),
        P("section", "fsdp", None),
        P("section", "fsdp", None),
    )
    return jax.shard_map(shards, mesh=mesh, in_specs=in_specs, out_specs=out_specs, check_vma=False)
```

```python
import math
from types import SimpleNamespace

import jax
import jax.numpy as jnp
from jax import lax
from jax.experimental import pallas as pl
from jax.experimental.pallas import tpu as pltpu
from jax.sharding import PartitionSpec as P
import numpy as np

HEADS = 14
KV_HEADS = 2
HEAD_DIM = 64
MICRO = 2
SEQ = 128
D = 896
DP = 1024
QKV = 1152
norm_epsilon = 1e-06
rope_base = 1000000.0

MESH = pl.DeviceIdType.MESH
BF = jnp.bfloat16
F32 = jnp.float32


class Place:
    def __init__(self):
        f = lax.axis_index("fsdp")
        self.s = lax.axis_index("section")
        self.c = lax.rem(f, 2)
        self.z = lax.rem(f // 2, 4)
        self.y = lax.rem(f // 8, 2)
        self.x = f // 16

    def at(self, x=None, y=None, z=None, c=None):
        x = self.x if x is None else x
        y = self.y if y is None else y
        z = self.z if z is None else z
        c = self.c if c is None else c
        return (self.s, ((x * 2 + y) * 4 + z) * 2 + c)

    def step(self, axis, k):
        here = self.x if axis == "x" else self.z
        return lax.rem(here + (k + 4), 4)

    def to(self, axis, k):
        return self.at(**{axis: self.step(axis, k)})

    def across(self):
        return self.at(y=1 - self.y)

    def mate(self):
        return self.at(c=1 - self.c)

    def beyond(self):
        return (1 - self.s, self.at(y=1 - self.y)[1])


def greet(place):
    barrier = pltpu.get_barrier_semaphore()
    near = (
        place.to("x", 1), place.to("x", -1), place.to("z", 1), place.to("z", -1),
        place.across(), place.mate(), place.beyond(),
    )
    for device in near:
        pl.semaphore_signal(barrier, inc=1, device_id=device, device_id_type=MESH)
    pl.semaphore_wait(barrier, len(near))


class Wire:
    def __init__(self, send_sems, recv_sems):
        self.send_sems, self.recv_sems = send_sems, recv_sems
        self.count, self.started = 0, []

    def send(self, src, dst, device):
        k = self.count
        self.count += 1
        assert k < self.send_sems.shape[0]
        copy = pltpu.make_async_remote_copy(
            src_ref=src, dst_ref=dst, send_sem=self.send_sems.at[k],
            recv_sem=self.recv_sems.at[k], device_id=device, device_id_type=MESH,
        )
        copy.start()
        self.started.append(copy)
        return copy

    def drain(self):
        for copy in self.started:
            copy.wait_send()
        self.started = []


def interleave(flows):
    waiting = [(next(flow), k, flow) for k, flow in enumerate(flows)]
    while waiting:
        waiting.sort(key=lambda item: item[:2])
        _, k, flow = waiting.pop(0)
        try:
            waiting.append((next(flow), k, flow))
        except StopIteration:
            pass


def gather_yab(wire, place, slot, first, last, ready, t0, unit):
    x, y, z = place.x, place.y, place.z
    yield t0
    for wait in ready:
        wait()
    cross = wire.send(slot(x, y, z), slot(x, y, z), place.across())

    def pos(a, b):
        return (b, a) if first == "z" else (a, b)

    def piece(a, b, half=None):
        px, pz = pos(a, b)
        return slot(px, half, pz)

    mine = {"x": x, "z": z}
    a0, b0 = mine[first], mine[last]
    t = t0 + unit * 1
    yield t
    cross.wait_recv()
    a_r = wire.send(piece(a0, b0), piece(a0, b0), place.to(first, 1))
    a_l = wire.send(piece(a0, b0), piece(a0, b0), place.to(first, -1))

    def last_sends(a):
        r = wire.send(piece(a, b0), piece(a, b0), place.to(last, 1))
        l = wire.send(piece(a, b0), piece(a, b0), place.to(last, -1))
        return r, l

    def last_forward(a, r, l):
        r.wait_recv()
        bm = place.step(last, -1)
        r2 = wire.send(piece(a, bm, 0), piece(a, bm, 0), place.to(last, 1))
        l.wait_recv()
        bp = place.step(last, 1)
        l2 = wire.send(piece(a, bp, 1), piece(a, bp, 1), place.to(last, -1))
        return r2, l2

    w0 = last_sends(a0)
    t += unit * 2
    yield t
    a_r.wait_recv()
    am = place.step(first, -1)
    a_r2 = wire.send(piece(am, b0, 0), piece(am, b0, 0), place.to(first, 1))
    a_l.wait_recv()
    ap = place.step(first, 1)
    a_l2 = wire.send(piece(ap, b0, 1), piece(ap, b0, 1), place.to(first, -1))
    w1 = last_sends(am)
    w2 = last_sends(ap)
    t += unit * 2
    yield t
    f0 = last_forward(a0, *w0)
    t += unit * 2
    yield t
    a_r2.wait_recv()
    a_l2.wait_recv()
    aq = place.step(first, 2)
    w3 = last_sends(aq)
    t += unit * 2
    yield t
    f1 = last_forward(am, *w1)
    t += unit * 2
    yield t
    f2 = last_forward(ap, *w2)
    t += unit * 2
    yield t
    f3 = last_forward(aq, *w3)
    t += unit * 2
    yield t
    for pair in (f0, f1, f2, f3):
        for copy in pair:
            copy.wait_recv()


def gather_aby(wire, place, slot, parts, t0, unit):
    x, y, z = place.x, place.y, place.z
    yield t0
    r = wire.send(slot(x, y, z), slot(x, y, z), place.to("x", 1))
    l = wire.send(slot(x, y, z), slot(x, y, z), place.to("x", -1))
    t = t0 + unit
    yield t
    r.wait_recv()
    xm, xp = place.step("x", -1), place.step("x", 1)
    r2 = wire.send(parts(xm, y, z, 0), parts(xm, y, z, 0), place.to("x", 1))
    l.wait_recv()
    l2 = wire.send(parts(xp, y, z, 1), parts(xp, y, z, 1), place.to("x", -1))
    t += unit
    yield t
    r2.wait_recv()
    l2.wait_recv()
    zr = wire.send(slot(None, y, z), slot(None, y, z), place.to("z", 1))
    zl = wire.send(slot(None, y, z), slot(None, y, z), place.to("z", -1))
    y0 = wire.send(slot(None, y, z), slot(None, y, z), place.across())
    t += unit * 4
    yield t
    zm, zp, zq = place.step("z", -1), place.step("z", 1), place.step("z", 2)
    zr.wait_recv()
    zr2 = wire.send(slot(0, y, zm), slot(0, y, zm), place.to("z", 1))
    y1 = wire.send(slot(None, y, zm), slot(None, y, zm), place.across())
    zl.wait_recv()
    zl2 = wire.send(slot(1, y, zp), slot(1, y, zp), place.to("z", -1))
    y2 = wire.send(slot(None, y, zp), slot(None, y, zp), place.across())
    t += unit * 4
    yield t
    zr2.wait_recv()
    zl2.wait_recv()
    y3 = wire.send(slot(None, y, zq), slot(None, y, zq), place.across())
    t += unit * 10
    yield t
    for copy in (y0, y1, y2, y3):
        copy.wait_recv()


BLOCK = dict(G=(32, 2560), U=(32, 2560), D=(80, 896), Q=(32, 1152), O=(32, 896))


def gather_flows(wire, place, ins, bufs, local_sems, done):
    x, y, z, c = place.x, place.y, place.z, place.c
    rows = pl.ds(pl.multiple_of(c * 16, 16), 16)
    G, U, D, Q, O = bufs
    g_in, u_in, d_in, q_in, o_in = ins
    own = []
    for k, (src, dst) in enumerate((
        (g_in.at[c], G.at[x, y, z, rows]), (u_in.at[c], U.at[x, y, z, rows]),
        (d_in, D.at[x, y, z]), (q_in, Q.at[x, y, z, rows]), (o_in, O.at[x, y, z, rows]),
    )):
        copy = pltpu.make_async_copy(src, dst, local_sems.at[k])
        copy.start()
        own.append(copy)
    swap_g = wire.send(g_in.at[1 - c], G.at[x, y, z, rows], place.mate())
    swap_u = wire.send(u_in.at[1 - c], U.at[x, y, z, rows], place.mate())

    def whole(buf):
        def slot(px, half, pz):
            if half is None:
                return buf.at[px, :, pz]
            return buf.at[px, half, pz]
        return slot

    def part(buf):
        def slot(px, half, pz):
            if half is None:
                return buf.at[px, :, pz, rows]
            return buf.at[px, half, pz, rows]
        return slot

    def down_slot(px, py, pz):
        if px is None:
            return D.at[:, py, pz]
        return D.at[px, py, pz]

    def down_zslot(px, py, pz):
        if px is None:
            return D.at[:, py, pz]
        if isinstance(px, int):
            return D.at[pl.ds(2 * px, 2), py, pz]
        return D.at[px, py, pz]

    def down_parts(px, py, pz, half):
        r = pl.ds(0, 48) if half == 0 else pl.ds(48, 32)
        return D.at[px, py, pz, r]

    def attention(name, buf, k, t0):
        yield from gather_yab(wire, place, part(buf), "z", "x", (own[k].wait,), t0, 1.0)
        mine = buf.at[:, :, :, rows]
        swap = wire.send(mine, mine, place.mate())
        yield t0 + 20.0
        swap.wait_recv()
        done.add(name)

    def down(t0):
        yield t0
        own[2].wait()
        yield from gather_aby(wire, place, down_zslot, down_parts, t0, 2.0)

    flows = [
        attention("Q", Q, 3, 0.0),
        attention("O", O, 4, 0.1),
        down(0.2),
        gather_yab(wire, place, whole(G), "z", "x", (own[0].wait, swap_g.wait_recv), 0.3, 4.0),
        gather_yab(wire, place, whole(U), "x", "z", (own[1].wait, swap_u.wait_recv), 0.4, 4.0),
    ]
    return flows


def bufs_shapes():
    return [(4, 2, 4) + BLOCK[k] for k in "GUDQO"]


def add(dst, *srcs):
    total = dst[...]
    for src in srcs:
        total = total + src[...]
    dst[...] = total


def add_each(count, dst, *srcs):
    def body(i, carry):
        add(dst(i), *[src(i) for src in srcs])
        return carry
    lax.fori_loop(0, count, body, 0)


def scatter_aby(wire, place, slot, R, first, last, t0, unit):
    r1a, r1b, r2a, r2b, s1a, s1b, s2a, s2b, t_buf = R
    mine = {"x": place.x, "z": place.z}
    a0, b0 = mine[first], mine[last]

    def piece(a, b, half=None):
        return slot(b, half, a) if first == "z" else slot(a, half, b)

    def blocks(a, b):
        return lambda i: piece(a, b, i)

    ap, am, aq = place.step(first, 1), place.step(first, -1), place.step(first, 2)
    order = [place.step(last, k) for k in (2, 1, -1)] + [b0]
    t = t0
    yield t
    one = []
    for k, b in enumerate(order):
        one.append((
            wire.send(piece(aq, b, 0), r1a.at[k], place.to(first, 1)),
            wire.send(piece(aq, b, 1), r1b.at[k], place.to(first, -1)),
        ))
    two = []
    for k, b in enumerate(order):
        t = t0 + unit * (k + 1)
        yield t
        one[k][0].wait_recv()
        add(piece(ap, b, 0), r1a.at[k])
        right = wire.send(piece(ap, b), r2a.at[k], place.to(first, 1))
        one[k][1].wait_recv()
        add(piece(am, b, 1), r1b.at[k])
        left = wire.send(piece(am, b), r2b.at[k], place.to(first, -1))
        two.append((right, left))
    t1 = t0 + unit * 4
    bp, bm, bq = order[1], order[2], order[0]

    def settle(k):
        two[k][0].wait_recv()
        two[k][1].wait_recv()
        for i in range(2):
            add(piece(a0, order[k], i), r2a.at[k, i], r2b.at[k, i])

    yield t1 + 2 * unit
    settle(0)
    d_r = wire.send(piece(a0, bq, 0), s1a, place.to(last, 1))
    d_l = wire.send(piece(a0, bq, 1), s1b, place.to(last, -1))
    yield t1 + 4 * unit
    settle(1)
    d_r.wait_recv()
    add(piece(a0, bp, 0), s1a)
    e_r = wire.send(piece(a0, bp), s2a, place.to(last, 1))
    yield t1 + 6 * unit
    settle(2)
    d_l.wait_recv()
    add(piece(a0, bm, 1), s1b)
    e_l = wire.send(piece(a0, bm), s2b, place.to(last, -1))
    yield t1 + 8 * unit
    settle(3)
    yield t1 + 9 * unit
    e_r.wait_recv()
    e_l.wait_recv()
    for i in range(2):
        add(piece(a0, b0, i), s2a.at[i], s2b.at[i])
    other = slot(place.x, 1 - place.y, place.z)
    cross = wire.send(other, t_buf, place.across())
    yield t1 + 10 * unit
    cross.wait_recv()
    add(slot(place.x, place.y, place.z), t_buf)


def scatter_down(wire, place, D, R, t0, unit):
    yb, z1a, z1b, z2a, z2b, xa, xb, x2a, x2b = R
    x, y, z = place.x, place.y, place.z
    zp, zm, zq = place.step("z", 1), place.step("z", -1), place.step("z", 2)
    xp, xm, xq = place.step("x", 1), place.step("x", -1), place.step("x", 2)
    top, low = pl.ds(0, 48), pl.ds(48, 32)
    lo, hi = pl.ds(0, 2), pl.ds(2, 2)
    order = (zq, zp, zm, z)
    yield t0
    crossing = [wire.send(D.at[:, 1 - y, b], yb.at[k], place.across()) for k, b in enumerate(order)]

    def settle(k):
        crossing[k].wait_recv()
        add_each(4, lambda i: D.at[i, y, order[k]], lambda i: yb.at[k, i])

    yield t0 + 3 * unit
    settle(0)
    d_r = wire.send(D.at[lo, y, zq], z1a, place.to("z", 1))
    d_l = wire.send(D.at[hi, y, zq], z1b, place.to("z", -1))
    yield t0 + 6 * unit
    settle(1)
    d_r.wait_recv()
    add_each(2, lambda i: D.at[i, y, zp], lambda i: z1a.at[i])
    e_r = wire.send(D.at[:, y, zp], z2a, place.to("z", 1))
    yield t0 + 9 * unit
    settle(2)
    d_l.wait_recv()
    add_each(2, lambda i: D.at[i + 2, y, zm], lambda i: z1b.at[i])
    e_l = wire.send(D.at[:, y, zm], z2b, place.to("z", -1))
    yield t0 + 12 * unit
    settle(3)
    yield t0 + 13 * unit
    e_r.wait_recv()
    e_l.wait_recv()
    add_each(4, lambda i: D.at[i, y, z], lambda i: z2a.at[i], lambda i: z2b.at[i])
    f_r = wire.send(D.at[xq, y, z, top], xa, place.to("x", 1))
    f_l = wire.send(D.at[xq, y, z, low], xb, place.to("x", -1))
    yield t0 + 14 * unit
    f_r.wait_recv()
    add(D.at[xp, y, z, top], xa)
    g_r = wire.send(D.at[xp, y, z], x2a, place.to("x", 1))
    f_l.wait_recv()
    add(D.at[xm, y, z, low], xb)
    g_l = wire.send(D.at[xm, y, z], x2b, place.to("x", -1))
    yield t0 + 15 * unit
    g_r.wait_recv()
    g_l.wait_recv()
    add(D.at[x, y, z], x2a, x2b)


def rs_scratch():
    def aby(rows, cols):
        shapes = [(4, rows, cols)] * 2 + [(4, 2, rows, cols)] * 2 + [(rows, cols)] * 2 + [(2, rows, cols)] * 2 + [(rows, cols)]
        return [pltpu.VMEM(s, BF) for s in shapes]
    out = []
    out += aby(32, 2560) + [pltpu.VMEM((16, 2560), BF)]
    out += aby(32, 2560) + [pltpu.VMEM((16, 2560), BF)]
    b = (80, 896)
    out += [pltpu.VMEM(s, BF) for s in (
        (4, 4) + b, (2,) + b, (2,) + b, (4,) + b, (4,) + b, (48, 896), (32, 896), b, b)]
    out += aby(16, 1152) + [pltpu.VMEM((4, 2, 4, 16, 1152), BF)]
    out += aby(16, 896) + [pltpu.VMEM((4, 2, 4, 16, 896), BF)]
    return out


N_RS_SCRATCH = 10 + 10 + 9 + 10 + 10


def scatter_flows(wire, place, bufs, R, made, outs):
    x, y, z, c = place.x, place.y, place.z, place.c
    G, U, D, Q, O = bufs
    g_o, u_o, d_o, q_o, o_o = outs
    rg, ru, rd, rq, ro = R[:10], R[10:20], R[20:29], R[29:39], R[39:49]
    rows = pl.ds(pl.multiple_of(c * 16, 16), 16)
    others = pl.ds(pl.multiple_of(16 - c * 16, 16), 16)

    def whole(buf):
        def slot(px, half, pz):
            return buf.at[px, :, pz] if half is None else buf.at[px, half, pz]
        return slot

    def part(buf):
        def slot(px, half, pz):
            return buf.at[px, :, pz, rows] if half is None else buf.at[px, half, pz, rows]
        return slot

    def made_of(name):
        t = 0.0
        while name not in made:
            yield t
            t += 0.5
        return t

    def hidden(name, buf, out, r, first, last):
        t0 = yield from made_of(name)
        yield from scatter_aby(wire, place, whole(buf), r[:9], first, last, t0, 4.0)
        swap = wire.send(buf.at[x, y, z, others], r[9], place.mate())
        yield 200.0
        swap.wait_recv()
        out[c] = buf[x, y, z, rows].astype(F32)
        out[1 - c] = r[9][...].astype(F32)

    def attention(name, buf, out, r):
        t0 = yield from made_of(name)
        swap = wire.send(buf.at[:, :, :, others], r[9], place.mate())
        yield t0 + 8.0
        swap.wait_recv()
        add_each(32, lambda i: buf.at[i // 8, lax.rem(i // 4, 2), lax.rem(i, 4), rows],
                 lambda i: r[9].at[i // 8, lax.rem(i // 4, 2), lax.rem(i, 4)])
        yield from scatter_aby(wire, place, part(buf), r[:9], "x", "z", t0 + 8.0, 1.0)
        out[...] = buf[x, y, z, rows].astype(F32)

    def down():
        t0 = yield from made_of("D")
        yield from scatter_down(wire, place, D, rd, t0, 4.0)
        d_o[...] = D[x, y, z].astype(F32)

    return [
        down(),
        hidden("G", G, g_o, rg, "x", "z"),
        hidden("U", U, u_o, ru, "z", "x"),
        attention("O", O, o_o, ro),
        attention("Q", Q, q_o, rq),
    ]


TOK = 256
FF = 2560


def mm(a, b):
    return jnp.dot(a, b, preferred_element_type=F32)


def mm_t(a, b):
    return lax.dot_general(a, b, (((1,), (1,)), ((), ())), preferred_element_type=F32)


def t_mm(a, b):
    return lax.dot_general(a, b, (((0,), (0,)), ((), ())), preferred_element_type=F32)


def constants():
    d = np.arange(D)
    spread = np.zeros((D, DP), np.float32)
    spread[d, 16 * (d // 14) + d % 14] = 1
    pick = np.zeros((64, DP), np.float32)
    pick[np.arange(64), 16 * np.arange(64) + 14] = 1
    own14 = (np.arange(64)[:, None] == d[None] // 14).astype(np.float32)
    j = np.arange(QKV)
    own18 = (np.arange(64)[:, None] == j[None] // 18).astype(np.float32)
    lane = np.arange(128)[:, None]
    e1 = (lane == d[None] % 14).astype(np.float32)
    eb = (lane == 64 + j[None] % 18).astype(np.float32)
    return [jnp.asarray(a, BF) for a in (spread, pick, own14, own18, e1, eb)]


CONST = ("spread", "pick", "own14", "own18", "e1", "eb")


def cols(buf, start, size):
    value = buf[:, :, :, :, pl.ds(start, size)]
    return value.reshape(-1, size)


def put(ref, value):
    ref[...] = value.reshape(ref.shape)


def rotate(x, lo32):
    return jnp.where(lo32, pltpu.roll(x, 96, 1), pltpu.roll(x, 32, 1))


def lane_is(shape, width, below):
    lane = lax.broadcasted_iota(jnp.int32, shape, 1)
    return lax.rem(lane, width) < below


def gains(R):
    q = cols(R.Q, 0, 128)
    s = mm(R.pick[...], q)
    s2 = pltpu.roll(s, 96, 1).astype(BF)
    s = s.astype(BF)
    R.g1[...] = jnp.sum(mm(s, R.e1[...]) * R.own14[...].astype(F32), axis=0, keepdims=True)
    R.g2[...] = jnp.sum(mm(s2, R.e1[...]) * R.own14[...].astype(F32), axis=0, keepdims=True)
    R.bias[...] = jnp.sum(mm(s, R.eb[...]) * R.own18[...].astype(F32), axis=0, keepdims=True)


def inverse_rms(h):
    return lax.rsqrt(jnp.sum(h * h, axis=-1, keepdims=True) * (1.0 / D) + norm_epsilon)


def project_qkv(R, source, tables, rows, size):
    h = source[rows].astype(F32)
    n1 = (h * inverse_rms(h) * R.g1[...]).astype(BF)
    R.N1[rows] = mm(n1, R.spread[...]).astype(BF)
    lo32 = lane_is((size, 128), 64, 32)
    lo = lane_is((size, 128), 128, 64)
    cos, sin = tables[0][rows], tables[1][rows]
    for start, width in ((0, 256), (256, 256), (512, 256), (768, 256), (1024, 128)):
        out = mm(R.N1[rows], cols(R.Q, start, width)) + R.bias[:, start:start + width]
        for k in range(width // 128):
            x = out[:, 128 * k:128 * k + 128]
            tile = (start + 128 * k) // 128
            if tile < 8:
                x = x * cos + rotate(x, lo32) * sin
            if tile < 7:
                R.QR[rows, 128 * tile:128 * tile + 128] = x.astype(BF)
            else:
                x = x.astype(BF).astype(F32)
                swapped = pltpu.roll(x, 64, 1)
                R.KV[tile - 7, 0, rows] = jnp.where(lo, x, swapped).astype(BF)
                R.KV[tile - 7, 1, rows] = x.astype(BF)
                R.KV[tile - 7, 2, rows] = jnp.where(lo, swapped, x).astype(BF)


def two_heads(R, tile):
    return jnp.concatenate([tile * R.lanes[0], tile * R.lanes[1]], axis=0)


def beside(x):
    return jnp.concatenate([x[:SEQ], x[SEQ:]], axis=1)


def variant_of(t):
    return 0 if t < 3 else (2 if t > 3 else 1)


def probs_of(R, mask, t, rows):
    q2 = two_heads(R, R.QR[rows, 128 * t:128 * t + 128])
    kk = R.KV[0, variant_of(t), rows]
    s = mm_t(q2, kk) * 0.125 + jnp.concatenate([mask, mask], axis=0)
    e = jnp.exp(s - jnp.max(s, axis=-1, keepdims=True))
    p = e * (1.0 / jnp.sum(e, axis=-1, keepdims=True))
    return q2, kk, p


def attend(R, tables, m):
    rows = own_rows(m)
    mask = tables[2][m]
    for t in range(7):
        _, _, p = probs_of(R, mask, t, rows)
        vv = two_heads(R, R.KV[1, variant_of(t), rows])
        R.DQKV[rows, 128 * t:128 * t + 128] = mm(beside(p.astype(BF)), vv).astype(BF)


def own_rows(m):
    return pl.ds(SEQ * m, SEQ)


def pair_own(m):
    return pl.ds(2 * SEQ * m, SEQ)


def pair_other(m):
    return pl.ds(2 * SEQ * m + SEQ, SEQ)


def pair(m):
    return pl.ds(2 * SEQ * m, 2 * SEQ)


def after_attention(R, source, m):
    rows = own_rows(m)
    R.CP[rows] = mm(R.DQKV[rows, :D], R.spread[...]).astype(BF)
    mid = source[rows].astype(F32) + mm(R.CP[rows], cols(R.O, 0, D))
    R.MID[rows] = mid
    n2 = (mid * inverse_rms(mid) * R.g2[...]).astype(BF)
    R.N2[pair_own(m)] = mm(n2, R.spread[...]).astype(BF)


def sigmoid(v):
    return 0.5 * jnp.tanh(0.5 * v) + 0.5


def hidden(R, m):
    rows = pair(m)

    def body(j, carry):
        at = pl.ds(pl.multiple_of(j * 256, 256), 256)
        n2 = R.N2[rows]
        gate = mm(n2, R.G[:, :, :, :, at].reshape(DP, 256))
        up = mm(n2, R.U[:, :, :, :, at].reshape(DP, 256))
        R.GA[rows, at] = gate.astype(BF)
        R.UP[rows, at] = up.astype(BF)
        R.ACT[rows, at] = (gate * sigmoid(gate) * up).astype(BF)
        return carry

    lax.fori_loop(0, FF // 256, body, 0)


class Swap:
    def __init__(self, R, place):
        own = own_rows
        mate, across, beyond = place.mate(), place.across(), place.beyond()

        def table(k, refs, device):
            return lambda m: pltpu.make_async_remote_copy(
                src_ref=refs(m)[0], dst_ref=refs(m)[1], send_sem=R.xs.at[2 * k + m],
                recv_sem=R.xr.at[2 * k + m], device_id=device, device_id_type=MESH,
            )

        self.n2 = table(0, lambda m: (R.N2.at[pair_own(m)], R.N2.at[pair_other(m)]), mate)
        self.part = table(1, lambda m: (R.DB.at[own(m)], R.DC.at[own(m)]), mate)
        self.dy = table(2, lambda m: (R.DY.at[pair_own(m)], R.DY.at[pair_other(m)]), mate)
        self.dn = table(3, lambda m: (R.dn, R.dn_in.at[own(m)]), mate)
        self.hop_h = table(4, lambda m: (R.ys.at[own(m)], R.h.at[own(m)]), beyond)
        self.hop_dy = table(5, lambda m: (R.dhs.at[own(m)], R.DY.at[pair_own(m)]), beyond)
        self.og = table(6, lambda m: (R.og.at[own(m)], R.DY.at[pair_own(m)]), across)
        self.cos = table(7, lambda m: (R.cos.at[own(m)], R.tcos.at[own(m)]), across)
        self.sin = table(8, lambda m: (R.sin.at[own(m)], R.tsin.at[own(m)]), across)
        self.mask = table(9, lambda m: (R.mask.at[m], R.tmask.at[m]), across)
        self.y = table(10, lambda m: (R.ys.at[own(m)], R.y.at[own(m)]), across)
        self.dh = table(11, lambda m: (R.dhs.at[own(m)], R.dh.at[own(m)]), across)


N_SWAP = 24


def down_sent(R, swap, m):
    R.DB[own_rows(m)] = mm(R.ACT[pair_other(m)], R.D[...].reshape(FF, D)).astype(BF)
    swap.part(m).start()
    R.acc[0:SEQ, 0:D] = R.MID[own_rows(m)] + mm(R.ACT[pair_own(m)], R.D[...].reshape(FF, D))


def down_done(R, swap, m):
    swap.part(m).wait_recv()
    R.ys[own_rows(m)] = (R.acc[0:SEQ, 0:D] + R.DC[own_rows(m)].astype(F32)).astype(BF)
    swap.part(m).wait_send()


def hidden_back(R, m):
    rows = pair(m)

    def body(j, carry):
        down = R.D[j].reshape(640, D)
        for start, size in ((0, 256), (256, 256), (512, 128)):
            sub = pl.ds(pl.multiple_of(j * 640 + start, 128), size)
            dact = mm_t(R.DY[rows], down[start:start + size])
            gate = R.GA[rows, sub].astype(F32)
            up = R.UP[rows, sub].astype(F32)
            sig = sigmoid(gate)
            R.GA[rows, sub] = (dact * up * sig * (1.0 + gate * (1.0 - sig))).astype(BF)
            R.UP[rows, sub] = (dact * gate * sig).astype(BF)
        return carry

    lax.fori_loop(0, FF // 640, body, 0)


def normed_back(R, swap, m):
    rows = pair(m)
    R.acc[...] = jnp.zeros_like(R.acc)

    def body(j, carry):
        at = pl.ds(pl.multiple_of(j * 512, 512), 512)
        R.acc[...] += mm_t(R.GA[rows, at], R.G[:, :, :, :, at].reshape(DP, 512)) + mm_t(
            R.UP[rows, at], R.U[:, :, :, :, at].reshape(DP, 512)
        )
        return carry

    lax.fori_loop(0, FF // 512, body, 0)
    R.dn[...] = R.acc[SEQ:].astype(BF)
    swap.dn(m).start()
    R.dno[...] = R.acc[:SEQ]


def middle_back(R, swap, m):
    rows = own_rows(m)
    swap.dn(m).wait_recv()
    dn2p = (R.dno[...] + R.dn_in[rows].astype(F32)).astype(BF)
    dn2 = mm_t(dn2p, R.spread[...])
    mid = R.MID[rows]
    inv2 = inverse_rms(mid)
    R.dg2[m] = jnp.sum(dn2 * mid * inv2, axis=0, keepdims=True)
    scaled = dn2 * R.g2[...]
    mean = jnp.sum(scaled * mid, axis=-1, keepdims=True) * (1.0 / D)
    dmid = R.DY[pair_own(m)].astype(F32) + inv2 * scaled - mid * (inv2 * inv2 * inv2 * mean)
    R.MID[rows] = dmid
    R.DB[rows] = dmid.astype(BF)
    dctx = mm_t(R.DB[rows], cols(R.O, 0, D)).astype(BF)
    R.DC[rows] = mm_t(dctx, R.spread[...]).astype(BF)
    swap.dn(m).wait_send()


def attend_back(R, tables, m):
    rows = own_rows(m)
    cos, sin, mask = tables[0][rows], tables[1][rows], tables[2][m]
    lo32 = lane_is((SEQ, 128), 64, 32)
    lo = lane_is((SEQ, 128), 128, 64)

    def spin_back(g):
        return g * cos + rotate(g * sin, lo32)

    for t in range(7):
        q2, kk, p = probs_of(R, mask, t, rows)
        var = variant_of(t)
        dc2 = two_heads(R, R.DC[rows, 128 * t:128 * t + 128])
        dp = mm_t(dc2, R.KV[1, var, rows])
        ds = (p * (dp - jnp.sum(p * dp, axis=-1, keepdims=True))).astype(BF)
        dk, dv = t_mm(ds, q2), t_mm(p.astype(BF), dc2)
        if t in (0, 3, 4):
            R.dkv[0, var] = dk
            R.dkv[1, var] = dv
        else:
            R.dkv[0, var] += dk
            R.dkv[1, var] += dv
        dq = mm(beside(ds), two_heads(R, kk)) * 0.125
        R.DQKV[rows, 128 * t:128 * t + 128] = spin_back(dq).astype(BF)

    def joined(k):
        first, mixed, last = R.dkv[k, 0], R.dkv[k, 1], R.dkv[k, 2]
        return mixed + jnp.where(
            lo, first + pltpu.roll(first, 64, 1), last + pltpu.roll(last, 64, 1)
        )

    R.DQKV[rows, 896:1024] = spin_back(joined(0) * 0.125).astype(BF)
    R.DQKV[rows, 1024:1152] = joined(1).astype(BF)


def stream_back(R, m):
    rows = own_rows(m)
    dqkv = R.DQKV[rows]
    R.dbias[m] = jnp.sum(dqkv.astype(F32), axis=0, keepdims=True)
    dn1 = mm_t(mm_t(dqkv, cols(R.Q, 0, QKV)).astype(BF), R.spread[...])
    h = R.h[rows].astype(F32)
    inv1 = inverse_rms(h)
    R.dg1[m] = jnp.sum(dn1 * h * inv1, axis=0, keepdims=True)
    scaled = dn1 * R.g1[...]
    mean = jnp.sum(scaled * h, axis=-1, keepdims=True) * (1.0 / D)
    R.dhs[rows] = (R.MID[rows] + inv1 * scaled - h * (inv1 * inv1 * inv1 * mean)).astype(BF)


def weight_grads(R, done, t, rest):
    def down(x, carry):
        at = pl.ds(pl.multiple_of(x * 640, 640), 640)
        for start, size in ((0, 512), (512, 384)):
            grad = t_mm(R.ACT[:, at], R.DY[:, start:start + size])
            put(R.D.at[x, :, :, :, pl.ds(start, size)], grad.astype(BF))
        return carry

    yield t
    lax.fori_loop(0, 4, down, 0)
    done.add("D")
    t += 3.0
    yield t
    rest[0]()
    for name, buf, grad in (("G", R.G, R.GA), ("U", R.U, R.UP)):
        def tile(x, carry):
            n2 = R.N2[:, pl.ds(pl.multiple_of(x * 256, 256), 256)]
            for start in range(0, FF, 512):
                at = pl.ds(start, 512)
                put(buf.at[x, :, :, :, at], t_mm(n2, grad[:, at]).astype(BF))
            return carry

        t += 3.0
        yield t
        lax.fori_loop(0, 4, tile, 0)
        done.add(name)
    for piece in rest[1:]:
        t += 3.0
        yield t
        piece()
    t += 3.0
    yield t

    def out_rows(x, carry):
        rows = pl.ds(pl.multiple_of(x * 256, 256), 256)
        put(R.O.at[x], t_mm(R.CP[:, rows], R.DB[...]).astype(BF))
        return carry

    lax.fori_loop(0, 4, out_rows, 0)
    done.add("O")
    t += 1.0
    yield t
    small = (
        mm_t((R.own14[...].astype(F32) * (R.dg1[0] + R.dg1[1])).astype(BF), R.e1[...])
        + pltpu.roll(
            mm_t((R.own14[...].astype(F32) * (R.dg2[0] + R.dg2[1])).astype(BF), R.e1[...]), 32, 1
        )
        + mm_t((R.own18[...].astype(F32) * (R.dbias[0] + R.dbias[1])).astype(BF), R.eb[...])
    )
    R.small[...] = small.astype(BF)

    def qkv_rows(x, carry):
        rows = pl.ds(pl.multiple_of(x * 256, 256), 256)
        n1 = R.N1[:, rows]
        for start in range(0, QKV, 384):
            g = t_mm(n1, R.DQKV[:, start:start + 384])
            if start == 0:
                g = jnp.concatenate([g[:, :128] + t_mm(R.pick[:, rows], R.small[...]), g[:, 128:]], axis=1)
            put(R.Q.at[x, :, :, :, pl.ds(start, 384)], g.astype(BF))
        return carry

    lax.fori_loop(0, 4, qkv_rows, 0)
    done.add("Q")


INS = ("g_in", "u_in", "d_in", "q_in", "o_in", "tokens", "og", "cos", "sin", "mask") + CONST
IN_HBM = ("g_in", "u_in", "d_in", "q_in", "o_in", "og")
OUTS = ("y", "dh", "g_o", "u_o", "d_o", "q_o", "o_o")
LOCAL = (
    ("h", (TOK, D), BF), ("N1", (TOK, DP), BF), ("QR", (TOK, D), BF),
    ("KV", (2, 3, TOK, 128), BF), ("CP", (TOK, DP), BF),
    ("MID", (TOK, D), F32), ("N2", (2 * TOK, DP), BF), ("GA", (2 * TOK, FF), BF),
    ("UP", (2 * TOK, FF), BF), ("ACT", (2 * TOK, FF), BF), ("DY", (2 * TOK, D), BF), ("acc", (TOK, DP), F32), ("dn", (SEQ, DP), BF), ("dn_in", (TOK, DP), BF),
    ("DB", (TOK, D), BF), ("DC", (TOK, D), BF), ("DQKV", (TOK, QKV), BF),
    ("dkv", (2, 3, SEQ, 128), F32), ("lanes", (2, SEQ, 128), BF),
    ("small", (64, 128), BF),
    ("g1", (1, D), F32), ("g2", (1, D), F32), ("bias", (1, QKV), F32),
    ("dg1", (2, 1, D), F32), ("dg2", (2, 1, D), F32), ("dbias", (2, 1, QKV), F32),
    ("ys", (TOK, D), BF), ("dhs", (TOK, D), BF), ("dno", (SEQ, DP), F32),
    ("tcos", (TOK, 128), F32), ("tsin", (TOK, 128), F32), ("tmask", (2, SEQ, SEQ), F32),
)


def layers_kernel(*refs):
    names = INS + OUTS + tuple("GUDQO") + tuple(name for name, _, _ in LOCAL)
    R = SimpleNamespace(**dict(zip(names, refs)))
    rest = refs[len(names):]
    R.ss, R.rs, R.ls, R.xs, R.xr = rest[N_RS_SCRATCH:]
    place = Place()
    greet(place)
    wire = Wire(R.ss, R.rs)
    swap = Swap(R, place)
    bufs = (R.G, R.U, R.D, R.Q, R.O)
    done = set()
    given = (R.cos, R.sin, R.mask)
    tables = (R.tcos, R.tsin, R.tmask)

    def only(section):
        return lambda body: pl.when(place.s == section)(body)

    @only(0)
    def _():
        R.h[...] = R.tokens[...]
        for src, dst in zip(given, tables):
            dst[...] = src[...]

    @only(1)
    def _():
        for m in range(MICRO):
            for move in (swap.og, swap.cos, swap.sin, swap.mask):
                move(m).start()

    def early():
        lo = lane_is((SEQ, 128), 128, 64).astype(F32)
        R.lanes[0] = lo.astype(BF)
        R.lanes[1] = (1.0 - lo).astype(BF)
        t = 20.0
        while not {"Q", "O"} <= done:
            yield t
            t += 1.0
        gains(R)
        project_qkv(R, R.tokens, given, pl.ds(0, TOK), TOK)
        for m in range(MICRO):
            t += 5.0
            yield t
            attend(R, given, m)
            t += 3.0
            yield t
            after_attention(R, R.tokens, m)

            @only(0)
            def _():
                swap.n2(m).start()

    ins = (R.g_in, R.u_in, R.d_in, R.q_in, R.o_in)
    interleave(gather_flows(wire, place, ins, bufs, R.ls, done) + [early()])

    @only(0)
    def _():
        for m in range(MICRO):
            swap.n2(m).wait_recv()
            hidden(R, m)
            down_sent(R, swap, m)
            down_done(R, swap, m)
            swap.hop_h(m).start()
        R.y[...] = R.ys[...]
        swap.hop_dy(0).wait_recv()
        swap.dy(0).start()
        swap.dy(0).wait_recv()
        hidden_back(R, 0)
        normed_back(R, swap, 0)
        middle_back(R, swap, 0)
        attend_back(R, tables, 0)
        stream_back(R, 0)
        swap.hop_dy(1).wait_recv()
        swap.dy(1).start()
        swap.dy(1).wait_recv()
        hidden_back(R, 1)

    @only(1)
    def _():
        def start(m):
            swap.hop_h(m).wait_recv()
            rows = own_rows(m)
            project_qkv(R, R.h, tables, rows, SEQ)
            attend(R, tables, m)
            after_attention(R, R.h, m)
            swap.n2(m).start()

        def feed(m):
            swap.n2(m).wait_recv()
            hidden(R, m)
            down_sent(R, swap, m)
            down_done(R, swap, m)
            swap.y(m).start()

        def finish(m):
            middle_back(R, swap, m)
            attend_back(R, tables, m)
            stream_back(R, m)
            swap.hop_dy(m).start()
            swap.dh(m).start()

        for m in range(MICRO):
            for move in (swap.og, swap.cos, swap.sin, swap.mask):
                move(m).wait_recv()
            swap.dy(m).start()
        start(0)
        feed(0)
        start(1)
        swap.dy(0).wait_recv()
        hidden_back(R, 0)
        normed_back(R, swap, 0)
        feed(1)
        finish(0)
        swap.dy(1).wait_recv()
        hidden_back(R, 1)
        normed_back(R, swap, 1)
        finish(1)

    wire.drain()

    def rest_a():
        only(0)(lambda: normed_back(R, swap, 1))

    def rest_b():
        only(0)(lambda: middle_back(R, swap, 1))

    def rest_c():
        only(0)(lambda: attend_back(R, tables, 1))

    def rest_d():
        @only(0)
        def _():
            stream_back(R, 1)
            R.dh[...] = R.dhs[...]

    outs = (R.g_o, R.u_o, R.d_o, R.q_o, R.o_o)
    made = set()
    flows = scatter_flows(wire, place, bufs, rest[:N_RS_SCRATCH], made, outs)
    interleave([weight_grads(R, made, 0.0, (rest_a, rest_b, rest_c, rest_d))] + flows)
    wire.drain()
    for m in range(MICRO):
        swap.n2(m).wait_send()
        swap.dy(m).wait_send()

    @only(0)
    def _():
        for m in range(MICRO):
            swap.hop_h(m).wait_send()

    @only(1)
    def _():
        for m in range(MICRO):
            for move in (swap.og, swap.cos, swap.sin, swap.mask, swap.y, swap.dh, swap.hop_dy):
                move(m).wait_send()
            swap.y(m).wait_recv()
            swap.dh(m).wait_recv()


N_WIRE = 208


def run_layers(ins):
    outs = [(TOK, D), (TOK, D), (2, 16, 2560), (2, 16, 2560), (80, 896), (16, 1152), (16, 896)]
    kinds = [BF, BF] + [F32] * 5
    vmem = pl.BlockSpec(memory_space=pltpu.VMEM)
    dma = pltpu.SemaphoreType.DMA
    return pl.pallas_call(
        layers_kernel,
        out_shape=[jax.ShapeDtypeStruct(s, k) for s, k in zip(outs, kinds)],
        in_specs=[pl.BlockSpec(memory_space=pl.ANY) if n in IN_HBM else vmem for n in INS],
        out_specs=[vmem] * len(OUTS),
        scratch_shapes=[pltpu.VMEM(s, BF) for s in bufs_shapes()]
        + [pltpu.VMEM(s, k) for _, s, k in LOCAL]
        + rs_scratch()
        + [dma((N_WIRE,)), dma((N_WIRE,)), dma((5,)), dma((N_SWAP,)), dma((N_SWAP,))],
        compiler_params=pltpu.CompilerParams(
            collective_id=0, has_side_effects=True, vmem_limit_bytes=127 * 2**19
        ),
        name="two_layers",
    )(*ins)


def rope_tables(segment_row, head_size):
    length = segment_row.shape[0]
    places = jnp.arange(length, dtype=jnp.int32)
    changes = jnp.concatenate(
        [jnp.ones((1,), jnp.int32), (segment_row[1:] != segment_row[:-1]).astype(jnp.int32)]
    )
    starts = lax.cummax(places * changes, axis=0)
    offsets = (places - starts).astype(F32)
    ladder = jnp.arange(head_size // 2, dtype=F32) * (-2.0 * math.log(rope_base) / head_size)
    angles = offsets[:, None] * jnp.exp(ladder)[None, :]
    cos, sin = jnp.cos(angles), jnp.sin(angles)
    return (
        jnp.concatenate([cos, cos, cos, cos], axis=-1),
        jnp.concatenate([-sin, sin, -sin, sin], axis=-1),
    )


def mask_of(segment_row):
    places = jnp.arange(segment_row.shape[0], dtype=jnp.int32)
    seen = (segment_row[:, None] == segment_row[None, :]) & (places[None, :] <= places[:, None])
    return jnp.where(seen, 0.0, -1e30).astype(F32)


def pack_hidden(w):
    w = jnp.pad(w.reshape(14, 32, 2, 76), ((0, 2), (0, 0), (0, 0), (0, 4)))
    return w.transpose(2, 0, 1, 3).reshape(2, 16, 2560)


def unpack_hidden(g):
    g = g.reshape(2, 16, 32, 80)[:, :14, :, :76]
    return g.transpose(1, 2, 0, 3).reshape(14, 4864)


def shards(
    tokens_in, out_grad, segments, norm1_gain, qkv_weight, qkv_bias, out_weight, norm2_gain,
    gate_weight, up_weight, down_weight,
):
    half = MICRO * SEQ
    rows = segments[:, 0]
    cos, sin = jax.vmap(rope_tables, in_axes=(0, None))(rows, HEAD_DIM)
    small_row = jnp.concatenate(
        [jnp.pad(norm1_gain[0], (0, 18)), jnp.pad(norm2_gain[0], (0, 18)), jnp.pad(qkv_bias[0], (0, 1152 - 82))]
    )
    y, dh, g, u, d, q, o = run_layers([
        pack_hidden(gate_weight[0]),
        pack_hidden(up_weight[0]),
        jnp.pad(down_weight[0], ((0, 4), (0, 0))),
        jnp.concatenate([qkv_weight[0], small_row[None], jnp.zeros((1, QKV), BF)], axis=0),
        jnp.pad(out_weight[0], ((0, 2), (0, 0))),
        tokens_in.reshape(half, D),
        out_grad.reshape(half, D),
        cos.reshape(half, 128),
        sin.reshape(half, 128),
        jax.vmap(mask_of)(rows),
        *constants(),
    ])
    shape = (1, MICRO, 1, SEQ, D)
    return (
        y.reshape(shape),
        dh.reshape(shape),
        q[14, 0:14][None],
        q[:14][None],
        q[14, 64:82][None],
        o[:14][None],
        q[14, 32:46][None],
        unpack_hidden(g)[None],
        unpack_hidden(u)[None],
        d[:76][None],
    )


def solution(mesh):
    in_specs = (
        P(None, "fsdp", None, None),
        P(None, "fsdp", None, None),
        P(None, "fsdp", None),
        P("section", "fsdp"),
        P("section", "fsdp", None),
        P("section", "fsdp"),
        P("section", "fsdp", None),
        P("section", "fsdp"),
        P("section", "fsdp", None),
        P("section", "fsdp", None),
        P("section", "fsdp", None),
    )
    out_specs = (
        P("section", None, "fsdp", None, None),
        P("section", None, "fsdp", None, None),
        P("section", "fsdp"),
        P("section", "fsdp", None),
        P("section", "fsdp"),
        P("section", "fsdp", None),
        P("section", "fsdp"),
        P("section", "fsdp", None),
        P("section", "fsdp", None),
        P("section", "fsdp", None),
    )
    return jax.shard_map(shards, mesh=mesh, in_specs=in_specs, out_specs=out_specs, check_vma=False)
```

```python
import math
from types import SimpleNamespace

import jax
import jax.numpy as jnp
from jax import lax
from jax.experimental import pallas as pl
from jax.experimental.pallas import tpu as pltpu
from jax.sharding import PartitionSpec as P
import numpy as np

HEADS = 14
KV_HEADS = 2
HEAD_DIM = 64
MICRO = 2
SEQ = 128
D = 896
DP = 1024
QKV = 1152
norm_epsilon = 1e-06
rope_base = 1000000.0

MESH = pl.DeviceIdType.MESH
BF = jnp.bfloat16
F32 = jnp.float32


class Peer:
    def __init__(self, id, link):
        self.id, self.link = id, link


class Place:
    def __init__(self):
        f = lax.axis_index("fsdp")
        self.s = lax.axis_index("section")
        self.c = lax.rem(f, 2)
        self.z = lax.rem(f // 2, 4)
        self.y = lax.rem(f // 8, 2)
        self.x = f // 16

    def at(self, s=None, x=None, y=None, z=None, c=None):
        s = self.s if s is None else s
        x = self.x if x is None else x
        y = self.y if y is None else y
        z = self.z if z is None else z
        c = self.c if c is None else c
        return (s, ((x * 2 + y) * 4 + z) * 2 + c)

    def step(self, axis, k):
        here = self.x if axis == "x" else self.z
        return lax.rem(here + (k + 4), 4)

    def to(self, axis, k):
        return Peer(self.at(**{axis: self.step(axis, k)}), (axis, k))

    def across(self):
        return Peer(self.at(y=1 - self.y), "y")

    def mate(self):
        return Peer(self.at(c=1 - self.c), "mate")

    def beyond(self):
        return Peer(self.at(s=1 - self.s, y=1 - self.y), "section")


def greet(place):
    barrier = pltpu.get_barrier_semaphore()
    near = (
        place.to("x", 1), place.to("x", -1), place.to("z", 1), place.to("z", -1),
        place.across(), place.mate(), place.beyond(),
    )
    for peer in near:
        pl.semaphore_signal(barrier, inc=1, device_id=peer.id, device_id_type=MESH)
    pl.semaphore_wait(barrier, len(near))


RATE = {"mate": 150e3}
LINK_RATE = 48e3
LATENCY = 1.5


class Wire:
    def __init__(self, send_sems, recv_sems):
        self.send_sems, self.recv_sems = send_sems, recv_sems
        self.count, self.started, self.flows = 0, [], []
        self.now, self.free = 0.0, {}

    def send(self, src, dst, peer):
        k = self.count
        self.count += 1
        assert k < self.send_sems.shape[0]
        copy = pltpu.make_async_remote_copy(
            src_ref=src, dst_ref=dst, send_sem=self.send_sems.at[k],
            recv_sem=self.recv_sems.at[k], device_id=peer.id, device_id_type=MESH,
        )
        copy.start()
        self.started.append(copy)
        size = 2 * math.prod(dst.shape)
        begin = max(self.now, self.free.get(peer.link, 0.0))
        self.free[peer.link] = begin + size / RATE.get(peer.link, LINK_RATE)
        copy.there = self.free[peer.link] + LATENCY
        return copy

    def drain(self):
        for copy in self.started:
            copy.wait_send()
        self.started = []

    def add(self, flow):
        self.flows.append([None, flow])
        self.go_on(self.flows[-1])

    def go_on(self, entry):
        try:
            entry[0] = next(entry[1])
        except StopIteration:
            self.flows.remove(entry)

    def run(self):
        while self.flows:
            times = [(entry[0](), k) for k, entry in enumerate(self.flows)]
            when, k = min((t, k) for t, k in times if t is not None)
            self.now = max(self.now, when)
            self.go_on(self.flows[k])

    def busy(self, us):
        self.now += us


def got(*copies):
    yield lambda: max(copy.there for copy in copies)
    for copy in copies:
        copy.wait_recv()


def until(condition):
    yield lambda: 0.0 if condition() else None


def ring(wire, place, axis, piece, spawn):
    me = place.x if axis == "x" else place.z
    before, after, far = place.step(axis, -1), place.step(axis, 1), place.step(axis, 2)
    r = wire.send(piece(me), piece(me), place.to(axis, 1))
    l = wire.send(piece(me), piece(me), place.to(axis, -1))
    last = []

    def right():
        yield from got(r)
        last.append(wire.send(piece(before, 0), piece(before, 0), place.to(axis, 1)))
        spawn(before)

    def left():
        yield from got(l)
        last.append(wire.send(piece(after, 1), piece(after, 1), place.to(axis, -1)))
        spawn(after)

    def rest():
        yield from until(lambda: len(last) == 2)
        yield from got(*last)
        spawn(far)

    for flow in (right(), left(), rest()):
        wire.add(flow)


def gather_yab(wire, place, slot, first, last, finished):
    x, y, z = place.x, place.y, place.z
    cross = wire.send(slot(x, y, z), slot(x, y, z), place.across())
    yield from got(cross)
    mine = {"x": x, "z": z}
    count = []

    def piece(a, b, half=None):
        return slot(b, half, a) if first == "z" else slot(a, half, b)

    def arrived(b):
        count.append(b)
        if len(count) == 16:
            finished()

    def along_last(a):
        arrived(a)
        ring(wire, place, last, lambda b, half=None: piece(a, b, half), arrived)

    ring(wire, place, first, lambda a, half=None: piece(a, mine[last], half), along_last)
    along_last(mine[first])


def gather_down(wire, place, D, finished):
    x, y, z = place.x, place.y, place.z
    count = []

    def by_x(a, half=None):
        if half is None:
            return D.at[a, y, z]
        return D.at[a, y, z, pl.ds(0, 48) if half == 0 else pl.ds(48, 32)]

    def by_z(b, half=None):
        if half is None:
            return D.at[:, y, b]
        return D.at[pl.ds(2 * half, 2), y, b]

    def along_y(b):
        cross = wire.send(by_z(b), by_z(b), place.across())

        def arrival():
            yield from got(cross)
            count.append(b)
            if len(count) == 4:
                finished()

        wire.add(arrival())

    def x_done(a):
        seen.append(a)
        if len(seen) == 3:
            ring(wire, place, "z", by_z, along_y)
            along_y(z)

    seen = []
    ring(wire, place, "x", by_x, x_done)


BLOCK = dict(G=(32, 2560), U=(32, 2560), D=(80, 896), Q=(32, 1152), O=(32, 896))


def start_gather(wire, place, ins, bufs, local_sems, done):
    x, y, z, c = place.x, place.y, place.z, place.c
    rows = pl.ds(pl.multiple_of(c * 16, 16), 16)
    G, U, D, Q, O = bufs
    g_in, u_in, d_in, q_in, o_in = ins
    own = {}
    for k, (name, src, dst) in enumerate((
        ("Q", q_in, Q.at[x, y, z, rows]), ("O", o_in, O.at[x, y, z, rows]), ("D", d_in, D.at[x, y, z]),
        ("G", g_in.at[c], G.at[x, y, z, rows]), ("U", u_in.at[c], U.at[x, y, z, rows]),
    )):
        own[name] = pltpu.make_async_copy(src, dst, local_sems.at[k])
        own[name].start()
    swap_g = wire.send(g_in.at[1 - c], G.at[x, y, z, rows], place.mate())
    swap_u = wire.send(u_in.at[1 - c], U.at[x, y, z, rows], place.mate())

    def whole(buf):
        def slot(px, half, pz):
            if half is None:
                return buf.at[px, :, pz]
            return buf.at[px, half, pz]
        return slot

    def part(buf):
        def slot(px, half, pz):
            if half is None:
                return buf.at[px, :, pz, rows]
            return buf.at[px, half, pz, rows]
        return slot

    def attention(name, buf):
        own[name].wait()
        filled = []
        yield from gather_yab(wire, place, part(buf), "z", "x", lambda: filled.append(1))
        yield from until(lambda: filled)
        mine = buf.at[:, :, :, rows]
        swap = wire.send(mine, mine, place.mate())
        yield from got(swap)
        done.add(name)

    def hidden(name, buf, swap, first, last):
        yield from got(swap)
        own[name].wait()
        yield from gather_yab(wire, place, whole(buf), first, last, lambda: done.add(name))

    wire.add(attention("Q", Q))
    wire.add(attention("O", O))
    own["D"].wait()
    gather_down(wire, place, D, lambda: done.add("D"))
    wire.add(hidden("G", G, swap_g, "z", "x"))
    wire.add(hidden("U", U, swap_u, "x", "z"))


def bufs_shapes():
    return [(4, 2, 4) + BLOCK[k] for k in "GUDQO"]


def add(dst, *srcs):
    total = dst[...]
    for src in srcs:
        total = total + src[...]
    dst[...] = total


def add_each(count, dst, *srcs):
    def body(i, carry):
        add(dst(i), *[src(i) for src in srcs])
        return carry
    lax.fori_loop(0, count, body, 0)


def scatter_ring(wire, place, axis, piece, land, halves, finished):
    me = place.x if axis == "x" else place.z
    before, after, far = place.step(axis, -1), place.step(axis, 1), place.step(axis, 2)
    l1a, l1b, l2a, l2b = land
    r = wire.send(piece(far, 0), l1a, place.to(axis, 1))
    l = wire.send(piece(far, 1), l1b, place.to(axis, -1))
    last = []

    def right():
        yield from got(r)
        add(piece(after, 0), l1a)
        last.append(wire.send(piece(after), l2a, place.to(axis, 1)))

    def left():
        yield from got(l)
        add(piece(before, 1), l1b)
        last.append(wire.send(piece(before), l2b, place.to(axis, -1)))

    def rest():
        yield from until(lambda: len(last) == 2)
        yield from got(*last)
        halves(lambda i: piece(me, i), l2a, l2b)
        finished()

    for flow in (right(), left(), rest()):
        wire.add(flow)


def two_halves(dst, a, b):
    for i in range(2):
        add(dst(i), a.at[i], b.at[i])


def scatter_aby(wire, place, slot, R, first, last):
    r1a, r1b, r2a, r2b, s1a, s1b, s2a, s2b, t_buf = R
    mine = {"x": place.x, "z": place.z}

    def piece(a, b, half=None):
        return slot(b, half, a) if first == "z" else slot(a, half, b)

    order = [place.step(last, k) for k in (2, 1, -1)] + [mine[last]]
    filled = []
    for k, b in enumerate(order):
        scatter_ring(
            wire, place, first, lambda a, half=None, b=b: piece(a, b, half),
            (r1a.at[k], r1b.at[k], r2a.at[k], r2b.at[k]), two_halves, lambda k=k: filled.append(k),
        )
    a0 = mine[first]
    bq, bp, bm, b0 = order
    sent = []

    def outer():
        yield from until(lambda: 0 in filled)
        d_r = wire.send(piece(a0, bq, 0), s1a, place.to(last, 1))
        d_l = wire.send(piece(a0, bq, 1), s1b, place.to(last, -1))

        def right():
            yield from until(lambda: 1 in filled)
            yield from got(d_r)
            add(piece(a0, bp, 0), s1a)
            sent.append(wire.send(piece(a0, bp), s2a, place.to(last, 1)))

        def left():
            yield from until(lambda: 2 in filled)
            yield from got(d_l)
            add(piece(a0, bm, 1), s1b)
            sent.append(wire.send(piece(a0, bm), s2b, place.to(last, -1)))

        wire.add(right())
        wire.add(left())

    wire.add(outer())
    yield from until(lambda: len(sent) == 2 and 3 in filled)
    yield from got(*sent)
    two_halves(lambda i: piece(a0, b0, i), s2a, s2b)
    cross = wire.send(slot(place.x, 1 - place.y, place.z), t_buf, place.across())
    yield from got(cross)
    add(slot(place.x, place.y, place.z), t_buf)


def scatter_down(wire, place, D, R):
    yb, z1a, z1b, z2a, z2b, xa, xb, x2a, x2b = R
    x, y, z = place.x, place.y, place.z
    zp, zm, zq = place.step("z", 1), place.step("z", -1), place.step("z", 2)
    order = (zq, zp, zm, z)
    crossing = [wire.send(D.at[:, 1 - y, b], yb.at[k], place.across()) for k, b in enumerate(order)]
    sent = []

    def settle(k):
        yield from got(crossing[k])
        add_each(4, lambda i: D.at[i, y, order[k]], lambda i: yb.at[k, i])

    yield from settle(0)
    d_r = wire.send(D.at[pl.ds(0, 2), y, zq], z1a, place.to("z", 1))
    d_l = wire.send(D.at[pl.ds(2, 2), y, zq], z1b, place.to("z", -1))

    def right():
        yield from settle(1)
        yield from got(d_r)
        add_each(2, lambda i: D.at[i, y, zp], lambda i: z1a.at[i])
        sent.append(wire.send(D.at[:, y, zp], z2a, place.to("z", 1)))

    def left():
        yield from settle(2)
        yield from got(d_l)
        add_each(2, lambda i: D.at[i + 2, y, zm], lambda i: z1b.at[i])
        sent.append(wire.send(D.at[:, y, zm], z2b, place.to("z", -1)))

    wire.add(right())
    wire.add(left())
    yield from settle(3)
    yield from until(lambda: len(sent) == 2)
    yield from got(*sent)
    add_each(4, lambda i: D.at[i, y, z], lambda i: z2a.at[i], lambda i: z2b.at[i])

    def by_x(a, half=None):
        if half is None:
            return D.at[a, y, z]
        return D.at[a, y, z, pl.ds(0, 48) if half == 0 else pl.ds(48, 32)]

    ended = []
    scatter_ring(
        wire, place, "x", by_x, (xa, xb, x2a, x2b),
        lambda dst, a, b: add(D.at[x, y, z], a, b), lambda: ended.append(1),
    )
    yield from until(lambda: ended)


def rs_scratch():
    def aby(rows, cols):
        shapes = [(4, rows, cols)] * 2 + [(4, 2, rows, cols)] * 2 + [(rows, cols)] * 2 + [(2, rows, cols)] * 2 + [(rows, cols)]
        return [pltpu.VMEM(s, BF) for s in shapes]
    out = []
    out += aby(32, 2560) + [pltpu.VMEM((16, 2560), BF)]
    out += aby(32, 2560) + [pltpu.VMEM((16, 2560), BF)]
    b = (80, 896)
    out += [pltpu.VMEM(s, BF) for s in (
        (4, 4) + b, (2,) + b, (2,) + b, (4,) + b, (4,) + b, (48, 896), (32, 896), b, b)]
    out += aby(16, 1152) + [pltpu.VMEM((4, 2, 4, 16, 1152), BF)]
    out += aby(16, 896) + [pltpu.VMEM((4, 2, 4, 16, 896), BF)]
    return out


N_RS_SCRATCH = 10 + 10 + 9 + 10 + 10


def start_scatter(wire, place, bufs, R, made, end):
    x, y, z, c = place.x, place.y, place.z, place.c
    G, U, D, Q, O = bufs
    rg, ru, rd, rq, ro = R[:10], R[10:20], R[20:29], R[29:39], R[39:49]
    rows = pl.ds(pl.multiple_of(c * 16, 16), 16)
    others = pl.ds(pl.multiple_of(16 - c * 16, 16), 16)

    def whole(buf):
        def slot(px, half, pz):
            return buf.at[px, :, pz] if half is None else buf.at[px, half, pz]
        return slot

    def part(buf):
        def slot(px, half, pz):
            return buf.at[px, :, pz, rows] if half is None else buf.at[px, half, pz, rows]
        return slot

    def hidden(name, buf, r, first, last):
        yield from until(lambda: name in made)
        yield from scatter_aby(wire, place, whole(buf), r[:9], first, last)
        swap = wire.send(buf.at[x, y, z, others], r[9], place.mate())
        yield from got(swap)
        end(name, c, buf[x, y, z, rows], r[9][...])

    def attention(name, buf, r):
        yield from until(lambda: name in made)
        swap = wire.send(buf.at[:, :, :, others], r[9], place.mate())
        yield from got(swap)
        add_each(32, lambda i: buf.at[i // 8, lax.rem(i // 4, 2), lax.rem(i, 4), rows],
                 lambda i: r[9].at[i // 8, lax.rem(i // 4, 2), lax.rem(i, 4)])
        yield from scatter_aby(wire, place, part(buf), r[:9], "x", "z")
        end(name, c, buf[x, y, z, rows])

    def down():
        yield from until(lambda: "D" in made)
        yield from scatter_down(wire, place, D, rd)
        end("D", c, D[x, y, z])

    wire.add(down())
    wire.add(hidden("G", G, rg, "x", "z"))
    wire.add(hidden("U", U, ru, "z", "x"))
    wire.add(attention("O", O, ro))
    wire.add(attention("Q", Q, rq))


TOK = 256
FF = 2560


def mm(a, b):
    return jnp.dot(a, b, preferred_element_type=F32)


def mm_t(a, b):
    return lax.dot_general(a, b, (((1,), (1,)), ((), ())), preferred_element_type=F32)


def t_mm(a, b):
    return lax.dot_general(a, b, (((0,), (0,)), ((), ())), preferred_element_type=F32)


def constants():
    d = np.arange(D)
    spread = np.zeros((D, DP), np.float32)
    spread[d, 16 * (d // 14) + d % 14] = 1
    pick = np.zeros((64, DP), np.float32)
    pick[np.arange(64), 16 * np.arange(64) + 14] = 1
    own14 = (np.arange(64)[:, None] == d[None] // 14).astype(np.float32)
    j = np.arange(QKV)
    own18 = (np.arange(64)[:, None] == j[None] // 18).astype(np.float32)
    lane = np.arange(128)[:, None]
    e1 = (lane == d[None] % 14).astype(np.float32)
    eb = (lane == 64 + j[None] % 18).astype(np.float32)
    return [jnp.asarray(a, BF) for a in (spread, pick, own14, own18, e1, eb)]


CONST = ("spread", "pick", "own14", "own18", "e1", "eb")


def cols(buf, start, size):
    value = buf[:, :, :, :, pl.ds(start, size)]
    return value.reshape(-1, size)


def put(ref, value):
    ref[...] = value.reshape(ref.shape)


def rotate(x, lo32):
    return jnp.where(lo32, pltpu.roll(x, 96, 1), pltpu.roll(x, 32, 1))


def lane_is(shape, width, below):
    lane = lax.broadcasted_iota(jnp.int32, shape, 1)
    return lax.rem(lane, width) < below


def gains(R):
    q = cols(R.Q, 0, 128)
    s = mm(R.pick[...], q)
    s2 = pltpu.roll(s, 96, 1).astype(BF)
    s = s.astype(BF)
    R.g1[...] = jnp.sum(mm(s, R.e1[...]) * R.own14[...].astype(F32), axis=0, keepdims=True)
    R.g2[...] = jnp.sum(mm(s2, R.e1[...]) * R.own14[...].astype(F32), axis=0, keepdims=True)
    R.bias[...] = jnp.sum(mm(s, R.eb[...]) * R.own18[...].astype(F32), axis=0, keepdims=True)


def inverse_rms(h):
    return lax.rsqrt(jnp.sum(h * h, axis=-1, keepdims=True) * (1.0 / D) + norm_epsilon)


def project_qkv(R, source, tables, rows, size):
    h = source[rows].astype(F32)
    n1 = (h * inverse_rms(h) * R.g1[...]).astype(BF)
    R.N1[rows] = mm(n1, R.spread[...]).astype(BF)
    lo32 = lane_is((size, 128), 64, 32)
    lo = lane_is((size, 128), 128, 64)
    cos, sin = tables[0][rows], tables[1][rows]
    for start, width in ((0, 256), (256, 256), (512, 256), (768, 256), (1024, 128)):
        out = mm(R.N1[rows], cols(R.Q, start, width)) + R.bias[:, start:start + width]
        for k in range(width // 128):
            x = out[:, 128 * k:128 * k + 128]
            tile = (start + 128 * k) // 128
            if tile < 8:
                x = x * cos + rotate(x, lo32) * sin
            if tile < 7:
                R.QR[rows, 128 * tile:128 * tile + 128] = x.astype(BF)
            else:
                x = x.astype(BF).astype(F32)
                swapped = pltpu.roll(x, 64, 1)
                R.KV[tile - 7, 0, rows] = jnp.where(lo, x, swapped).astype(BF)
                R.KV[tile - 7, 1, rows] = x.astype(BF)
                R.KV[tile - 7, 2, rows] = jnp.where(lo, swapped, x).astype(BF)


def two_heads(R, tile):
    return jnp.concatenate([tile * R.lanes[0], tile * R.lanes[1]], axis=0)


def beside(x):
    return jnp.concatenate([x[:SEQ], x[SEQ:]], axis=1)


def variant_of(t):
    return 0 if t < 3 else (2 if t > 3 else 1)


def probs_of(R, mask, t, rows):
    q2 = two_heads(R, R.QR[rows, 128 * t:128 * t + 128])
    kk = R.KV[0, variant_of(t), rows]
    s = mm_t(q2, kk) * 0.125 + jnp.concatenate([mask, mask], axis=0)
    e = jnp.exp(s - jnp.max(s, axis=-1, keepdims=True))
    p = e * (1.0 / jnp.sum(e, axis=-1, keepdims=True))
    return q2, kk, p


def attend(R, tables, m):
    rows = own_rows(m)
    mask = tables[2][m]
    for t in range(7):
        _, _, p = probs_of(R, mask, t, rows)
        vv = two_heads(R, R.KV[1, variant_of(t), rows])
        R.DQKV[rows, 128 * t:128 * t + 128] = mm(beside(p.astype(BF)), vv).astype(BF)


def own_rows(m):
    return pl.ds(SEQ * m, SEQ)


def pair_own(m):
    return pl.ds(2 * SEQ * m, SEQ)


def pair_other(m):
    return pl.ds(2 * SEQ * m + SEQ, SEQ)


def pair(m):
    return pl.ds(2 * SEQ * m, 2 * SEQ)


def after_attention(R, source, m):
    rows = own_rows(m)
    R.CP[rows] = mm(R.DQKV[rows, :D], R.spread[...]).astype(BF)
    mid = source[rows].astype(F32) + mm(R.CP[rows], cols(R.O, 0, D))
    R.MID[rows] = mid
    n2 = (mid * inverse_rms(mid) * R.g2[...]).astype(BF)
    R.N2[pair_own(m)] = mm(n2, R.spread[...]).astype(BF)


def sigmoid(v):
    return 0.5 * jnp.tanh(0.5 * v) + 0.5


def hidden(R, m):
    rows = pair(m)

    def body(j, carry):
        at = pl.ds(pl.multiple_of(j * 256, 256), 256)
        n2 = R.N2[rows]
        gate = mm(n2, R.G[:, :, :, :, at].reshape(DP, 256))
        up = mm(n2, R.U[:, :, :, :, at].reshape(DP, 256))
        R.GA[rows, at] = gate.astype(BF)
        R.UP[rows, at] = up.astype(BF)
        R.ACT[rows, at] = (gate * sigmoid(gate) * up).astype(BF)
        return carry

    lax.fori_loop(0, FF // 256, body, 0)


class Swap:
    def __init__(self, R, place):
        own = own_rows
        mate, across, beyond = place.mate(), place.across(), place.beyond()

        def table(k, refs, device):
            return lambda m: pltpu.make_async_remote_copy(
                src_ref=refs(m)[0], dst_ref=refs(m)[1], send_sem=R.xs.at[2 * k + m],
                recv_sem=R.xr.at[2 * k + m], device_id=device.id, device_id_type=MESH,
            )

        self.n2 = table(0, lambda m: (R.N2.at[pair_own(m)], R.N2.at[pair_other(m)]), mate)
        self.part = table(1, lambda m: (R.DB.at[own(m)], R.DC.at[own(m)]), mate)
        self.dy = table(2, lambda m: (R.DY.at[pair_own(m)], R.DY.at[pair_other(m)]), mate)
        self.dn = table(3, lambda m: (R.dn, R.dn_in.at[own(m)]), mate)
        self.hop_h = table(4, lambda m: (R.ys.at[own(m)], R.h.at[own(m)]), beyond)
        self.hop_dy = table(5, lambda m: (R.dhs.at[own(m)], R.DY.at[pair_own(m)]), beyond)
        self.og = table(6, lambda m: (R.og.at[own(m)], R.DY.at[pair_own(m)]), across)
        self.cos = table(7, lambda m: (R.cos.at[own(m)], R.tcos.at[own(m)]), across)
        self.sin = table(8, lambda m: (R.sin.at[own(m)], R.tsin.at[own(m)]), across)
        self.mask = table(9, lambda m: (R.mask.at[m], R.tmask.at[m]), across)
        self.y = table(10, lambda m: (R.ys.at[own(m)], R.y.at[own(m)]), across)
        self.dh = table(11, lambda m: (R.dhs.at[own(m)], R.dh.at[own(m)]), across)


N_SWAP = 24


def down_sent(R, swap, m):
    R.DB[own_rows(m)] = mm(R.ACT[pair_other(m)], R.D[...].reshape(FF, D)).astype(BF)
    swap.part(m).start()
    R.acc[SEQ:, 0:D] = R.MID[own_rows(m)] + mm(R.ACT[pair_own(m)], R.D[...].reshape(FF, D))


def down_done(R, swap, m):
    swap.part(m).wait_recv()
    R.ys[own_rows(m)] = (R.acc[SEQ:, 0:D] + R.DC[own_rows(m)].astype(F32)).astype(BF)
    swap.part(m).wait_send()


def hidden_back(R, m):
    rows = pair(m)

    def body(j, carry):
        down = R.D[j].reshape(640, D)
        for start, size in ((0, 256), (256, 256), (512, 128)):
            sub = pl.ds(pl.multiple_of(j * 640 + start, 128), size)
            dact = mm_t(R.DY[rows], down[start:start + size])
            gate = R.GA[rows, sub].astype(F32)
            up = R.UP[rows, sub].astype(F32)
            sig = sigmoid(gate)
            R.GA[rows, sub] = (dact * up * sig * (1.0 + gate * (1.0 - sig))).astype(BF)
            R.UP[rows, sub] = (dact * gate * sig).astype(BF)
        return carry

    lax.fori_loop(0, FF // 640, body, 0)


def normed_back(R, swap, m):
    rows = pair(m)
    R.acc[...] = jnp.zeros_like(R.acc)

    def body(j, carry):
        at = pl.ds(pl.multiple_of(j * 512, 512), 512)
        R.acc[...] += mm_t(R.GA[rows, at], R.G[:, :, :, :, at].reshape(DP, 512)) + mm_t(
            R.UP[rows, at], R.U[:, :, :, :, at].reshape(DP, 512)
        )
        return carry

    lax.fori_loop(0, FF // 512, body, 0)
    R.dn[...] = R.acc[SEQ:].astype(BF)
    swap.dn(m).start()


def middle_back(R, swap, m):
    rows = own_rows(m)
    swap.dn(m).wait_recv()
    dn2p = (R.acc[:SEQ] + R.dn_in[rows].astype(F32)).astype(BF)
    dn2 = mm_t(dn2p, R.spread[...])
    mid = R.MID[rows]
    inv2 = inverse_rms(mid)
    R.dg2[m] = jnp.sum(dn2 * mid * inv2, axis=0, keepdims=True)
    scaled = dn2 * R.g2[...]
    mean = jnp.sum(scaled * mid, axis=-1, keepdims=True) * (1.0 / D)
    dmid = R.DY[pair_own(m)].astype(F32) + inv2 * scaled - mid * (inv2 * inv2 * inv2 * mean)
    R.MID[rows] = dmid
    R.DB[rows] = dmid.astype(BF)
    dctx = mm_t(R.DB[rows], cols(R.O, 0, D)).astype(BF)
    R.DC[rows] = mm_t(dctx, R.spread[...]).astype(BF)
    swap.dn(m).wait_send()


def attend_back(R, tables, m):
    rows = own_rows(m)
    cos, sin, mask = tables[0][rows], tables[1][rows], tables[2][m]
    lo32 = lane_is((SEQ, 128), 64, 32)
    lo = lane_is((SEQ, 128), 128, 64)

    def spin_back(g):
        return g * cos + rotate(g * sin, lo32)

    for t in range(7):
        q2, kk, p = probs_of(R, mask, t, rows)
        var = variant_of(t)
        dc2 = two_heads(R, R.DC[rows, 128 * t:128 * t + 128])
        dp = mm_t(dc2, R.KV[1, var, rows])
        ds = (p * (dp - jnp.sum(p * dp, axis=-1, keepdims=True))).astype(BF)
        dk, dv = t_mm(ds, q2), t_mm(p.astype(BF), dc2)
        if t in (0, 3, 4):
            R.dkv[0, var] = dk
            R.dkv[1, var] = dv
        else:
            R.dkv[0, var] += dk
            R.dkv[1, var] += dv
        dq = mm(beside(ds), two_heads(R, kk)) * 0.125
        R.DQKV[rows, 128 * t:128 * t + 128] = spin_back(dq).astype(BF)

    def joined(k):
        first, mixed, last = R.dkv[k, 0], R.dkv[k, 1], R.dkv[k, 2]
        return mixed + jnp.where(
            lo, first + pltpu.roll(first, 64, 1), last + pltpu.roll(last, 64, 1)
        )

    R.DQKV[rows, 896:1024] = spin_back(joined(0) * 0.125).astype(BF)
    R.DQKV[rows, 1024:1152] = joined(1).astype(BF)


def stream_back(R, m):
    rows = own_rows(m)
    dqkv = R.DQKV[rows]
    R.dbias[m] = jnp.sum(dqkv.astype(F32), axis=0, keepdims=True)
    dn1 = mm_t(mm_t(dqkv, cols(R.Q, 0, QKV)).astype(BF), R.spread[...])
    h = R.h[rows].astype(F32)
    inv1 = inverse_rms(h)
    R.dg1[m] = jnp.sum(dn1 * h * inv1, axis=0, keepdims=True)
    scaled = dn1 * R.g1[...]
    mean = jnp.sum(scaled * h, axis=-1, keepdims=True) * (1.0 / D)
    R.dhs[rows] = (R.MID[rows] + inv1 * scaled - h * (inv1 * inv1 * inv1 * mean)).astype(BF)


def pause(wire):
    now = wire.now
    yield lambda: now


def weight_grads(R, wire, done, rest):
    def down(x, carry):
        at = pl.ds(pl.multiple_of(x * 640, 640), 640)
        for start, size in ((0, 512), (512, 384)):
            grad = t_mm(R.ACT[:, at], R.DY[:, start:start + size])
            put(R.D.at[x, :, :, :, pl.ds(start, size)], grad.astype(BF))
        return carry

    lax.fori_loop(0, 4, down, 0)
    done.add("D")
    wire.busy(3.0)
    yield from pause(wire)
    rest[0]()
    wire.busy(4.0)
    for name, buf, grad in (("G", R.G, R.GA), ("U", R.U, R.UP)):
        def tile(x, carry):
            n2 = R.N2[:, pl.ds(pl.multiple_of(x * 256, 256), 256)]
            for start in range(0, FF, 512):
                at = pl.ds(start, 512)
                put(buf.at[x, :, :, :, at], t_mm(n2, grad[:, at]).astype(BF))
            return carry

        yield from pause(wire)
        lax.fori_loop(0, 4, tile, 0)
        done.add(name)
        wire.busy(4.5)
    for piece in rest[1:]:
        yield from pause(wire)
        piece()
        wire.busy(3.0)
    yield from pause(wire)

    def out_rows(x, carry):
        rows = pl.ds(pl.multiple_of(x * 256, 256), 256)
        put(R.O.at[x], t_mm(R.CP[:, rows], R.DB[...]).astype(BF))
        return carry

    lax.fori_loop(0, 4, out_rows, 0)
    done.add("O")
    wire.busy(1.5)
    yield from pause(wire)
    small = (
        mm_t((R.own14[...].astype(F32) * (R.dg1[0] + R.dg1[1])).astype(BF), R.e1[...])
        + pltpu.roll(
            mm_t((R.own14[...].astype(F32) * (R.dg2[0] + R.dg2[1])).astype(BF), R.e1[...]), 32, 1
        )
        + mm_t((R.own18[...].astype(F32) * (R.dbias[0] + R.dbias[1])).astype(BF), R.eb[...])
    )
    R.small[...] = small.astype(BF)

    def qkv_rows(x, carry):
        rows = pl.ds(pl.multiple_of(x * 256, 256), 256)
        n1 = R.N1[:, rows]
        for start in range(0, QKV, 384):
            g = t_mm(n1, R.DQKV[:, start:start + 384])
            if start == 0:
                g = jnp.concatenate([g[:, :128] + t_mm(R.pick[:, rows], R.small[...]), g[:, 128:]], axis=1)
            put(R.Q.at[x, :, :, :, pl.ds(start, 384)], g.astype(BF))
        return carry

    lax.fori_loop(0, 4, qkv_rows, 0)
    done.add("Q")


def pack(R):
    for src, wide, dst in ((R.g_in, R.g_s, R.g_st), (R.u_in, R.g_s, R.u_st)):
        wide[...] = jnp.zeros_like(wide)
        for f in range(64):
            piece = src[:, 76 * f:76 * f + 76].astype(F32)
            wide[f % 2, 0:14, 80 * (f // 2):80 * (f // 2) + 76] = piece
        dst[...] = wide[...].astype(BF)
    R.acc[0:80, 0:D] = jnp.zeros((80, D), F32)
    R.acc[0:76, 0:D] = R.d_in[...].astype(F32)
    R.d_st[...] = R.acc[0:80, 0:D].astype(BF)
    R.o_s[...] = jnp.zeros_like(R.o_s)
    R.o_s[0:14] = R.o_in[...].astype(F32)
    R.o_st[...] = R.o_s[...].astype(BF)
    R.q_s[...] = jnp.zeros_like(R.q_s)
    R.q_s[0:14] = R.q_in[...].astype(F32)
    R.q_s[14:15, 0:14] = R.a_in[...].astype(F32)
    R.q_s[14:15, 32:46] = R.c_in[...].astype(F32)
    R.q_s[14:15, 64:82] = R.b_in[...].astype(F32)
    R.q_st[...] = R.q_s[...].astype(BF)


def unpack(R, name, c, mine, other=None):
    if name in "GU":
        R.g_s[c] = mine.astype(F32)
        R.g_s[1 - c] = other.astype(F32)
        dst = R.g_o if name == "G" else R.u_o
        for f in range(64):
            at = 80 * (f // 2)
            dst[:, 76 * f:76 * f + 76] = R.g_s[f % 2, 0:14, at:at + 76]
    elif name == "D":
        R.acc[0:80, 0:D] = mine.astype(F32)
        R.d_o[...] = R.acc[0:76, 0:D]
    elif name == "O":
        R.o_s[...] = mine.astype(F32)
        R.o_o[...] = R.o_s[0:14]
    else:
        R.q_s[...] = mine.astype(F32)
        R.q_o[...] = R.q_s[0:14]
        R.a_o[...] = R.q_s[14:15, 0:14]
        R.c_o[...] = R.q_s[14:15, 32:46]
        R.b_o[...] = R.q_s[14:15, 64:82]


INS = ("g_in", "u_in", "d_in", "q_in", "o_in", "a_in", "b_in", "c_in", "tokens", "og", "cos", "sin", "mask") + CONST
IN_HBM = ("og", "tokens", "cos", "sin", "mask")
OUTS = ("y", "dh", "g_o", "u_o", "d_o", "q_o", "o_o", "a_o", "b_o", "c_o")
LOCAL = (
    ("h", (TOK, D), BF), ("N1", (TOK, DP), BF), ("QR", (TOK, D), BF),
    ("KV", (2, 3, TOK, 128), BF), ("CP", (TOK, DP), BF),
    ("MID", (TOK, D), F32), ("N2", (2 * TOK, DP), BF), ("GA", (2 * TOK, FF), BF),
    ("UP", (2 * TOK, FF), BF), ("ACT", (2 * TOK, FF), BF), ("DY", (2 * TOK, D), BF), ("acc", (TOK, DP), F32), ("dn", (SEQ, DP), BF), ("dn_in", (TOK, DP), BF),
    ("DB", (TOK, D), BF), ("DC", (TOK, D), BF), ("DQKV", (TOK, QKV), BF),
    ("dkv", (2, 3, SEQ, 128), F32), ("lanes", (2, SEQ, 128), BF),
    ("small", (64, 128), BF),
    ("g1", (1, D), F32), ("g2", (1, D), F32), ("bias", (1, QKV), F32),
    ("dg1", (2, 1, D), F32), ("dg2", (2, 1, D), F32), ("dbias", (2, 1, QKV), F32),
    ("g_st", (2, 16, FF), BF), ("u_st", (2, 16, FF), BF), ("d_st", (80, D), BF),
    ("q_st", (16, QKV), BF), ("o_st", (16, D), BF), ("g_s", (2, 16, FF), F32),
    ("q_s", (16, QKV), F32), ("o_s", (16, D), F32),
    ("ys", (TOK, D), BF), ("dhs", (TOK, D), BF),
    ("tcos", (TOK, 128), F32), ("tsin", (TOK, 128), F32), ("tmask", (2, SEQ, SEQ), F32),
)


def layers_kernel(*refs):
    names = INS + OUTS + tuple("GUDQO") + tuple(name for name, _, _ in LOCAL)
    R = SimpleNamespace(**dict(zip(names, refs)))
    rest = refs[len(names):]
    R.ss, R.rs, R.ls, R.xs, R.xr = rest[N_RS_SCRATCH:]
    place = Place()
    greet(place)
    wire = Wire(R.ss, R.rs)
    swap = Swap(R, place)
    bufs = (R.G, R.U, R.D, R.Q, R.O)
    done = set()
    tables = (R.tcos, R.tsin, R.tmask)

    def only(section):
        return lambda body: pl.when(place.s == section)(body)

    @only(0)
    def _():
        moves = [
            pltpu.make_async_copy(src, dst, R.ls.at[5 + k])
            for k, (src, dst) in enumerate(zip((R.tokens, R.cos, R.sin, R.mask), (R.h,) + tables))
        ]
        for move in moves:
            move.start()
        for move in moves:
            move.wait()

    @only(1)
    def _():
        for m in range(MICRO):
            for move in (swap.og, swap.cos, swap.sin, swap.mask):
                move(m).start()

    def early():
        yield from until(lambda: {"Q", "O"} <= done)
        gains(R)
        only(0)(lambda: project_qkv(R, R.h, tables, pl.ds(0, TOK), TOK))
        wire.busy(2.5)
        for m in range(MICRO):
            yield from pause(wire)
            only(0)(lambda: attend(R, tables, m))
            wire.busy(2.5)
            yield from pause(wire)

            @only(0)
            def _():
                after_attention(R, R.h, m)
                swap.n2(m).start()

            wire.busy(1.5)

    pack(R)
    start_gather(wire, place, (R.g_st, R.u_st, R.d_st, R.q_st, R.o_st), bufs, R.ls, done)
    lo = lane_is((SEQ, 128), 128, 64).astype(F32)
    R.lanes[0] = lo.astype(BF)
    R.lanes[1] = (1.0 - lo).astype(BF)
    wire.add(early())
    wire.run()

    @only(0)
    def _():
        for m in range(MICRO):
            swap.n2(m).wait_recv()
            hidden(R, m)
            down_sent(R, swap, m)
            down_done(R, swap, m)
            swap.hop_h(m).start()
        R.y[...] = R.ys[...]
        swap.hop_dy(0).wait_recv()
        swap.dy(0).start()
        swap.dy(0).wait_recv()
        hidden_back(R, 0)
        normed_back(R, swap, 0)
        middle_back(R, swap, 0)
        attend_back(R, tables, 0)
        stream_back(R, 0)
        swap.hop_dy(1).wait_recv()
        swap.dy(1).start()
        swap.dy(1).wait_recv()
        hidden_back(R, 1)

    @only(1)
    def _():
        def start(m):
            swap.hop_h(m).wait_recv()
            rows = own_rows(m)
            project_qkv(R, R.h, tables, rows, SEQ)
            attend(R, tables, m)
            after_attention(R, R.h, m)
            swap.n2(m).start()

        def feed(m):
            swap.n2(m).wait_recv()
            hidden(R, m)
            down_sent(R, swap, m)
            down_done(R, swap, m)
            swap.y(m).start()

        def finish(m):
            middle_back(R, swap, m)
            attend_back(R, tables, m)
            stream_back(R, m)
            swap.hop_dy(m).start()
            swap.dh(m).start()

        for m in range(MICRO):
            for move in (swap.og, swap.cos, swap.sin, swap.mask):
                move(m).wait_recv()
            swap.dy(m).start()
        start(0)
        feed(0)
        start(1)
        swap.dy(0).wait_recv()
        hidden_back(R, 0)
        normed_back(R, swap, 0)
        feed(1)
        finish(0)
        swap.dy(1).wait_recv()
        hidden_back(R, 1)
        normed_back(R, swap, 1)
        finish(1)

    wire.drain()

    def rest_a():
        only(0)(lambda: normed_back(R, swap, 1))

    def rest_b():
        only(0)(lambda: middle_back(R, swap, 1))

    def rest_c():
        only(0)(lambda: attend_back(R, tables, 1))

    def rest_d():
        @only(0)
        def _():
            stream_back(R, 1)
            R.dh[...] = R.dhs[...]

    made = set()
    start_scatter(wire, place, bufs, rest[:N_RS_SCRATCH], made, lambda *a: unpack(R, *a))
    wire.add(weight_grads(R, wire, made, (rest_a, rest_b, rest_c, rest_d)))
    wire.run()
    wire.drain()
    for m in range(MICRO):
        swap.n2(m).wait_send()
        swap.dy(m).wait_send()

    @only(0)
    def _():
        for m in range(MICRO):
            swap.hop_h(m).wait_send()

    @only(1)
    def _():
        for m in range(MICRO):
            for move in (swap.og, swap.cos, swap.sin, swap.mask, swap.y, swap.dh, swap.hop_dy):
                move(m).wait_send()
            swap.y(m).wait_recv()
            swap.dh(m).wait_recv()


N_WIRE = 208


def run_layers(ins):
    outs = [(TOK, D)] * 2 + [(14, 4864)] * 2 + [(76, D), (14, QKV), (14, D), (1, 14), (1, 18), (1, 14)]
    kinds = [BF, BF] + [F32] * 8
    vmem = pl.BlockSpec(memory_space=pltpu.VMEM)
    dma = pltpu.SemaphoreType.DMA
    return pl.pallas_call(
        layers_kernel,
        out_shape=[jax.ShapeDtypeStruct(s, k) for s, k in zip(outs, kinds)],
        in_specs=[pl.BlockSpec(memory_space=pl.ANY) if n in IN_HBM else vmem for n in INS],
        out_specs=[vmem] * len(OUTS),
        scratch_shapes=[pltpu.VMEM(s, BF) for s in bufs_shapes()]
        + [pltpu.VMEM(s, k) for _, s, k in LOCAL]
        + rs_scratch()
        + [dma((N_WIRE,)), dma((N_WIRE,)), dma((9,)), dma((N_SWAP,)), dma((N_SWAP,))],
        compiler_params=pltpu.CompilerParams(
            collective_id=0, has_side_effects=True, vmem_limit_bytes=127 * 2**19
        ),
        name="two_layers",
    )(*ins)


def rope_tables(segment_row, head_size):
    length = segment_row.shape[0]
    places = jnp.arange(length, dtype=jnp.int32)
    changes = jnp.concatenate(
        [jnp.ones((1,), jnp.int32), (segment_row[1:] != segment_row[:-1]).astype(jnp.int32)]
    )
    starts = lax.cummax(places * changes, axis=0)
    offsets = (places - starts).astype(F32)
    ladder = jnp.arange(head_size // 2, dtype=F32) * (-2.0 * math.log(rope_base) / head_size)
    angles = offsets[:, None] * jnp.exp(ladder)[None, :]
    cos, sin = jnp.cos(angles), jnp.sin(angles)
    return (
        jnp.concatenate([cos, cos, cos, cos], axis=-1),
        jnp.concatenate([-sin, sin, -sin, sin], axis=-1),
    )


def mask_of(segment_row):
    places = jnp.arange(segment_row.shape[0], dtype=jnp.int32)
    seen = (segment_row[:, None] == segment_row[None, :]) & (places[None, :] <= places[:, None])
    return jnp.where(seen, 0.0, -1e30).astype(F32)


def shards(
    tokens_in, out_grad, segments, norm1_gain, qkv_weight, qkv_bias, out_weight, norm2_gain,
    gate_weight, up_weight, down_weight,
):
    half = MICRO * SEQ
    rows = segments[:, 0]
    cos, sin = jax.vmap(rope_tables, in_axes=(0, None))(rows, HEAD_DIM)
    y, dh, g, u, d, q, o, a, b, c = run_layers([
        gate_weight[0],
        up_weight[0],
        down_weight[0],
        qkv_weight[0],
        out_weight[0],
        norm1_gain,
        qkv_bias,
        norm2_gain,
        tokens_in.reshape(half, D),
        out_grad.reshape(half, D),
        cos.reshape(half, 128),
        sin.reshape(half, 128),
        jax.vmap(mask_of)(rows),
        *constants(),
    ])
    shape = (1, MICRO, 1, SEQ, D)
    return (
        y.reshape(shape), dh.reshape(shape), a, q[None], b, o[None], c, g[None], u[None], d[None]
    )


def solution(mesh):
    in_specs = (
        P(None, "fsdp", None, None),
        P(None, "fsdp", None, None),
        P(None, "fsdp", None),
        P("section", "fsdp"),
        P("section", "fsdp", None),
        P("section", "fsdp"),
        P("section", "fsdp", None),
        P("section", "fsdp"),
        P("section", "fsdp", None),
        P("section", "fsdp", None),
        P("section", "fsdp", None),
    )
    out_specs = (
        P("section", None, "fsdp", None, None),
        P("section", None, "fsdp", None, None),
        P("section", "fsdp"),
        P("section", "fsdp", None),
        P("section", "fsdp"),
        P("section", "fsdp", None),
        P("section", "fsdp"),
        P("section", "fsdp", None),
        P("section", "fsdp", None),
        P("section", "fsdp", None),
    )
    return jax.shard_map(shards, mesh=mesh, in_specs=in_specs, out_specs=out_specs, check_vma=False)
```

```python
import math
from types import SimpleNamespace

import jax
import jax.numpy as jnp
from jax import lax
from jax.experimental import pallas as pl
from jax.experimental.pallas import tpu as pltpu
from jax.sharding import PartitionSpec as P
import numpy as np

HEADS = 14
KV_HEADS = 2
HEAD_DIM = 64
MICRO = 2
SEQ = 128
D = 896
DP = 1024
QKV = 1152
norm_epsilon = 1e-06
rope_base = 1000000.0

MESH = pl.DeviceIdType.MESH
BF = jnp.bfloat16
F32 = jnp.float32


class Peer:
    def __init__(self, id, link):
        self.id, self.link = id, link


class Place:
    def __init__(self):
        f = lax.axis_index("fsdp")
        self.s = lax.axis_index("section")
        self.c = lax.rem(f, 2)
        self.z = lax.rem(f // 2, 4)
        self.y = lax.rem(f // 8, 2)
        self.x = f // 16

    def at(self, s=None, x=None, y=None, z=None, c=None):
        s = self.s if s is None else s
        x = self.x if x is None else x
        y = self.y if y is None else y
        z = self.z if z is None else z
        c = self.c if c is None else c
        return (s, ((x * 2 + y) * 4 + z) * 2 + c)

    def step(self, axis, k):
        here = self.x if axis == "x" else self.z
        return lax.rem(here + (k + 4), 4)

    def to(self, axis, k):
        return Peer(self.at(**{axis: self.step(axis, k)}), (axis, k))

    def across(self):
        return Peer(self.at(y=1 - self.y), "y")

    def mate(self):
        return Peer(self.at(c=1 - self.c), "mate")

    def beyond(self):
        return Peer(self.at(s=1 - self.s, y=1 - self.y), "section")


def greet(place):
    barrier = pltpu.get_barrier_semaphore()
    near = (
        place.to("x", 1), place.to("x", -1), place.to("z", 1), place.to("z", -1),
        place.across(), place.mate(), place.beyond(),
    )
    for peer in near:
        pl.semaphore_signal(barrier, inc=1, device_id=peer.id, device_id_type=MESH)
    pl.semaphore_wait(barrier, len(near))


RATE = {"mate": 150e3}
LINK_RATE = 48e3
LATENCY = 1.5


class Wire:
    def __init__(self, send_sems, recv_sems):
        self.send_sems, self.recv_sems = send_sems, recv_sems
        self.count, self.started, self.flows = 0, [], []
        self.now, self.free = 0.0, {}

    def send(self, src, dst, peer):
        k = self.count
        self.count += 1
        assert k < self.send_sems.shape[0]
        copy = pltpu.make_async_remote_copy(
            src_ref=src, dst_ref=dst, send_sem=self.send_sems.at[k],
            recv_sem=self.recv_sems.at[k], device_id=peer.id, device_id_type=MESH,
        )
        copy.start()
        self.started.append(copy)
        size = 2 * math.prod(dst.shape)
        begin = max(self.now, self.free.get(peer.link, 0.0))
        self.free[peer.link] = begin + size / RATE.get(peer.link, LINK_RATE)
        copy.there = self.free[peer.link] + LATENCY
        return copy

    def drain(self):
        for copy in self.started:
            copy.wait_send()
        self.started = []

    def add(self, flow):
        self.flows.append([None, flow])
        self.go_on(self.flows[-1])

    def go_on(self, entry):
        try:
            entry[0] = next(entry[1])
        except StopIteration:
            self.flows.remove(entry)

    def run(self):
        while self.flows:
            times = [(entry[0](), k) for k, entry in enumerate(self.flows)]
            when, k = min((t, k) for t, k in times if t is not None)
            self.now = max(self.now, when)
            self.go_on(self.flows[k])

    def busy(self, us):
        self.now += us


def got(*copies):
    yield lambda: max(copy.there for copy in copies)
    for copy in copies:
        copy.wait_recv()


def until(condition):
    yield lambda: 0.0 if condition() else None


def ring(wire, place, axis, piece, spawn):
    me = place.x if axis == "x" else place.z
    before, after, far = place.step(axis, -1), place.step(axis, 1), place.step(axis, 2)
    r = wire.send(piece(me), piece(me), place.to(axis, 1))
    l = wire.send(piece(me), piece(me), place.to(axis, -1))
    last = []

    def right():
        yield from got(r)
        last.append(wire.send(piece(before, 0), piece(before, 0), place.to(axis, 1)))
        spawn(before)

    def left():
        yield from got(l)
        last.append(wire.send(piece(after, 1), piece(after, 1), place.to(axis, -1)))
        spawn(after)

    def rest():
        yield from until(lambda: len(last) == 2)
        yield from got(*last)
        spawn(far)

    for flow in (right(), left(), rest()):
        wire.add(flow)


def gather_yab(wire, place, slot, first, last, finished):
    x, y, z = place.x, place.y, place.z
    cross = wire.send(slot(x, y, z), slot(x, y, z), place.across())
    yield from got(cross)
    mine = {"x": x, "z": z}
    count = []

    def piece(a, b, half=None):
        return slot(b, half, a) if first == "z" else slot(a, half, b)

    def arrived(b):
        count.append(b)
        if len(count) == 16:
            finished()

    def along_last(a):
        arrived(a)
        ring(wire, place, last, lambda b, half=None: piece(a, b, half), arrived)

    ring(wire, place, first, lambda a, half=None: piece(a, mine[last], half), along_last)
    along_last(mine[first])


def gather_down(wire, place, D, finished):
    x, y, z = place.x, place.y, place.z
    count = []

    def by_x(a, half=None):
        if half is None:
            return D.at[a, y, z]
        return D.at[a, y, z, pl.ds(0, 48) if half == 0 else pl.ds(48, 32)]

    def by_z(b, half=None):
        if half is None:
            return D.at[:, y, b]
        return D.at[pl.ds(2 * half, 2), y, b]

    def along_y(b):
        cross = wire.send(by_z(b), by_z(b), place.across())

        def arrival():
            yield from got(cross)
            count.append(b)
            if len(count) == 4:
                finished()

        wire.add(arrival())

    def x_done(a):
        seen.append(a)
        if len(seen) == 3:
            ring(wire, place, "z", by_z, along_y)
            along_y(z)

    seen = []
    ring(wire, place, "x", by_x, x_done)


BLOCK = dict(G=(32, 2560), U=(32, 2560), D=(80, 896), Q=(32, 1152), O=(32, 896))


def start_gather(wire, place, ins, bufs, local_sems, done):
    x, y, z, c = place.x, place.y, place.z, place.c
    rows = pl.ds(pl.multiple_of(c * 16, 16), 16)
    G, U, D, Q, O = bufs
    g_in, u_in, d_in, q_in, o_in = ins
    own = {}
    for k, (name, src, dst) in enumerate((
        ("Q", q_in, Q.at[x, y, z, rows]), ("O", o_in, O.at[x, y, z, rows]), ("D", d_in, D.at[x, y, z]),
        ("G", g_in.at[c], G.at[x, y, z, rows]), ("U", u_in.at[c], U.at[x, y, z, rows]),
    )):
        own[name] = pltpu.make_async_copy(src, dst, local_sems.at[k])
        own[name].start()
    swap_g = wire.send(g_in.at[1 - c], G.at[x, y, z, rows], place.mate())
    swap_u = wire.send(u_in.at[1 - c], U.at[x, y, z, rows], place.mate())

    def whole(buf):
        def slot(px, half, pz):
            if half is None:
                return buf.at[px, :, pz]
            return buf.at[px, half, pz]
        return slot

    def part(buf):
        def slot(px, half, pz):
            if half is None:
                return buf.at[px, :, pz, rows]
            return buf.at[px, half, pz, rows]
        return slot

    def attention(name, buf):
        own[name].wait()
        filled = []
        yield from gather_yab(wire, place, part(buf), "z", "x", lambda: filled.append(1))
        yield from until(lambda: filled)
        mine = buf.at[:, :, :, rows]
        swap = wire.send(mine, mine, place.mate())
        yield from got(swap)
        done.add(name)

    def hidden(name, buf, swap, first, last):
        yield from got(swap)
        own[name].wait()
        yield from gather_yab(wire, place, whole(buf), first, last, lambda: done.add(name))

    wire.add(attention("Q", Q))
    wire.add(attention("O", O))
    own["D"].wait()
    gather_down(wire, place, D, lambda: done.add("D"))
    wire.add(hidden("G", G, swap_g, "z", "x"))
    wire.add(hidden("U", U, swap_u, "x", "z"))


def bufs_shapes():
    return [(4, 2, 4) + BLOCK[k] for k in "GUDQO"]


def add(dst, *srcs):
    total = dst[...]
    for src in srcs:
        total = total + src[...]
    dst[...] = total


def add_each(count, dst, *srcs):
    def body(i, carry):
        add(dst(i), *[src(i) for src in srcs])
        return carry
    lax.fori_loop(0, count, body, 0)


def scatter_ring(wire, place, axis, piece, land, halves, finished):
    me = place.x if axis == "x" else place.z
    before, after, far = place.step(axis, -1), place.step(axis, 1), place.step(axis, 2)
    l1a, l1b, l2a, l2b = land
    r = wire.send(piece(far, 0), l1a, place.to(axis, 1))
    l = wire.send(piece(far, 1), l1b, place.to(axis, -1))
    last = []

    def right():
        yield from got(r)
        add(piece(after, 0), l1a)
        last.append(wire.send(piece(after), l2a, place.to(axis, 1)))

    def left():
        yield from got(l)
        add(piece(before, 1), l1b)
        last.append(wire.send(piece(before), l2b, place.to(axis, -1)))

    def rest():
        yield from until(lambda: len(last) == 2)
        yield from got(*last)
        halves(lambda i: piece(me, i), l2a, l2b)
        finished()

    for flow in (right(), left(), rest()):
        wire.add(flow)


def two_halves(dst, a, b):
    for i in range(2):
        add(dst(i), a.at[i], b.at[i])


def scatter_aby(wire, place, slot, R, first, last):
    r1a, r1b, r2a, r2b, s1a, s1b, s2a, s2b, t_buf = R
    mine = {"x": place.x, "z": place.z}

    def piece(a, b, half=None):
        return slot(b, half, a) if first == "z" else slot(a, half, b)

    order = [place.step(last, k) for k in (2, 1, -1)] + [mine[last]]
    filled = []
    for k, b in enumerate(order):
        scatter_ring(
            wire, place, first, lambda a, half=None, b=b: piece(a, b, half),
            (r1a.at[k], r1b.at[k], r2a.at[k], r2b.at[k]), two_halves, lambda k=k: filled.append(k),
        )
    a0 = mine[first]
    bq, bp, bm, b0 = order
    sent = []

    def outer():
        yield from until(lambda: 0 in filled)
        d_r = wire.send(piece(a0, bq, 0), s1a, place.to(last, 1))
        d_l = wire.send(piece(a0, bq, 1), s1b, place.to(last, -1))

        def right():
            yield from until(lambda: 1 in filled)
            yield from got(d_r)
            add(piece(a0, bp, 0), s1a)
            sent.append(wire.send(piece(a0, bp), s2a, place.to(last, 1)))

        def left():
            yield from until(lambda: 2 in filled)
            yield from got(d_l)
            add(piece(a0, bm, 1), s1b)
            sent.append(wire.send(piece(a0, bm), s2b, place.to(last, -1)))

        wire.add(right())
        wire.add(left())

    wire.add(outer())
    yield from until(lambda: len(sent) == 2 and 3 in filled)
    yield from got(*sent)
    two_halves(lambda i: piece(a0, b0, i), s2a, s2b)
    cross = wire.send(slot(place.x, 1 - place.y, place.z), t_buf, place.across())
    yield from got(cross)
    add(slot(place.x, place.y, place.z), t_buf)


def scatter_down(wire, place, D, R):
    yb, z1a, z1b, z2a, z2b, xa, xb, x2a, x2b = R
    x, y, z = place.x, place.y, place.z
    zp, zm, zq = place.step("z", 1), place.step("z", -1), place.step("z", 2)
    order = (zq, zp, zm, z)
    crossing = [wire.send(D.at[:, 1 - y, b], yb.at[k], place.across()) for k, b in enumerate(order)]
    sent = []

    def settle(k):
        yield from got(crossing[k])
        add_each(4, lambda i: D.at[i, y, order[k]], lambda i: yb.at[k, i])

    yield from settle(0)
    d_r = wire.send(D.at[pl.ds(0, 2), y, zq], z1a, place.to("z", 1))
    d_l = wire.send(D.at[pl.ds(2, 2), y, zq], z1b, place.to("z", -1))

    def right():
        yield from settle(1)
        yield from got(d_r)
        add_each(2, lambda i: D.at[i, y, zp], lambda i: z1a.at[i])
        sent.append(wire.send(D.at[:, y, zp], z2a, place.to("z", 1)))

    def left():
        yield from settle(2)
        yield from got(d_l)
        add_each(2, lambda i: D.at[i + 2, y, zm], lambda i: z1b.at[i])
        sent.append(wire.send(D.at[:, y, zm], z2b, place.to("z", -1)))

    wire.add(right())
    wire.add(left())
    yield from settle(3)
    yield from until(lambda: len(sent) == 2)
    yield from got(*sent)
    add_each(4, lambda i: D.at[i, y, z], lambda i: z2a.at[i], lambda i: z2b.at[i])

    def by_x(a, half=None):
        if half is None:
            return D.at[a, y, z]
        return D.at[a, y, z, pl.ds(0, 48) if half == 0 else pl.ds(48, 32)]

    ended = []
    scatter_ring(
        wire, place, "x", by_x, (xa, xb, x2a, x2b),
        lambda dst, a, b: add(D.at[x, y, z], a, b), lambda: ended.append(1),
    )
    yield from until(lambda: ended)


def rs_scratch():
    def aby(rows, cols):
        shapes = [(4, rows, cols)] * 2 + [(4, 2, rows, cols)] * 2 + [(rows, cols)] * 2 + [(2, rows, cols)] * 2 + [(rows, cols)]
        return [pltpu.VMEM(s, BF) for s in shapes]
    out = []
    out += aby(32, 2560) + [pltpu.VMEM((16, 2560), BF)]
    out += aby(32, 2560) + [pltpu.VMEM((16, 2560), BF)]
    b = (80, 896)
    out += [pltpu.VMEM(s, BF) for s in (
        (4, 4) + b, (2,) + b, (2,) + b, (4,) + b, (4,) + b, (48, 896), (32, 896), b, b)]
    out += aby(16, 1152) + [pltpu.VMEM((4, 2, 4, 16, 1152), BF)]
    out += aby(16, 896) + [pltpu.VMEM((4, 2, 4, 16, 896), BF)]
    return out


N_RS_SCRATCH = 10 + 10 + 9 + 10 + 10


def start_scatter(wire, place, bufs, R, made, end):
    x, y, z, c = place.x, place.y, place.z, place.c
    G, U, D, Q, O = bufs
    rg, ru, rd, rq, ro = R[:10], R[10:20], R[20:29], R[29:39], R[39:49]
    rows = pl.ds(pl.multiple_of(c * 16, 16), 16)
    others = pl.ds(pl.multiple_of(16 - c * 16, 16), 16)

    def whole(buf):
        def slot(px, half, pz):
            return buf.at[px, :, pz] if half is None else buf.at[px, half, pz]
        return slot

    def part(buf):
        def slot(px, half, pz):
            return buf.at[px, :, pz, rows] if half is None else buf.at[px, half, pz, rows]
        return slot

    def hidden(name, buf, r, first, last):
        yield from until(lambda: name in made)
        yield from scatter_aby(wire, place, whole(buf), r[:9], first, last)
        swap = wire.send(buf.at[x, y, z, others], r[9], place.mate())
        yield from got(swap)
        end(name, c, buf[x, y, z, rows], r[9][...])

    def attention(name, buf, r):
        yield from until(lambda: name in made)
        swap = wire.send(buf.at[:, :, :, others], r[9], place.mate())
        yield from got(swap)
        add_each(32, lambda i: buf.at[i // 8, lax.rem(i // 4, 2), lax.rem(i, 4), rows],
                 lambda i: r[9].at[i // 8, lax.rem(i // 4, 2), lax.rem(i, 4)])
        yield from scatter_aby(wire, place, part(buf), r[:9], "x", "z")
        end(name, c, buf[x, y, z, rows])

    def down():
        yield from until(lambda: "D" in made)
        yield from scatter_down(wire, place, D, rd)
        end("D", c, D[x, y, z])

    wire.add(down())
    wire.add(hidden("G", G, rg, "x", "z"))
    wire.add(hidden("U", U, ru, "z", "x"))
    wire.add(attention("O", O, ro))
    wire.add(attention("Q", Q, rq))


TOK = 256
FF = 2560


def mm(a, b):
    return jnp.dot(a, b, preferred_element_type=F32)


def mm_t(a, b):
    return lax.dot_general(a, b, (((1,), (1,)), ((), ())), preferred_element_type=F32)


def t_mm(a, b):
    return lax.dot_general(a, b, (((0,), (0,)), ((), ())), preferred_element_type=F32)


def constants():
    d = np.arange(D)
    spread = np.zeros((D, DP), np.float32)
    spread[d, 16 * (d // 14) + d % 14] = 1
    pick = np.zeros((64, DP), np.float32)
    pick[np.arange(64), 16 * np.arange(64) + 14] = 1
    own14 = (np.arange(64)[:, None] == d[None] // 14).astype(np.float32)
    j = np.arange(QKV)
    own18 = (np.arange(64)[:, None] == j[None] // 18).astype(np.float32)
    lane = np.arange(128)[:, None]
    e1 = (lane == d[None] % 14).astype(np.float32)
    eb = (lane == 64 + j[None] % 18).astype(np.float32)
    return [jnp.asarray(a, BF) for a in (spread, pick, own14, own18, e1, eb)]


CONST = ("spread", "pick", "own14", "own18", "e1", "eb")


def cols(buf, start, size):
    value = buf[:, :, :, :, pl.ds(start, size)]
    return value.reshape(-1, size)


def put(ref, value):
    ref[...] = value.reshape(ref.shape)


def rotate(x, lo32):
    return jnp.where(lo32, pltpu.roll(x, 96, 1), pltpu.roll(x, 32, 1))


def lane_is(shape, width, below):
    lane = lax.broadcasted_iota(jnp.int32, shape, 1)
    return lax.rem(lane, width) < below


def gains(R):
    q = cols(R.Q, 0, 128)
    s = mm(R.pick[...], q)
    s2 = pltpu.roll(s, 96, 1).astype(BF)
    s = s.astype(BF)
    R.g1[...] = jnp.sum(mm(s, R.e1[...]) * R.own14[...].astype(F32), axis=0, keepdims=True)
    R.g2[...] = jnp.sum(mm(s2, R.e1[...]) * R.own14[...].astype(F32), axis=0, keepdims=True)
    R.bias[...] = jnp.sum(mm(s, R.eb[...]) * R.own18[...].astype(F32), axis=0, keepdims=True)


def inverse_rms(h):
    return lax.rsqrt(jnp.sum(h * h, axis=-1, keepdims=True) * (1.0 / D) + norm_epsilon)


def project_qkv(R, source, tables, rows, size):
    h = source[rows].astype(F32)
    n1 = (h * inverse_rms(h) * R.g1[...]).astype(BF)
    R.N1[rows] = mm(n1, R.spread[...]).astype(BF)
    lo32 = lane_is((size, 128), 64, 32)
    lo = lane_is((size, 128), 128, 64)
    cos, sin = tables[0][rows], tables[1][rows]
    for start, width in ((0, 256), (256, 256), (512, 256), (768, 256), (1024, 128)):
        out = mm(R.N1[rows], cols(R.Q, start, width)) + R.bias[:, start:start + width]
        for k in range(width // 128):
            x = out[:, 128 * k:128 * k + 128]
            tile = (start + 128 * k) // 128
            if tile < 8:
                x = x * cos + rotate(x, lo32) * sin
            if tile < 7:
                R.QR[rows, 128 * tile:128 * tile + 128] = x.astype(BF)
            else:
                x = x.astype(BF).astype(F32)
                swapped = pltpu.roll(x, 64, 1)
                R.KV[tile - 7, 0, rows] = jnp.where(lo, x, swapped).astype(BF)
                R.KV[tile - 7, 1, rows] = x.astype(BF)
                R.KV[tile - 7, 2, rows] = jnp.where(lo, swapped, x).astype(BF)


def two_heads(R, tile):
    return jnp.concatenate([tile * R.lanes[0], tile * R.lanes[1]], axis=0)


def beside(x):
    return jnp.concatenate([x[:SEQ], x[SEQ:]], axis=1)


def variant_of(t):
    return 0 if t < 3 else (2 if t > 3 else 1)


def probs_of(R, mask, t, rows):
    q2 = two_heads(R, R.QR[rows, 128 * t:128 * t + 128])
    kk = R.KV[0, variant_of(t), rows]
    s = mm_t(q2, kk) * 0.125 + jnp.concatenate([mask, mask], axis=0)
    e = jnp.exp(s - jnp.max(s, axis=-1, keepdims=True))
    p = e * (1.0 / jnp.sum(e, axis=-1, keepdims=True))
    return q2, kk, p


def attend(R, tables, m):
    rows = own_rows(m)
    mask = tables[2][m]
    for t in range(7):
        _, _, p = probs_of(R, mask, t, rows)
        vv = two_heads(R, R.KV[1, variant_of(t), rows])
        R.DQKV[rows, 128 * t:128 * t + 128] = mm(beside(p.astype(BF)), vv).astype(BF)


def own_rows(m):
    return pl.ds(SEQ * m, SEQ)


def pair_own(m):
    return pl.ds(2 * SEQ * m, SEQ)


def pair_other(m):
    return pl.ds(2 * SEQ * m + SEQ, SEQ)


def pair(m):
    return pl.ds(2 * SEQ * m, 2 * SEQ)


def after_attention(R, source, m):
    rows = own_rows(m)
    R.CP[rows] = mm(R.DQKV[rows, :D], R.spread[...]).astype(BF)
    mid = source[rows].astype(F32) + mm(R.CP[rows], cols(R.O, 0, D))
    R.MID[rows] = mid
    n2 = (mid * inverse_rms(mid) * R.g2[...]).astype(BF)
    R.N2[pair_own(m)] = mm(n2, R.spread[...]).astype(BF)


def sigmoid(v):
    return 0.5 * jnp.tanh(0.5 * v) + 0.5


def hidden(R, rows):
    def body(j, carry):
        at = pl.ds(pl.multiple_of(j * 1280, 1280), 1280)
        n2 = R.N2[rows]
        gate = mm(n2, R.G[:, :, :, :, at].reshape(DP, 1280))
        up = mm(n2, R.U[:, :, :, :, at].reshape(DP, 1280))
        R.GA[rows, at] = gate.astype(BF)
        R.UP[rows, at] = up.astype(BF)
        R.ACT[rows, at] = (gate * sigmoid(gate) * up).astype(BF)
        return carry

    lax.fori_loop(0, FF // 1280, body, 0)


def hidden_other(R, swap, m):
    swap.n2(m).wait_recv()
    hidden(R, pair_other(m))


class Swap:
    def __init__(self, R, place):
        own = own_rows
        mate, across, beyond = place.mate(), place.across(), place.beyond()

        def table(k, refs, device):
            return lambda m: pltpu.make_async_remote_copy(
                src_ref=refs(m)[0], dst_ref=refs(m)[1], send_sem=R.xs.at[2 * k + m],
                recv_sem=R.xr.at[2 * k + m], device_id=device.id, device_id_type=MESH,
            )

        self.n2 = table(0, lambda m: (R.N2.at[pair_own(m)], R.N2.at[pair_other(m)]), mate)
        self.part = table(1, lambda m: (R.DB.at[own(m)], R.DC.at[own(m)]), mate)
        self.dy = table(2, lambda m: (R.DY.at[pair_own(m)], R.DY.at[pair_other(m)]), mate)
        self.dn = table(3, lambda m: (R.dn, R.dn_in.at[own(m)]), mate)
        self.hop_h = table(4, lambda m: (R.ys.at[own(m)], R.h.at[own(m)]), beyond)
        self.hop_dy = table(5, lambda m: (R.dhs.at[own(m)], R.DY.at[pair_own(m)]), beyond)
        self.og = table(6, lambda m: (R.og.at[own(m)], R.DY.at[pair_own(m)]), across)
        self.cos = table(7, lambda m: (R.cos.at[own(m)], R.tcos.at[own(m)]), across)
        self.sin = table(8, lambda m: (R.sin.at[own(m)], R.tsin.at[own(m)]), across)
        self.mask = table(9, lambda m: (R.mask.at[m], R.tmask.at[m]), across)
        self.y = table(10, lambda m: (R.ys.at[own(m)], R.y.at[own(m)]), across)
        self.dh = table(11, lambda m: (R.dhs.at[own(m)], R.dh.at[own(m)]), across)


N_SWAP = 24


def down_sent(R, swap, m):
    R.DB[own_rows(m)] = mm(R.ACT[pair_other(m)], R.D[...].reshape(FF, D)).astype(BF)
    swap.part(m).start()
    R.acc[SEQ:, 0:D] = R.MID[own_rows(m)] + mm(R.ACT[pair_own(m)], R.D[...].reshape(FF, D))


def down_done(R, swap, m):
    swap.part(m).wait_recv()
    R.ys[own_rows(m)] = (R.acc[SEQ:, 0:D] + R.DC[own_rows(m)].astype(F32)).astype(BF)
    swap.part(m).wait_send()


def hidden_back(R, m):
    rows = pair(m)

    def body(j, carry):
        down = R.D[j].reshape(640, D)
        for start, size in ((0, 256), (256, 256), (512, 128)):
            sub = pl.ds(pl.multiple_of(j * 640 + start, 128), size)
            dact = mm_t(R.DY[rows], down[start:start + size])
            gate = R.GA[rows, sub].astype(F32)
            up = R.UP[rows, sub].astype(F32)
            sig = sigmoid(gate)
            R.GA[rows, sub] = (dact * up * sig * (1.0 + gate * (1.0 - sig))).astype(BF)
            R.UP[rows, sub] = (dact * gate * sig).astype(BF)
        return carry

    lax.fori_loop(0, FF // 640, body, 0)


def normed_back(R, swap, m):
    rows = pair(m)

    def body(x, carry):
        at = pl.ds(pl.multiple_of(x * 256, 256), 256)
        R.acc[:, at] = mm_t(R.GA[rows], R.G[x].reshape(256, FF)) + mm_t(R.UP[rows], R.U[x].reshape(256, FF))
        return carry

    lax.fori_loop(0, 4, body, 0)
    R.dn[...] = R.acc[SEQ:].astype(BF)
    swap.dn(m).start()


def middle_back(R, swap, m):
    rows = own_rows(m)
    swap.dn(m).wait_recv()
    dn2p = (R.acc[:SEQ] + R.dn_in[rows].astype(F32)).astype(BF)
    dn2 = mm_t(dn2p, R.spread[...])
    mid = R.MID[rows]
    inv2 = inverse_rms(mid)
    R.dg2[m] = jnp.sum(dn2 * mid * inv2, axis=0, keepdims=True)
    scaled = dn2 * R.g2[...]
    mean = jnp.sum(scaled * mid, axis=-1, keepdims=True) * (1.0 / D)
    dmid = R.DY[pair_own(m)].astype(F32) + inv2 * scaled - mid * (inv2 * inv2 * inv2 * mean)
    R.MID[rows] = dmid
    R.DB[rows] = dmid.astype(BF)
    dctx = mm_t(R.DB[rows], cols(R.O, 0, D)).astype(BF)
    R.DC[rows] = mm_t(dctx, R.spread[...]).astype(BF)
    swap.dn(m).wait_send()


def attend_back(R, tables, m):
    rows = own_rows(m)
    cos, sin, mask = tables[0][rows], tables[1][rows], tables[2][m]
    lo32 = lane_is((SEQ, 128), 64, 32)
    lo = lane_is((SEQ, 128), 128, 64)

    def spin_back(g):
        return g * cos + rotate(g * sin, lo32)

    for t in range(7):
        q2, kk, p = probs_of(R, mask, t, rows)
        var = variant_of(t)
        dc2 = two_heads(R, R.DC[rows, 128 * t:128 * t + 128])
        dp = mm_t(dc2, R.KV[1, var, rows])
        ds = (p * (dp - jnp.sum(p * dp, axis=-1, keepdims=True))).astype(BF)
        dk, dv = t_mm(ds, q2), t_mm(p.astype(BF), dc2)
        if t in (0, 3, 4):
            R.dkv[0, var] = dk
            R.dkv[1, var] = dv
        else:
            R.dkv[0, var] += dk
            R.dkv[1, var] += dv
        dq = mm(beside(ds), two_heads(R, kk)) * 0.125
        R.DQKV[rows, 128 * t:128 * t + 128] = spin_back(dq).astype(BF)

    def joined(k):
        first, mixed, last = R.dkv[k, 0], R.dkv[k, 1], R.dkv[k, 2]
        return mixed + jnp.where(
            lo, first + pltpu.roll(first, 64, 1), last + pltpu.roll(last, 64, 1)
        )

    R.DQKV[rows, 896:1024] = spin_back(joined(0) * 0.125).astype(BF)
    R.DQKV[rows, 1024:1152] = joined(1).astype(BF)


def stream_back(R, m):
    rows = own_rows(m)
    dqkv = R.DQKV[rows]
    R.dbias[m] = jnp.sum(dqkv.astype(F32), axis=0, keepdims=True)
    dn1 = mm_t(mm_t(dqkv, cols(R.Q, 0, QKV)).astype(BF), R.spread[...])
    h = R.h[rows].astype(F32)
    inv1 = inverse_rms(h)
    R.dg1[m] = jnp.sum(dn1 * h * inv1, axis=0, keepdims=True)
    scaled = dn1 * R.g1[...]
    mean = jnp.sum(scaled * h, axis=-1, keepdims=True) * (1.0 / D)
    R.dhs[rows] = (R.MID[rows] + inv1 * scaled - h * (inv1 * inv1 * inv1 * mean)).astype(BF)


def pause(wire):
    now = wire.now
    yield lambda: now


def weight_grads(R, wire, done, rest):
    def down(x, carry):
        at = pl.ds(pl.multiple_of(x * 640, 640), 640)
        for start, size in ((0, 512), (512, 384)):
            grad = t_mm(R.ACT[:, at], R.DY[:, start:start + size])
            put(R.D.at[x, :, :, :, pl.ds(start, size)], grad.astype(BF))
        return carry

    lax.fori_loop(0, 4, down, 0)
    done.add("D")
    wire.busy(3.0)
    yield from pause(wire)
    rest[0]()
    wire.busy(4.0)
    for name, buf, grad in (("G", R.G, R.GA), ("U", R.U, R.UP)):
        def tile(x, carry):
            n2 = R.N2[:, pl.ds(pl.multiple_of(x * 256, 256), 256)]
            for start in range(0, FF, 512):
                at = pl.ds(start, 512)
                put(buf.at[x, :, :, :, at], t_mm(n2, grad[:, at]).astype(BF))
            return carry

        yield from pause(wire)
        lax.fori_loop(0, 4, tile, 0)
        done.add(name)
        wire.busy(4.5)
    for piece in rest[1:]:
        yield from pause(wire)
        piece()
        wire.busy(3.0)
    yield from pause(wire)

    def out_rows(x, carry):
        rows = pl.ds(pl.multiple_of(x * 256, 256), 256)
        put(R.O.at[x], t_mm(R.CP[:, rows], R.DB[...]).astype(BF))
        return carry

    lax.fori_loop(0, 4, out_rows, 0)
    done.add("O")
    wire.busy(1.5)
    yield from pause(wire)
    small = (
        mm_t((R.own14[...].astype(F32) * (R.dg1[0] + R.dg1[1])).astype(BF), R.e1[...])
        + pltpu.roll(
            mm_t((R.own14[...].astype(F32) * (R.dg2[0] + R.dg2[1])).astype(BF), R.e1[...]), 32, 1
        )
        + mm_t((R.own18[...].astype(F32) * (R.dbias[0] + R.dbias[1])).astype(BF), R.eb[...])
    )
    R.small[...] = small.astype(BF)

    def qkv_rows(x, carry):
        rows = pl.ds(pl.multiple_of(x * 256, 256), 256)
        n1 = R.N1[:, rows]
        for start in range(0, QKV, 384):
            g = t_mm(n1, R.DQKV[:, start:start + 384])
            if start == 0:
                g = jnp.concatenate([g[:, :128] + t_mm(R.pick[:, rows], R.small[...]), g[:, 128:]], axis=1)
            put(R.Q.at[x, :, :, :, pl.ds(start, 384)], g.astype(BF))
        return carry

    lax.fori_loop(0, 4, qkv_rows, 0)
    done.add("Q")


def pack(R):
    for src, wide, dst in ((R.g_in, R.g_s, R.g_st), (R.u_in, R.g_s, R.u_st)):
        wide[...] = jnp.zeros_like(wide)
        for f in range(64):
            piece = src[:, 76 * f:76 * f + 76].astype(F32)
            wide[f % 2, 0:14, 80 * (f // 2):80 * (f // 2) + 76] = piece
        dst[...] = wide[...].astype(BF)
    R.acc[0:80, 0:D] = jnp.zeros((80, D), F32)
    R.acc[0:76, 0:D] = R.d_in[...].astype(F32)
    R.d_st[...] = R.acc[0:80, 0:D].astype(BF)
    R.o_s[...] = jnp.zeros_like(R.o_s)
    R.o_s[0:14] = R.o_in[...].astype(F32)
    R.o_st[...] = R.o_s[...].astype(BF)
    R.q_s[...] = jnp.zeros_like(R.q_s)
    R.q_s[0:14] = R.q_in[...].astype(F32)
    R.q_s[14:15, 0:14] = R.a_in[...].astype(F32)
    R.q_s[14:15, 32:46] = R.c_in[...].astype(F32)
    R.q_s[14:15, 64:82] = R.b_in[...].astype(F32)
    R.q_st[...] = R.q_s[...].astype(BF)


def keep(R, name, c, mine, other=None):
    dst = getattr(R, name.lower() + "_o")
    if other is None:
        dst[...] = mine
    else:
        dst[c] = mine
        dst[1 - c] = other


def finish_kernel(y, dh, g, u, d, q, o, y_o, dh_o, a_o, q_o, b_o, o_o, c_o, g_o, u_o, d_o, wide, flat):
    y_o[...] = y[...]
    dh_o[...] = dh[...]
    for src, dst in ((g, g_o), (u, u_o)):
        wide[...] = src[...].astype(F32)
        for f in range(64):
            at = 80 * (f // 2)
            flat[0:14, 76 * f:76 * f + 76] = wide[f % 2, 0:14, at:at + 76]
        for r in range(14):
            dst[r] = flat[r:r + 1, :]
    flat[0:80, 0:D] = d[...].astype(F32)
    for r in range(76):
        d_o[r] = flat[r:r + 1, 0:D]
    flat[0:16, 0:QKV] = q[...].astype(F32)
    for r in range(14):
        q_o[r] = flat[r:r + 1, 0:QKV]
    a_o[...] = flat[14:15, 0:14]
    c_o[...] = flat[14:15, 32:46]
    b_o[...] = flat[14:15, 64:82]
    flat[16:32, 0:D] = o[...].astype(F32)
    for r in range(14):
        o_o[r] = flat[16 + r:17 + r, 0:D]


def finish_grads(parts):
    shapes = [
        (TOK, D), (TOK, D), (1, 14), (14, 1, QKV), (1, 18), (14, 1, D), (1, 14),
        (14, 1, 4864), (14, 1, 4864), (76, 1, D),
    ]
    vmem = pl.BlockSpec(memory_space=pltpu.VMEM)
    return pl.pallas_call(
        finish_kernel,
        out_shape=[jax.ShapeDtypeStruct(s, BF if k < 2 else F32) for k, s in enumerate(shapes)],
        in_specs=[vmem] * len(parts),
        out_specs=[vmem] * len(shapes),
        scratch_shapes=[pltpu.VMEM((2, 16, FF), F32), pltpu.VMEM((80, 4864), F32)],
        compiler_params=pltpu.CompilerParams(vmem_limit_bytes=32 * 2**20),
        name="finish_grads",
    )(*parts)


INS = ("g_in", "u_in", "d_in", "q_in", "o_in", "a_in", "b_in", "c_in", "tokens", "og", "cos", "sin", "mask") + CONST
IN_HBM = ("og", "tokens", "cos", "sin", "mask")
OUTS = ("y", "dh", "g_o", "u_o", "d_o", "q_o", "o_o")
LOCAL = (
    ("h", (TOK, D), BF), ("N1", (TOK, DP), BF), ("QR", (TOK, D), BF),
    ("KV", (2, 3, TOK, 128), BF), ("CP", (TOK, DP), BF),
    ("MID", (TOK, D), F32), ("N2", (2 * TOK, DP), BF), ("GA", (2 * TOK, FF), BF),
    ("UP", (2 * TOK, FF), BF), ("ACT", (2 * TOK, FF), BF), ("DY", (2 * TOK, D), BF), ("acc", (TOK, DP), F32), ("dn", (SEQ, DP), BF), ("dn_in", (TOK, DP), BF),
    ("DB", (TOK, D), BF), ("DC", (TOK, D), BF), ("DQKV", (TOK, QKV), BF),
    ("dkv", (2, 3, SEQ, 128), F32), ("lanes", (2, SEQ, 128), BF),
    ("small", (64, 128), BF),
    ("g1", (1, D), F32), ("g2", (1, D), F32), ("bias", (1, QKV), F32),
    ("dg1", (2, 1, D), F32), ("dg2", (2, 1, D), F32), ("dbias", (2, 1, QKV), F32),
    ("g_st", (2, 16, FF), BF), ("u_st", (2, 16, FF), BF), ("d_st", (80, D), BF),
    ("q_st", (16, QKV), BF), ("o_st", (16, D), BF), ("g_s", (2, 16, FF), F32),
    ("q_s", (16, QKV), F32), ("o_s", (16, D), F32),
    ("ys", (TOK, D), BF), ("dhs", (TOK, D), BF),
    ("tcos", (TOK, 128), F32), ("tsin", (TOK, 128), F32), ("tmask", (2, SEQ, SEQ), F32),
)


def layers_kernel(*refs):
    names = INS + OUTS + tuple("GUDQO") + tuple(name for name, _, _ in LOCAL)
    R = SimpleNamespace(**dict(zip(names, refs)))
    rest = refs[len(names):]
    R.ss, R.rs, R.ls, R.xs, R.xr = rest[N_RS_SCRATCH:]
    place = Place()
    greet(place)
    wire = Wire(R.ss, R.rs)
    swap = Swap(R, place)
    bufs = (R.G, R.U, R.D, R.Q, R.O)
    done = set()
    tables = (R.tcos, R.tsin, R.tmask)

    def only(section):
        return lambda body: pl.when(place.s == section)(body)

    @only(0)
    def _():
        moves = [
            pltpu.make_async_copy(src, dst, R.ls.at[5 + k])
            for k, (src, dst) in enumerate(zip((R.tokens, R.cos, R.sin, R.mask), (R.h,) + tables))
        ]
        for move in moves:
            move.start()
        for move in moves:
            move.wait()

    @only(1)
    def _():
        for m in range(MICRO):
            for move in (swap.og, swap.cos, swap.sin, swap.mask):
                move(m).start()

    def early():
        yield from until(lambda: {"Q", "O"} <= done)
        gains(R)
        only(0)(lambda: project_qkv(R, R.h, tables, pl.ds(0, TOK), TOK))
        wire.busy(2.5)
        for m in range(MICRO):
            yield from pause(wire)
            only(0)(lambda: attend(R, tables, m))
            wire.busy(2.5)
            yield from pause(wire)

            @only(0)
            def _():
                after_attention(R, R.h, m)
                swap.n2(m).start()

            wire.busy(1.5)

    pack(R)
    start_gather(wire, place, (R.g_st, R.u_st, R.d_st, R.q_st, R.o_st), bufs, R.ls, done)
    lo = lane_is((SEQ, 128), 128, 64).astype(F32)
    R.lanes[0] = lo.astype(BF)
    R.lanes[1] = (1.0 - lo).astype(BF)
    wire.add(early())
    wire.run()

    @only(0)
    def _():
        hidden(R, pair_own(0))
        hidden_other(R, swap, 0)
        down_sent(R, swap, 0)
        hidden(R, pair_own(1))
        down_done(R, swap, 0)
        swap.hop_h(0).start()
        hidden_other(R, swap, 1)
        down_sent(R, swap, 1)
        down_done(R, swap, 1)
        swap.hop_h(1).start()
        R.y[...] = R.ys[...]
        swap.hop_dy(0).wait_recv()
        swap.dy(0).start()
        swap.dy(0).wait_recv()
        hidden_back(R, 0)
        normed_back(R, swap, 0)
        middle_back(R, swap, 0)
        attend_back(R, tables, 0)
        stream_back(R, 0)
        swap.hop_dy(1).wait_recv()
        swap.dy(1).start()
        swap.dy(1).wait_recv()
        hidden_back(R, 1)

    @only(1)
    def _():
        def start(m):
            swap.hop_h(m).wait_recv()
            rows = own_rows(m)
            project_qkv(R, R.h, tables, rows, SEQ)
            attend(R, tables, m)
            after_attention(R, R.h, m)
            swap.n2(m).start()

        def feed(m):
            hidden(R, pair_own(m))
            hidden_other(R, swap, m)
            down_sent(R, swap, m)

        def fed(m):
            down_done(R, swap, m)
            swap.y(m).start()

        def finish(m):
            middle_back(R, swap, m)
            attend_back(R, tables, m)
            stream_back(R, m)
            swap.hop_dy(m).start()
            swap.dh(m).start()

        for m in range(MICRO):
            for move in (swap.og, swap.cos, swap.sin, swap.mask):
                move(m).wait_recv()
            swap.dy(m).start()
        start(0)
        feed(0)
        start(1)
        fed(0)
        swap.dy(0).wait_recv()
        hidden_back(R, 0)
        normed_back(R, swap, 0)
        feed(1)
        finish(0)
        fed(1)
        swap.dy(1).wait_recv()
        hidden_back(R, 1)
        normed_back(R, swap, 1)
        finish(1)

    wire.drain()

    def rest_a():
        only(0)(lambda: normed_back(R, swap, 1))

    def rest_b():
        only(0)(lambda: middle_back(R, swap, 1))

    def rest_c():
        only(0)(lambda: attend_back(R, tables, 1))

    def rest_d():
        @only(0)
        def _():
            stream_back(R, 1)
            R.dh[...] = R.dhs[...]

    made = set()
    start_scatter(wire, place, bufs, rest[:N_RS_SCRATCH], made, lambda *a: keep(R, *a))
    wire.add(weight_grads(R, wire, made, (rest_a, rest_b, rest_c, rest_d)))
    wire.run()
    wire.drain()
    for m in range(MICRO):
        swap.n2(m).wait_send()
        swap.dy(m).wait_send()

    @only(0)
    def _():
        for m in range(MICRO):
            swap.hop_h(m).wait_send()

    @only(1)
    def _():
        for m in range(MICRO):
            for move in (swap.og, swap.cos, swap.sin, swap.mask, swap.y, swap.dh, swap.hop_dy):
                move(m).wait_send()
            swap.y(m).wait_recv()
            swap.dh(m).wait_recv()


N_WIRE = 208


def run_layers(ins):
    outs = [(TOK, D)] * 2 + [(2, 16, FF)] * 2 + [(80, D), (16, QKV), (16, D)]
    kinds = [BF] * 7
    vmem = pl.BlockSpec(memory_space=pltpu.VMEM)
    dma = pltpu.SemaphoreType.DMA
    return pl.pallas_call(
        layers_kernel,
        out_shape=[jax.ShapeDtypeStruct(s, k) for s, k in zip(outs, kinds)],
        in_specs=[pl.BlockSpec(memory_space=pl.ANY) if n in IN_HBM else vmem for n in INS],
        out_specs=[vmem] * len(OUTS),
        scratch_shapes=[pltpu.VMEM(s, BF) for s in bufs_shapes()]
        + [pltpu.VMEM(s, k) for _, s, k in LOCAL]
        + rs_scratch()
        + [dma((N_WIRE,)), dma((N_WIRE,)), dma((9,)), dma((N_SWAP,)), dma((N_SWAP,))],
        compiler_params=pltpu.CompilerParams(
            collective_id=0, has_side_effects=True, vmem_limit_bytes=127 * 2**19
        ),
        name="two_layers",
    )(*ins)


def rope_tables(segment_row, head_size):
    length = segment_row.shape[0]
    places = jnp.arange(length, dtype=jnp.int32)
    changes = jnp.concatenate(
        [jnp.ones((1,), jnp.int32), (segment_row[1:] != segment_row[:-1]).astype(jnp.int32)]
    )
    starts = lax.cummax(places * changes, axis=0)
    offsets = (places - starts).astype(F32)
    ladder = jnp.arange(head_size // 2, dtype=F32) * (-2.0 * math.log(rope_base) / head_size)
    angles = offsets[:, None] * jnp.exp(ladder)[None, :]
    cos, sin = jnp.cos(angles), jnp.sin(angles)
    return (
        jnp.concatenate([cos, cos, cos, cos], axis=-1),
        jnp.concatenate([-sin, sin, -sin, sin], axis=-1),
    )


def mask_of(segment_row):
    places = jnp.arange(segment_row.shape[0], dtype=jnp.int32)
    seen = (segment_row[:, None] == segment_row[None, :]) & (places[None, :] <= places[:, None])
    return jnp.where(seen, 0.0, -1e30).astype(F32)


def shards(
    tokens_in, out_grad, segments, norm1_gain, qkv_weight, qkv_bias, out_weight, norm2_gain,
    gate_weight, up_weight, down_weight,
):
    half = MICRO * SEQ
    rows = segments[:, 0]
    cos, sin = jax.vmap(rope_tables, in_axes=(0, None))(rows, HEAD_DIM)
    parts = run_layers([
        gate_weight[0],
        up_weight[0],
        down_weight[0],
        qkv_weight[0],
        out_weight[0],
        norm1_gain,
        qkv_bias,
        norm2_gain,
        tokens_in.reshape(half, D),
        out_grad.reshape(half, D),
        cos.reshape(half, 128),
        sin.reshape(half, 128),
        jax.vmap(mask_of)(rows),
        *constants(),
    ])
    shape = (1, MICRO, 1, SEQ, D)
    y, dh, a, q, b, o, c, g, u, d = finish_grads(parts)
    q, o, g, u, d = [part.transpose(1, 0, 2) for part in (q, o, g, u, d)]
    return y.reshape(shape), dh.reshape(shape), a, q, b, o, c, g, u, d


def solution(mesh):
    in_specs = (
        P(None, "fsdp", None, None),
        P(None, "fsdp", None, None),
        P(None, "fsdp", None),
        P("section", "fsdp"),
        P("section", "fsdp", None),
        P("section", "fsdp"),
        P("section", "fsdp", None),
        P("section", "fsdp"),
        P("section", "fsdp", None),
        P("section", "fsdp", None),
        P("section", "fsdp", None),
    )
    out_specs = (
        P("section", None, "fsdp", None, None),
        P("section", None, "fsdp", None, None),
        P("section", "fsdp"),
        P("section", "fsdp", None),
        P("section", "fsdp"),
        P("section", "fsdp", None),
        P("section", "fsdp"),
        P("section", "fsdp", None),
        P("section", "fsdp", None),
        P("section", "fsdp", None),
    )
    return jax.shard_map(shards, mesh=mesh, in_specs=in_specs, out_specs=out_specs, check_vma=False)
```

```python
import math
from types import SimpleNamespace

import jax
import jax.numpy as jnp
from jax import lax
from jax.experimental import pallas as pl
from jax.experimental.pallas import tpu as pltpu
from jax.sharding import PartitionSpec as P
import numpy as np

HEADS = 14
KV_HEADS = 2
HEAD_DIM = 64
MICRO = 2
SEQ = 128
D = 896
DP = 1024
QKV = 1152
norm_epsilon = 1e-06
rope_base = 1000000.0

MESH = pl.DeviceIdType.MESH
BF = jnp.bfloat16
F32 = jnp.float32


class Peer:
    def __init__(self, id, link):
        self.id, self.link = id, link


class Place:
    def __init__(self):
        f = lax.axis_index("fsdp")
        self.s = lax.axis_index("section")
        self.c = lax.rem(f, 2)
        self.z = lax.rem(f // 2, 4)
        self.y = lax.rem(f // 8, 2)
        self.x = f // 16

    def at(self, s=None, x=None, y=None, z=None, c=None):
        s = self.s if s is None else s
        x = self.x if x is None else x
        y = self.y if y is None else y
        z = self.z if z is None else z
        c = self.c if c is None else c
        return (s, ((x * 2 + y) * 4 + z) * 2 + c)

    def step(self, axis, k):
        here = self.x if axis == "x" else self.z
        return lax.rem(here + (k + 4), 4)

    def to(self, axis, k):
        return Peer(self.at(**{axis: self.step(axis, k)}), (axis, k))

    def across(self):
        return Peer(self.at(y=1 - self.y), "y")

    def mate(self):
        return Peer(self.at(c=1 - self.c), "mate")

    def beyond(self):
        return Peer(self.at(s=1 - self.s, y=1 - self.y), "section")


def greet(place):
    barrier = pltpu.get_barrier_semaphore()
    near = (
        place.to("x", 1), place.to("x", -1), place.to("z", 1), place.to("z", -1),
        place.across(), place.mate(), place.beyond(),
    )
    for peer in near:
        pl.semaphore_signal(barrier, inc=1, device_id=peer.id, device_id_type=MESH)
    pl.semaphore_wait(barrier, len(near))


RATE = {"mate": 150e3}
LINK_RATE = 48e3
LATENCY = 1.5


class Wire:
    def __init__(self, send_sems, recv_sems):
        self.send_sems, self.recv_sems = send_sems, recv_sems
        self.count, self.started, self.flows = 0, [], []
        self.now, self.free = 0.0, {}

    def send(self, src, dst, peer):
        k = self.count
        self.count += 1
        assert k < self.send_sems.shape[0]
        copy = pltpu.make_async_remote_copy(
            src_ref=src, dst_ref=dst, send_sem=self.send_sems.at[k],
            recv_sem=self.recv_sems.at[k], device_id=peer.id, device_id_type=MESH,
        )
        copy.start()
        self.started.append(copy)
        size = 2 * math.prod(dst.shape)
        begin = max(self.now, self.free.get(peer.link, 0.0))
        self.free[peer.link] = begin + size / RATE.get(peer.link, LINK_RATE)
        copy.there = self.free[peer.link] + LATENCY
        return copy

    def drain(self):
        for copy in self.started:
            copy.wait_send()
        self.started = []

    def add(self, flow):
        self.flows.append([None, flow])
        self.go_on(self.flows[-1])

    def go_on(self, entry):
        try:
            entry[0] = next(entry[1])
        except StopIteration:
            self.flows.remove(entry)

    def run(self):
        while self.flows:
            times = [(entry[0](), k) for k, entry in enumerate(self.flows)]
            when, k = min((t, k) for t, k in times if t is not None)
            self.now = max(self.now, when)
            self.go_on(self.flows[k])

    def busy(self, us):
        self.now += us


def got(*copies):
    yield lambda: max(copy.there for copy in copies)
    for copy in copies:
        copy.wait_recv()


def until(condition):
    yield lambda: 0.0 if condition() else None


def ring(wire, place, axis, piece, spawn):
    me = place.x if axis == "x" else place.z
    before, after, far = place.step(axis, -1), place.step(axis, 1), place.step(axis, 2)
    r = wire.send(piece(me), piece(me), place.to(axis, 1))
    l = wire.send(piece(me), piece(me), place.to(axis, -1))
    last = []

    def right():
        yield from got(r)
        last.append(wire.send(piece(before, 0), piece(before, 0), place.to(axis, 1)))
        spawn(before)

    def left():
        yield from got(l)
        last.append(wire.send(piece(after, 1), piece(after, 1), place.to(axis, -1)))
        spawn(after)

    def rest():
        yield from until(lambda: len(last) == 2)
        yield from got(*last)
        spawn(far)

    for flow in (right(), left(), rest()):
        wire.add(flow)


def gather_yab(wire, place, slot, first, last, finished):
    x, y, z = place.x, place.y, place.z
    cross = wire.send(slot(x, y, z), slot(x, y, z), place.across())
    yield from got(cross)
    mine = {"x": x, "z": z}
    count = []

    def piece(a, b, half=None):
        return slot(b, half, a) if first == "z" else slot(a, half, b)

    def arrived(b):
        count.append(b)
        if len(count) == 16:
            finished()

    def along_last(a):
        arrived(a)
        ring(wire, place, last, lambda b, half=None: piece(a, b, half), arrived)

    ring(wire, place, first, lambda a, half=None: piece(a, mine[last], half), along_last)
    along_last(mine[first])


def gather_down(wire, place, D, finished):
    x, y, z = place.x, place.y, place.z
    count = []

    def by_x(a, half=None):
        if half is None:
            return D.at[a, y, z]
        return D.at[a, y, z, pl.ds(0, 48) if half == 0 else pl.ds(48, 32)]

    def by_z(b, half=None):
        if half is None:
            return D.at[:, y, b]
        return D.at[pl.ds(2 * half, 2), y, b]

    def along_y(b):
        cross = wire.send(by_z(b), by_z(b), place.across())

        def arrival():
            yield from got(cross)
            count.append(b)
            if len(count) == 4:
                finished()

        wire.add(arrival())

    def x_done(a):
        seen.append(a)
        if len(seen) == 3:
            ring(wire, place, "z", by_z, along_y)
            along_y(z)

    seen = []
    ring(wire, place, "x", by_x, x_done)


BLOCK = dict(G=(32, 2560), U=(32, 2560), D=(80, 896), Q=(32, 1152), O=(32, 896))


def start_gather(wire, place, ins, bufs, local_sems, done, pack):
    x, y, z, c = place.x, place.y, place.z, place.c
    rows = pl.ds(pl.multiple_of(c * 16, 16), 16)
    G, U, D, Q, O = bufs
    g_in, u_in, d_in, q_in, o_in = ins
    own = {}

    def place_own(name, k, src, dst):
        pack(name)
        own[name] = pltpu.make_async_copy(src, dst, local_sems.at[k])
        own[name].start()

    def whole(buf):
        def slot(px, half, pz):
            if half is None:
                return buf.at[px, :, pz]
            return buf.at[px, half, pz]
        return slot

    def part(buf):
        def slot(px, half, pz):
            if half is None:
                return buf.at[px, :, pz, rows]
            return buf.at[px, half, pz, rows]
        return slot

    def attention(name, buf):
        own[name].wait()
        filled = []
        yield from gather_yab(wire, place, part(buf), "z", "x", lambda: filled.append(1))
        yield from until(lambda: filled)
        mine = buf.at[:, :, :, rows]
        swap = wire.send(mine, mine, place.mate())
        yield from got(swap)
        done.add(name)

    def hidden(name, buf, swap, first, last):
        yield from got(swap)
        own[name].wait()
        yield from gather_yab(wire, place, whole(buf), first, last, lambda: done.add(name))

    place_own("Q", 0, q_in, Q.at[x, y, z, rows])
    wire.add(attention("Q", Q))
    place_own("O", 1, o_in, O.at[x, y, z, rows])
    wire.add(attention("O", O))
    place_own("D", 2, d_in, D.at[x, y, z])
    own["D"].wait()
    gather_down(wire, place, D, lambda: done.add("D"))
    for name, k, src, dst, first, last in (("G", 3, g_in, G, "z", "x"), ("U", 4, u_in, U, "x", "z")):
        place_own(name, k, src.at[c], dst.at[x, y, z, rows])
        swap = wire.send(src.at[1 - c], dst.at[x, y, z, rows], place.mate())
        wire.add(hidden(name, dst, swap, first, last))


def bufs_shapes():
    return [(4, 2, 4) + BLOCK[k] for k in "GUDQO"]


def add(dst, *srcs):
    total = dst[...]
    for src in srcs:
        total = total + src[...]
    dst[...] = total


def add_each(count, dst, *srcs):
    def body(i, carry):
        add(dst(i), *[src(i) for src in srcs])
        return carry
    lax.fori_loop(0, count, body, 0)


def scatter_ring(wire, place, axis, piece, land, halves, finished):
    me = place.x if axis == "x" else place.z
    before, after, far = place.step(axis, -1), place.step(axis, 1), place.step(axis, 2)
    l1a, l1b, l2a, l2b = land
    r = wire.send(piece(far, 0), l1a, place.to(axis, 1))
    l = wire.send(piece(far, 1), l1b, place.to(axis, -1))
    last = []

    def right():
        yield from got(r)
        add(piece(after, 0), l1a)
        last.append(wire.send(piece(after), l2a, place.to(axis, 1)))

    def left():
        yield from got(l)
        add(piece(before, 1), l1b)
        last.append(wire.send(piece(before), l2b, place.to(axis, -1)))

    def rest():
        yield from until(lambda: len(last) == 2)
        yield from got(*last)
        halves(lambda i: piece(me, i), l2a, l2b)
        finished()

    for flow in (right(), left(), rest()):
        wire.add(flow)


def two_halves(dst, a, b):
    for i in range(2):
        add(dst(i), a.at[i], b.at[i])


def far_first(place, axis):
    me = place.x if axis == "x" else place.z
    return [place.step(axis, k) for k in (2, 1, -1)] + [me]


def scatter_aby(wire, place, slot, R, first, last, have=lambda k: True):
    r1a, r1b, r2a, r2b, s1a, s1b, s2a, s2b, t_buf = R
    mine = {"x": place.x, "z": place.z}

    def piece(a, b, half=None):
        return slot(b, half, a) if first == "z" else slot(a, half, b)

    order = far_first(place, last)
    filled = []

    def start(k, b):
        yield from until(lambda: have(k))
        scatter_ring(
            wire, place, first, lambda a, half=None: piece(a, b, half),
            (r1a.at[k], r1b.at[k], r2a.at[k], r2b.at[k]), two_halves, lambda: filled.append(k),
        )

    for k, b in enumerate(order):
        wire.add(start(k, b))
    a0 = mine[first]
    bq, bp, bm, b0 = order
    sent = []

    def outer():
        yield from until(lambda: 0 in filled)
        d_r = wire.send(piece(a0, bq, 0), s1a, place.to(last, 1))
        d_l = wire.send(piece(a0, bq, 1), s1b, place.to(last, -1))

        def right():
            yield from until(lambda: 1 in filled)
            yield from got(d_r)
            add(piece(a0, bp, 0), s1a)
            sent.append(wire.send(piece(a0, bp), s2a, place.to(last, 1)))

        def left():
            yield from until(lambda: 2 in filled)
            yield from got(d_l)
            add(piece(a0, bm, 1), s1b)
            sent.append(wire.send(piece(a0, bm), s2b, place.to(last, -1)))

        wire.add(right())
        wire.add(left())

    wire.add(outer())
    yield from until(lambda: len(sent) == 2 and 3 in filled)
    yield from got(*sent)
    two_halves(lambda i: piece(a0, b0, i), s2a, s2b)
    cross = wire.send(slot(place.x, 1 - place.y, place.z), t_buf, place.across())
    yield from got(cross)
    add(slot(place.x, place.y, place.z), t_buf)


def scatter_down(wire, place, D, R):
    yb, z1a, z1b, z2a, z2b, xa, xb, x2a, x2b = R
    x, y, z = place.x, place.y, place.z
    zp, zm, zq = place.step("z", 1), place.step("z", -1), place.step("z", 2)
    order = (zq, zp, zm, z)
    crossing = [wire.send(D.at[:, 1 - y, b], yb.at[k], place.across()) for k, b in enumerate(order)]
    sent = []

    def settle(k):
        yield from got(crossing[k])
        add_each(4, lambda i: D.at[i, y, order[k]], lambda i: yb.at[k, i])

    yield from settle(0)
    d_r = wire.send(D.at[pl.ds(0, 2), y, zq], z1a, place.to("z", 1))
    d_l = wire.send(D.at[pl.ds(2, 2), y, zq], z1b, place.to("z", -1))

    def right():
        yield from settle(1)
        yield from got(d_r)
        add_each(2, lambda i: D.at[i, y, zp], lambda i: z1a.at[i])
        sent.append(wire.send(D.at[:, y, zp], z2a, place.to("z", 1)))

    def left():
        yield from settle(2)
        yield from got(d_l)
        add_each(2, lambda i: D.at[i + 2, y, zm], lambda i: z1b.at[i])
        sent.append(wire.send(D.at[:, y, zm], z2b, place.to("z", -1)))

    wire.add(right())
    wire.add(left())
    yield from settle(3)
    yield from until(lambda: len(sent) == 2)
    yield from got(*sent)
    add_each(4, lambda i: D.at[i, y, z], lambda i: z2a.at[i], lambda i: z2b.at[i])

    def by_x(a, half=None):
        if half is None:
            return D.at[a, y, z]
        return D.at[a, y, z, pl.ds(0, 48) if half == 0 else pl.ds(48, 32)]

    ended = []
    scatter_ring(
        wire, place, "x", by_x, (xa, xb, x2a, x2b),
        lambda dst, a, b: add(D.at[x, y, z], a, b), lambda: ended.append(1),
    )
    yield from until(lambda: ended)


def rs_scratch():
    def aby(rows, cols):
        shapes = [(4, rows, cols)] * 2 + [(4, 2, rows, cols)] * 2 + [(rows, cols)] * 2 + [(2, rows, cols)] * 2 + [(rows, cols)]
        return [pltpu.VMEM(s, BF) for s in shapes]
    out = []
    out += aby(32, 2560) + [pltpu.VMEM((16, 2560), BF)]
    out += aby(32, 2560) + [pltpu.VMEM((16, 2560), BF)]
    b = (80, 896)
    out += [pltpu.VMEM(s, BF) for s in (
        (4, 4) + b, (2,) + b, (2,) + b, (4,) + b, (4,) + b, (48, 896), (32, 896), b, b)]
    out += aby(16, 1152) + [pltpu.VMEM((4, 2, 4, 16, 1152), BF)]
    out += aby(16, 896) + [pltpu.VMEM((4, 2, 4, 16, 896), BF)]
    return out


N_RS_SCRATCH = 10 + 10 + 9 + 10 + 10


def start_scatter(wire, place, bufs, R, made, end):
    x, y, z, c = place.x, place.y, place.z, place.c
    G, U, D, Q, O = bufs
    rg, ru, rd, rq, ro = R[:10], R[10:20], R[20:29], R[29:39], R[39:49]
    rows = pl.ds(pl.multiple_of(c * 16, 16), 16)
    others = pl.ds(pl.multiple_of(16 - c * 16, 16), 16)

    def whole(buf):
        def slot(px, half, pz):
            return buf.at[px, :, pz] if half is None else buf.at[px, half, pz]
        return slot

    def part(buf):
        def slot(px, half, pz):
            return buf.at[px, :, pz, rows] if half is None else buf.at[px, half, pz, rows]
        return slot

    def hidden(name, buf, r, first, last):
        if name == "G":
            yield from until(lambda: name in made)
            have = lambda k: True
        else:
            have = lambda k: name + str(k) in made
        yield from scatter_aby(wire, place, whole(buf), r[:9], first, last, have)
        swap = wire.send(buf.at[x, y, z, others], r[9], place.mate())
        yield from got(swap)
        end(name, c, buf[x, y, z, rows], r[9][...])

    def attention(name, buf, r):
        yield from until(lambda: name in made)
        swap = wire.send(buf.at[:, :, :, others], r[9], place.mate())
        yield from got(swap)
        add_each(32, lambda i: buf.at[i // 8, lax.rem(i // 4, 2), lax.rem(i, 4), rows],
                 lambda i: r[9].at[i // 8, lax.rem(i // 4, 2), lax.rem(i, 4)])
        yield from scatter_aby(wire, place, part(buf), r[:9], "x", "z")
        end(name, c, buf[x, y, z, rows])

    def down():
        yield from until(lambda: "D" in made)
        yield from scatter_down(wire, place, D, rd)
        end("D", c, D[x, y, z])

    wire.add(down())
    wire.add(hidden("G", G, rg, "x", "z"))
    wire.add(hidden("U", U, ru, "z", "x"))
    wire.add(attention("O", O, ro))
    wire.add(attention("Q", Q, rq))


TOK = 256
FF = 2560


def mm(a, b):
    return jnp.dot(a, b, preferred_element_type=F32)


def mm_t(a, b):
    return lax.dot_general(a, b, (((1,), (1,)), ((), ())), preferred_element_type=F32)


def t_mm(a, b):
    return lax.dot_general(a, b, (((0,), (0,)), ((), ())), preferred_element_type=F32)


def constants():
    d = np.arange(D)
    spread = np.zeros((D, DP), np.float32)
    spread[d, 16 * (d // 14) + d % 14] = 1
    pick = np.zeros((64, DP), np.float32)
    pick[np.arange(64), 16 * np.arange(64) + 14] = 1
    own14 = (np.arange(64)[:, None] == d[None] // 14).astype(np.float32)
    j = np.arange(QKV)
    own18 = (np.arange(64)[:, None] == j[None] // 18).astype(np.float32)
    lane = np.arange(128)[:, None]
    e1 = (lane == d[None] % 14).astype(np.float32)
    eb = (lane == 64 + j[None] % 18).astype(np.float32)
    return [jnp.asarray(a, BF) for a in (spread, pick, own14, own18, e1, eb)]


CONST = ("spread", "pick", "own14", "own18", "e1", "eb")


def cols(buf, start, size):
    value = buf[:, :, :, :, pl.ds(start, size)]
    return value.reshape(-1, size)


def put(ref, value):
    ref[...] = value.reshape(ref.shape)


def rotate(x, lo32):
    return jnp.where(lo32, pltpu.roll(x, 96, 1), pltpu.roll(x, 32, 1))


def lane_is(shape, width, below):
    lane = lax.broadcasted_iota(jnp.int32, shape, 1)
    return lax.rem(lane, width) < below


def gains(R):
    q = cols(R.Q, 0, 128)
    s = mm(R.pick[...], q)
    s2 = pltpu.roll(s, 96, 1).astype(BF)
    s = s.astype(BF)
    R.g1[...] = jnp.sum(mm(s, R.e1[...]) * R.own14[...].astype(F32), axis=0, keepdims=True)
    R.g2[...] = jnp.sum(mm(s2, R.e1[...]) * R.own14[...].astype(F32), axis=0, keepdims=True)
    R.bias[...] = jnp.sum(mm(s, R.eb[...]) * R.own18[...].astype(F32), axis=0, keepdims=True)


def inverse_rms(h):
    return lax.rsqrt(jnp.sum(h * h, axis=-1, keepdims=True) * (1.0 / D) + norm_epsilon)


def project_qkv(R, source, tables, rows, size):
    h = source[rows].astype(F32)
    n1 = (h * inverse_rms(h) * R.g1[...]).astype(BF)
    R.N1[rows] = mm(n1, R.spread[...]).astype(BF)
    lo32 = lane_is((size, 128), 64, 32)
    lo = lane_is((size, 128), 128, 64)
    cos, sin = tables[0][rows], tables[1][rows]
    for start, width in ((0, 256), (256, 256), (512, 256), (768, 256), (1024, 128)):
        out = mm(R.N1[rows], cols(R.Q, start, width)) + R.bias[:, start:start + width]
        for k in range(width // 128):
            x = out[:, 128 * k:128 * k + 128]
            tile = (start + 128 * k) // 128
            if tile < 8:
                x = x * cos + rotate(x, lo32) * sin
            if tile < 7:
                R.QR[rows, 128 * tile:128 * tile + 128] = x.astype(BF)
            else:
                x = x.astype(BF).astype(F32)
                swapped = pltpu.roll(x, 64, 1)
                R.KV[tile - 7, 0, rows] = jnp.where(lo, x, swapped).astype(BF)
                R.KV[tile - 7, 1, rows] = x.astype(BF)
                R.KV[tile - 7, 2, rows] = jnp.where(lo, swapped, x).astype(BF)


def two_heads(R, tile):
    return jnp.concatenate([tile * R.lanes[0], tile * R.lanes[1]], axis=0)


def beside(x):
    return jnp.concatenate([x[:SEQ], x[SEQ:]], axis=1)


def variant_of(t):
    return 0 if t < 3 else (2 if t > 3 else 1)


def probs_of(R, mask, t, rows):
    q2 = two_heads(R, R.QR[rows, 128 * t:128 * t + 128])
    kk = R.KV[0, variant_of(t), rows]
    s = mm_t(q2, kk) * 0.125 + jnp.concatenate([mask, mask], axis=0)
    e = jnp.exp(s - jnp.max(s, axis=-1, keepdims=True))
    p = e * (1.0 / jnp.sum(e, axis=-1, keepdims=True))
    return q2, kk, p


def attend(R, tables, m):
    rows = own_rows(m)
    mask = tables[2][m]
    for t in range(7):
        _, _, p = probs_of(R, mask, t, rows)
        vv = two_heads(R, R.KV[1, variant_of(t), rows])
        R.DQKV[rows, 128 * t:128 * t + 128] = mm(beside(p.astype(BF)), vv).astype(BF)


def own_rows(m):
    return pl.ds(SEQ * m, SEQ)


def pair_own(m):
    return pl.ds(2 * SEQ * m, SEQ)


def pair_other(m):
    return pl.ds(2 * SEQ * m + SEQ, SEQ)


def pair(m):
    return pl.ds(2 * SEQ * m, 2 * SEQ)


def after_attention(R, source, m):
    rows = own_rows(m)
    R.CP[rows] = mm(R.DQKV[rows, :D], R.spread[...]).astype(BF)
    mid = source[rows].astype(F32) + mm(R.CP[rows], cols(R.O, 0, D))
    R.MID[rows] = mid
    n2 = (mid * inverse_rms(mid) * R.g2[...]).astype(BF)
    R.N2[pair_own(m)] = mm(n2, R.spread[...]).astype(BF)


def sigmoid(v):
    return 0.5 * jnp.tanh(0.5 * v) + 0.5


def hidden(R, rows):
    def body(j, carry):
        at = pl.ds(pl.multiple_of(j * 1280, 1280), 1280)
        n2 = R.N2[rows]
        gate = mm(n2, R.G[:, :, :, :, at].reshape(DP, 1280))
        up = mm(n2, R.U[:, :, :, :, at].reshape(DP, 1280))
        R.GA[rows, at] = gate.astype(BF)
        R.UP[rows, at] = up.astype(BF)
        R.ACT[rows, at] = (gate * sigmoid(gate) * up).astype(BF)
        return carry

    lax.fori_loop(0, FF // 1280, body, 0)


def hidden_other(R, swap, m):
    swap.n2(m).wait_recv()
    hidden(R, pair_other(m))


class Swap:
    def __init__(self, R, place):
        own = own_rows
        mate, across, beyond = place.mate(), place.across(), place.beyond()

        def table(k, refs, device):
            return lambda m: pltpu.make_async_remote_copy(
                src_ref=refs(m)[0], dst_ref=refs(m)[1], send_sem=R.xs.at[2 * k + m],
                recv_sem=R.xr.at[2 * k + m], device_id=device.id, device_id_type=MESH,
            )

        self.n2 = table(0, lambda m: (R.N2.at[pair_own(m)], R.N2.at[pair_other(m)]), mate)
        self.part = table(1, lambda m: (R.DB.at[own(m)], R.DC.at[own(m)]), mate)
        self.dy = table(2, lambda m: (R.DY.at[pair_own(m)], R.DY.at[pair_other(m)]), mate)
        self.dn = table(3, lambda m: (R.dn, R.dn_in.at[own(m)]), mate)
        self.hop_h = table(4, lambda m: (R.ys.at[own(m)], R.h.at[own(m)]), beyond)
        self.hop_dy = table(5, lambda m: (R.dhs.at[own(m)], R.DY.at[pair_own(m)]), beyond)
        self.og = table(6, lambda m: (R.og.at[own(m)], R.DY.at[pair_own(m)]), across)
        self.cos = table(7, lambda m: (R.cos.at[own(m)], R.tcos.at[own(m)]), across)
        self.sin = table(8, lambda m: (R.sin.at[own(m)], R.tsin.at[own(m)]), across)
        self.mask = table(9, lambda m: (R.mask.at[m], R.tmask.at[m]), across)
        self.y = table(10, lambda m: (R.ys.at[own(m)], R.y.at[own(m)]), across)
        self.dh = table(11, lambda m: (R.dhs.at[own(m)], R.dh.at[own(m)]), across)


N_SWAP = 24


def down_sent(R, swap, m):
    R.DB[own_rows(m)] = mm(R.ACT[pair_other(m)], R.D[...].reshape(FF, D)).astype(BF)
    swap.part(m).start()
    R.acc[SEQ:, 0:D] = R.MID[own_rows(m)] + mm(R.ACT[pair_own(m)], R.D[...].reshape(FF, D))


def down_done(R, swap, m):
    swap.part(m).wait_recv()
    R.ys[own_rows(m)] = (R.acc[SEQ:, 0:D] + R.DC[own_rows(m)].astype(F32)).astype(BF)
    swap.part(m).wait_send()


def hidden_back(R, m):
    rows = pair(m)

    def body(j, carry):
        down = R.D[j].reshape(640, D)
        for start, size in ((0, 256), (256, 256), (512, 128)):
            sub = pl.ds(pl.multiple_of(j * 640 + start, 128), size)
            dact = mm_t(R.DY[rows], down[start:start + size])
            gate = R.GA[rows, sub].astype(F32)
            up = R.UP[rows, sub].astype(F32)
            sig = sigmoid(gate)
            R.GA[rows, sub] = (dact * up * sig * (1.0 + gate * (1.0 - sig))).astype(BF)
            R.UP[rows, sub] = (dact * gate * sig).astype(BF)
        return carry

    lax.fori_loop(0, FF // 640, body, 0)


def normed_piece(R, m, x):
    rows = pair(m)
    at = pl.ds(pl.multiple_of(x * 256, 256), 256)
    R.acc[:, at] = mm_t(R.GA[rows], R.G[x].reshape(256, FF)) + mm_t(R.UP[rows], R.U[x].reshape(256, FF))


def normed_sent(R, swap, m):
    R.dn[...] = R.acc[SEQ:].astype(BF)
    swap.dn(m).start()


def normed_back(R, swap, m):
    def body(x, carry):
        normed_piece(R, m, x)
        return carry

    lax.fori_loop(0, 4, body, 0)
    normed_sent(R, swap, m)


def middle_back(R, swap, m):
    rows = own_rows(m)
    swap.dn(m).wait_recv()
    dn2p = (R.acc[:SEQ] + R.dn_in[rows].astype(F32)).astype(BF)
    dn2 = mm_t(dn2p, R.spread[...])
    mid = R.MID[rows]
    inv2 = inverse_rms(mid)
    R.dg2[m] = jnp.sum(dn2 * mid * inv2, axis=0, keepdims=True)
    scaled = dn2 * R.g2[...]
    mean = jnp.sum(scaled * mid, axis=-1, keepdims=True) * (1.0 / D)
    dmid = R.DY[pair_own(m)].astype(F32) + inv2 * scaled - mid * (inv2 * inv2 * inv2 * mean)
    R.MID[rows] = dmid
    R.DB[rows] = dmid.astype(BF)
    dctx = mm_t(R.DB[rows], cols(R.O, 0, D)).astype(BF)
    R.DC[rows] = mm_t(dctx, R.spread[...]).astype(BF)
    swap.dn(m).wait_send()


def attend_back(R, tables, m, tiles=range(7)):
    rows = own_rows(m)
    cos, sin, mask = tables[0][rows], tables[1][rows], tables[2][m]
    lo32 = lane_is((SEQ, 128), 64, 32)
    lo = lane_is((SEQ, 128), 128, 64)

    def spin_back(g):
        return g * cos + rotate(g * sin, lo32)

    for t in tiles:
        q2, kk, p = probs_of(R, mask, t, rows)
        var = variant_of(t)
        dc2 = two_heads(R, R.DC[rows, 128 * t:128 * t + 128])
        dp = mm_t(dc2, R.KV[1, var, rows])
        ds = (p * (dp - jnp.sum(p * dp, axis=-1, keepdims=True))).astype(BF)
        dk, dv = t_mm(ds, q2), t_mm(p.astype(BF), dc2)
        if t in (0, 3, 4):
            R.dkv[0, var] = dk
            R.dkv[1, var] = dv
        else:
            R.dkv[0, var] += dk
            R.dkv[1, var] += dv
        dq = mm(beside(ds), two_heads(R, kk)) * 0.125
        R.DQKV[rows, 128 * t:128 * t + 128] = spin_back(dq).astype(BF)

    if 6 not in tiles:
        return

    def joined(k):
        first, mixed, last = R.dkv[k, 0], R.dkv[k, 1], R.dkv[k, 2]
        return mixed + jnp.where(
            lo, first + pltpu.roll(first, 64, 1), last + pltpu.roll(last, 64, 1)
        )

    R.DQKV[rows, 896:1024] = spin_back(joined(0) * 0.125).astype(BF)
    R.DQKV[rows, 1024:1152] = joined(1).astype(BF)


def stream_back(R, m):
    rows = own_rows(m)
    dqkv = R.DQKV[rows]
    R.dbias[m] = jnp.sum(dqkv.astype(F32), axis=0, keepdims=True)
    dn1 = mm_t(mm_t(dqkv, cols(R.Q, 0, QKV)).astype(BF), R.spread[...])
    h = R.h[rows].astype(F32)
    inv1 = inverse_rms(h)
    R.dg1[m] = jnp.sum(dn1 * h * inv1, axis=0, keepdims=True)
    scaled = dn1 * R.g1[...]
    mean = jnp.sum(scaled * h, axis=-1, keepdims=True) * (1.0 / D)
    R.dhs[rows] = (R.MID[rows] + inv1 * scaled - h * (inv1 * inv1 * inv1 * mean)).astype(BF)


def pause(wire):
    now = wire.now
    yield lambda: now


ORDER = ("N", "U0", "G", "U1", "U2", "U3", "D", "M", "O", "R", "Q")


def weight_grads(R, wire, done, rest, slabs):
    def step(us, body):
        body()
        wire.busy(us)
        yield from pause(wire)

    def down(x):
        at = pl.ds(640 * x, 640)
        for start, size in ((0, 512), (512, 384)):
            grad = t_mm(R.ACT[:, at], R.DY[:, start:start + size])
            put(R.D.at[x, :, :, :, pl.ds(start, size)], grad.astype(BF))

    def wide(buf, grad, x):
        n2 = R.N2[:, pl.ds(pl.multiple_of(x * 256, 256), 256)]
        for start in range(0, FF, 512):
            at = pl.ds(start, 512)
            put(buf.at[x, :, :, :, at], t_mm(n2, grad[:, at]).astype(BF))

    def out_rows(x):
        rows = pl.ds(256 * x, 256)
        put(R.O.at[x], t_mm(R.CP[:, rows], R.DB[...]).astype(BF))

    def small_rows():
        small = (
            mm_t((R.own14[...].astype(F32) * (R.dg1[0] + R.dg1[1])).astype(BF), R.e1[...])
            + pltpu.roll(
                mm_t((R.own14[...].astype(F32) * (R.dg2[0] + R.dg2[1])).astype(BF), R.e1[...]), 32, 1
            )
            + mm_t((R.own18[...].astype(F32) * (R.dbias[0] + R.dbias[1])).astype(BF), R.eb[...])
        )
        R.small[...] = small.astype(BF)

    def qkv_rows(x):
        rows = pl.ds(256 * x, 256)
        n1 = R.N1[:, rows]
        for start in range(0, QKV, 384):
            g = t_mm(n1, R.DQKV[:, start:start + 384])
            if start == 0:
                g = jnp.concatenate([g[:, :128] + t_mm(R.pick[:, rows], R.small[...]), g[:, 128:]], axis=1)
            put(R.Q.at[x, :, :, :, pl.ds(start, 384)], g.astype(BF))

    early, middle, late = rest
    for name in ORDER:
        if name == "N":
            for piece in early:
                yield from step(0.9, piece)
        elif name == "M":
            for piece in middle:
                yield from step(2.3, piece)
        elif name == "R":
            for piece in late:
                yield from step(1.9, piece)
        elif name == "Q":
            yield from step(0.2, small_rows)
            for x in range(4):
                yield from step(0.4, lambda: qkv_rows(x))
        elif name == "O":
            for x in range(4):
                yield from step(0.3, lambda: out_rows(x))
        elif name == "D":
            for x in range(4):
                yield from step(0.75, lambda: down(x))
        elif name == "G":
            for x in range(4):
                yield from step(1.1, lambda: wide(R.G, R.GA, x))
        else:
            yield from step(1.1, lambda: wide(R.U, R.UP, slabs[int(name[1])]))
        done.add(name)


def pack(R, name):
    if name in "GU":
        src, dst = (R.g_in, R.g_st) if name == "G" else (R.u_in, R.u_st)
        R.g_s[...] = jnp.zeros_like(R.g_s)
        for f in range(64):
            piece = src[:, 76 * f:76 * f + 76].astype(F32)
            R.g_s[f % 2, 0:14, 80 * (f // 2):80 * (f // 2) + 76] = piece
        dst[...] = R.g_s[...].astype(BF)
    elif name == "D":
        R.acc[0:80, 0:D] = jnp.zeros((80, D), F32)
        R.acc[0:76, 0:D] = R.d_in[...].astype(F32)
        R.d_st[...] = R.acc[0:80, 0:D].astype(BF)
    elif name == "O":
        R.o_s[...] = jnp.zeros_like(R.o_s)
        R.o_s[0:14] = R.o_in[...].astype(F32)
        R.o_st[...] = R.o_s[...].astype(BF)
    else:
        R.q_s[...] = jnp.zeros_like(R.q_s)
        R.q_s[0:14] = R.q_in[...].astype(F32)
        R.q_s[14:15, 0:14] = R.a_in[...].astype(F32)
        R.q_s[14:15, 32:46] = R.c_in[...].astype(F32)
        R.q_s[14:15, 64:82] = R.b_in[...].astype(F32)
        R.q_st[...] = R.q_s[...].astype(BF)


def keep(R, name, c, mine, other=None):
    dst = getattr(R, name.lower() + "_o")
    if other is None:
        dst[...] = mine
    else:
        dst[c] = mine
        dst[1 - c] = other


def finish_kernel(
    y, dh, g_h, u_h, d_h, q_h, o_h, y_o, dh_o, a_o, q_o, b_o, o_o, c_o, g_o, u_o, d_o, g, u, d, q, o, wide, flat, sems
):
    moves = [
        pltpu.make_async_copy(src, dst, sems.at[k])
        for k, (src, dst) in enumerate(
            ((g_h, g), (u_h, u), (d_h, d), (q_h, q), (o_h, o), (y, y_o), (dh, dh_o))
        )
    ]
    for move in moves:
        move.start()
    for move in moves:
        move.wait()
    for src, dst in ((g, g_o), (u, u_o)):
        wide[...] = src[...].astype(F32)
        for f in range(64):
            at = 80 * (f // 2)
            flat[0:14, 76 * f:76 * f + 76] = wide[f % 2, 0:14, at:at + 76]
        for r in range(14):
            dst[r] = flat[r:r + 1, :]
    flat[0:80, 0:D] = d[...].astype(F32)
    for r in range(76):
        d_o[r] = flat[r:r + 1, 0:D]
    flat[0:16, 0:QKV] = q[...].astype(F32)
    for r in range(14):
        q_o[r] = flat[r:r + 1, 0:QKV]
    a_o[...] = flat[14:15, 0:14]
    c_o[...] = flat[14:15, 32:46]
    b_o[...] = flat[14:15, 64:82]
    flat[16:32, 0:D] = o[...].astype(F32)
    for r in range(14):
        o_o[r] = flat[16 + r:17 + r, 0:D]


def finish_grads(parts):
    shapes = [
        (TOK, D), (TOK, D), (1, 14), (14, 1, QKV), (1, 18), (14, 1, D), (1, 14),
        (14, 1, 4864), (14, 1, 4864), (76, 1, D),
    ]
    vmem = pl.BlockSpec(memory_space=pltpu.VMEM)
    return pl.pallas_call(
        finish_kernel,
        out_shape=[jax.ShapeDtypeStruct(s, BF if k < 2 else F32) for k, s in enumerate(shapes)],
        in_specs=[pl.BlockSpec(memory_space=pl.ANY)] * len(parts),
        out_specs=[vmem] * len(shapes),
        scratch_shapes=[pltpu.VMEM(part.shape, BF) for part in parts[2:]]
        + [pltpu.VMEM((2, 16, FF), F32), pltpu.VMEM((80, 4864), F32), pltpu.SemaphoreType.DMA((7,))],
        compiler_params=pltpu.CompilerParams(vmem_limit_bytes=127 * 2**19),
        name="finish_grads",
    )(*parts)


INS = ("g_in", "u_in", "d_in", "q_in", "o_in", "a_in", "b_in", "c_in", "tokens", "og", "cos", "sin", "mask") + CONST
IN_HBM = ("og", "tokens", "cos", "sin", "mask")
OUTS = ("y", "dh", "g_o", "u_o", "d_o", "q_o", "o_o")
LOCAL = (
    ("h", (TOK, D), BF), ("N1", (TOK, DP), BF), ("QR", (TOK, D), BF),
    ("KV", (2, 3, TOK, 128), BF), ("CP", (TOK, DP), BF),
    ("MID", (TOK, D), F32), ("N2", (2 * TOK, DP), BF), ("GA", (2 * TOK, FF), BF),
    ("UP", (2 * TOK, FF), BF), ("ACT", (2 * TOK, FF), BF), ("DY", (2 * TOK, D), BF), ("acc", (TOK, DP), F32), ("dn", (SEQ, DP), BF), ("dn_in", (TOK, DP), BF),
    ("DB", (TOK, D), BF), ("DC", (TOK, D), BF), ("DQKV", (TOK, QKV), BF),
    ("dkv", (2, 3, SEQ, 128), F32), ("lanes", (2, SEQ, 128), BF),
    ("small", (64, 128), BF),
    ("g1", (1, D), F32), ("g2", (1, D), F32), ("bias", (1, QKV), F32),
    ("dg1", (2, 1, D), F32), ("dg2", (2, 1, D), F32), ("dbias", (2, 1, QKV), F32),
    ("g_st", (2, 16, FF), BF), ("u_st", (2, 16, FF), BF), ("d_st", (80, D), BF),
    ("q_st", (16, QKV), BF), ("o_st", (16, D), BF), ("g_s", (2, 16, FF), F32),
    ("q_s", (16, QKV), F32), ("o_s", (16, D), F32),
    ("ys", (TOK, D), BF), ("dhs", (TOK, D), BF),
    ("tcos", (TOK, 128), F32), ("tsin", (TOK, 128), F32), ("tmask", (2, SEQ, SEQ), F32),
)


def layers_kernel(*refs):
    names = INS + OUTS + tuple("GUDQO") + tuple(name for name, _, _ in LOCAL)
    R = SimpleNamespace(**dict(zip(names, refs)))
    rest = refs[len(names):]
    R.ss, R.rs, R.ls, R.xs, R.xr = rest[N_RS_SCRATCH:]
    place = Place()
    greet(place)
    wire = Wire(R.ss, R.rs)
    swap = Swap(R, place)
    bufs = (R.G, R.U, R.D, R.Q, R.O)
    done = set()
    tables = (R.tcos, R.tsin, R.tmask)

    def only(section):
        return lambda body: pl.when(place.s == section)(body)

    @only(0)
    def _():
        moves = [
            pltpu.make_async_copy(src, dst, R.ls.at[5 + k])
            for k, (src, dst) in enumerate(zip((R.tokens, R.cos, R.sin, R.mask), (R.h,) + tables))
        ]
        for move in moves:
            move.start()
        for move in moves:
            move.wait()

    def early():
        yield from until(lambda: {"Q", "O"} <= done)
        gains(R)
        wire.busy(0.5)
        for m in range(MICRO):
            yield from pause(wire)
            only(0)(lambda: project_qkv(R, R.h, tables, own_rows(m), SEQ))
            wire.busy(1.2)
            yield from pause(wire)
            only(0)(lambda: attend(R, tables, m))
            wire.busy(1.3)
            yield from pause(wire)

            @only(0)
            def _():
                after_attention(R, R.h, m)
                swap.n2(m).start()

            wire.busy(1.5)

    start_gather(wire, place, (R.g_st, R.u_st, R.d_st, R.q_st, R.o_st), bufs, R.ls, done, lambda name: pack(R, name))
    @only(1)
    def _():
        for m in range(MICRO):
            for move in (swap.og, swap.cos, swap.sin, swap.mask):
                move(m).start()

    lo = lane_is((SEQ, 128), 128, 64).astype(F32)
    R.lanes[0] = lo.astype(BF)
    R.lanes[1] = (1.0 - lo).astype(BF)
    wire.add(early())
    wire.run()

    @only(0)
    def _():
        hidden(R, pair_own(0))
        hidden_other(R, swap, 0)
        down_sent(R, swap, 0)
        hidden(R, pair_own(1))
        down_done(R, swap, 0)
        swap.hop_h(0).start()
        hidden_other(R, swap, 1)
        down_sent(R, swap, 1)
        down_done(R, swap, 1)
        swap.hop_h(1).start()
        R.y[...] = R.ys[...]
        swap.hop_dy(0).wait_recv()
        swap.dy(0).start()
        swap.dy(0).wait_recv()
        hidden_back(R, 0)
        normed_back(R, swap, 0)
        middle_back(R, swap, 0)
        attend_back(R, tables, 0)
        stream_back(R, 0)
        swap.hop_dy(1).wait_recv()
        swap.dy(1).start()
        swap.dy(1).wait_recv()
        hidden_back(R, 1)

    @only(1)
    def _():
        def start(m):
            swap.hop_h(m).wait_recv()
            rows = own_rows(m)
            project_qkv(R, R.h, tables, rows, SEQ)
            attend(R, tables, m)
            after_attention(R, R.h, m)
            swap.n2(m).start()

        def feed(m):
            hidden(R, pair_own(m))
            hidden_other(R, swap, m)
            down_sent(R, swap, m)

        def fed(m):
            down_done(R, swap, m)
            swap.y(m).start()

        def finish(m):
            middle_back(R, swap, m)
            attend_back(R, tables, m)
            stream_back(R, m)
            swap.hop_dy(m).start()
            swap.dh(m).start()

        for m in range(MICRO):
            for move in (swap.og, swap.cos, swap.sin, swap.mask):
                move(m).wait_recv()
            swap.dy(m).start()
        start(0)
        feed(0)
        start(1)
        fed(0)
        swap.dy(0).wait_recv()
        hidden_back(R, 0)
        normed_back(R, swap, 0)
        feed(1)
        finish(0)
        fed(1)
        swap.dy(1).wait_recv()
        hidden_back(R, 1)
        normed_back(R, swap, 1)
        finish(1)

    wire.drain()

    def last(body):
        return lambda: only(0)(body)

    rest_early = [last(lambda x=x: normed_piece(R, 1, x)) for x in range(4)]
    rest_early.append(last(lambda: normed_sent(R, swap, 1)))

    def dh_done():
        stream_back(R, 1)
        R.dh[...] = R.dhs[...]

    rest_middle = [last(lambda: middle_back(R, swap, 1))]
    rest_late = [
        last(lambda: attend_back(R, tables, 1, range(0, 4))),
        last(lambda: attend_back(R, tables, 1, range(4, 7))),
        last(dh_done),
    ]
    made = set()
    start_scatter(wire, place, bufs, rest[:N_RS_SCRATCH], made, lambda *a: keep(R, *a))
    wire.add(weight_grads(R, wire, made, (rest_early, rest_middle, rest_late), far_first(place, "x")))
    wire.run()
    wire.drain()
    for m in range(MICRO):
        swap.n2(m).wait_send()
        swap.dy(m).wait_send()

    @only(0)
    def _():
        for m in range(MICRO):
            swap.hop_h(m).wait_send()

    @only(1)
    def _():
        for m in range(MICRO):
            for move in (swap.og, swap.cos, swap.sin, swap.mask, swap.y, swap.dh, swap.hop_dy):
                move(m).wait_send()
            swap.y(m).wait_recv()
            swap.dh(m).wait_recv()


N_WIRE = 208


def run_layers(ins):
    outs = [(TOK, D)] * 2 + [(2, 16, FF)] * 2 + [(80, D), (16, QKV), (16, D)]
    kinds = [BF] * 7
    vmem = pl.BlockSpec(memory_space=pltpu.VMEM)
    dma = pltpu.SemaphoreType.DMA
    return pl.pallas_call(
        layers_kernel,
        out_shape=[jax.ShapeDtypeStruct(s, k) for s, k in zip(outs, kinds)],
        in_specs=[pl.BlockSpec(memory_space=pl.ANY) if n in IN_HBM else vmem for n in INS],
        out_specs=[vmem] * len(OUTS),
        scratch_shapes=[pltpu.VMEM(s, BF) for s in bufs_shapes()]
        + [pltpu.VMEM(s, k) for _, s, k in LOCAL]
        + rs_scratch()
        + [dma((N_WIRE,)), dma((N_WIRE,)), dma((9,)), dma((N_SWAP,)), dma((N_SWAP,))],
        compiler_params=pltpu.CompilerParams(
            collective_id=0, has_side_effects=True, vmem_limit_bytes=127 * 2**19
        ),
        name="two_layers",
    )(*ins)


def rope_tables(segment_row, head_size):
    length = segment_row.shape[0]
    places = jnp.arange(length, dtype=jnp.int32)
    changes = jnp.concatenate(
        [jnp.ones((1,), jnp.int32), (segment_row[1:] != segment_row[:-1]).astype(jnp.int32)]
    )
    starts = lax.cummax(places * changes, axis=0)
    offsets = (places - starts).astype(F32)
    ladder = jnp.arange(head_size // 2, dtype=F32) * (-2.0 * math.log(rope_base) / head_size)
    angles = offsets[:, None] * jnp.exp(ladder)[None, :]
    cos, sin = jnp.cos(angles), jnp.sin(angles)
    return (
        jnp.concatenate([cos, cos, cos, cos], axis=-1),
        jnp.concatenate([-sin, sin, -sin, sin], axis=-1),
    )


def mask_of(segment_row):
    places = jnp.arange(segment_row.shape[0], dtype=jnp.int32)
    seen = (segment_row[:, None] == segment_row[None, :]) & (places[None, :] <= places[:, None])
    return jnp.where(seen, 0.0, -1e30).astype(F32)


def shards(
    tokens_in, out_grad, segments, norm1_gain, qkv_weight, qkv_bias, out_weight, norm2_gain,
    gate_weight, up_weight, down_weight,
):
    half = MICRO * SEQ
    rows = segments[:, 0]
    cos, sin = jax.vmap(rope_tables, in_axes=(0, None))(rows, HEAD_DIM)
    parts = run_layers([
        gate_weight[0],
        up_weight[0],
        down_weight[0],
        qkv_weight[0],
        out_weight[0],
        norm1_gain,
        qkv_bias,
        norm2_gain,
        tokens_in.reshape(half, D),
        out_grad.reshape(half, D),
        cos.reshape(half, 128),
        sin.reshape(half, 128),
        jax.vmap(mask_of)(rows),
        *constants(),
    ])
    shape = (1, MICRO, 1, SEQ, D)
    y, dh, a, q, b, o, c, g, u, d = finish_grads(parts)
    q, o, g, u, d = [part.transpose(1, 0, 2) for part in (q, o, g, u, d)]
    return y.reshape(shape), dh.reshape(shape), a, q, b, o, c, g, u, d


def solution(mesh):
    in_specs = (
        P(None, "fsdp", None, None),
        P(None, "fsdp", None, None),
        P(None, "fsdp", None),
        P("section", "fsdp"),
        P("section", "fsdp", None),
        P("section", "fsdp"),
        P("section", "fsdp", None),
        P("section", "fsdp"),
        P("section", "fsdp", None),
        P("section", "fsdp", None),
        P("section", "fsdp", None),
    )
    out_specs = (
        P("section", None, "fsdp", None, None),
        P("section", None, "fsdp", None, None),
        P("section", "fsdp"),
        P("section", "fsdp", None),
        P("section", "fsdp"),
        P("section", "fsdp", None),
        P("section", "fsdp"),
        P("section", "fsdp", None),
        P("section", "fsdp", None),
        P("section", "fsdp", None),
    )
    return jax.shard_map(shards, mesh=mesh, in_specs=in_specs, out_specs=out_specs, check_vma=False)
```

```python
import math
from types import SimpleNamespace

import jax
import jax.numpy as jnp
from jax import lax
from jax.experimental import pallas as pl
from jax.experimental.pallas import tpu as pltpu
from jax.sharding import PartitionSpec as P
import numpy as np

HEADS = 14
KV_HEADS = 2
HEAD_DIM = 64
MICRO = 2
SEQ = 128
D = 896
DP = 1024
QKV = 1152
norm_epsilon = 1e-06
rope_base = 1000000.0

MESH = pl.DeviceIdType.MESH
BF = jnp.bfloat16
F32 = jnp.float32


class Peer:
    def __init__(self, id, link):
        self.id, self.link = id, link


class Place:
    def __init__(self):
        f = lax.axis_index("fsdp")
        self.s = lax.axis_index("section")
        self.c = lax.rem(f, 2)
        self.z = lax.rem(f // 2, 4)
        self.y = lax.rem(f // 8, 2)
        self.x = f // 16

    def at(self, s=None, x=None, y=None, z=None, c=None):
        s = self.s if s is None else s
        x = self.x if x is None else x
        y = self.y if y is None else y
        z = self.z if z is None else z
        c = self.c if c is None else c
        return (s, ((x * 2 + y) * 4 + z) * 2 + c)

    def step(self, axis, k):
        here = self.x if axis == "x" else self.z
        return lax.rem(here + (k + 4), 4)

    def to(self, axis, k):
        return Peer(self.at(**{axis: self.step(axis, k)}), (axis, k))

    def across(self):
        return Peer(self.at(y=1 - self.y), "y")

    def mate(self):
        return Peer(self.at(c=1 - self.c), "mate")

    def beyond(self):
        return Peer(self.at(s=1 - self.s, y=1 - self.y), "section")


def greet(place):
    barrier = pltpu.get_barrier_semaphore()
    near = (
        place.to("x", 1), place.to("x", -1), place.to("z", 1), place.to("z", -1),
        place.across(), place.mate(), place.beyond(),
    )
    for peer in near:
        pl.semaphore_signal(barrier, inc=1, device_id=peer.id, device_id_type=MESH)
    pl.semaphore_wait(barrier, len(near))


RATE = {"mate": 150e3}
LINK_RATE = 48e3
LATENCY = 1.5


class Wire:
    def __init__(self, send_sems, recv_sems):
        self.send_sems, self.recv_sems = send_sems, recv_sems
        self.count, self.started, self.flows = 0, [], []
        self.now, self.free = 0.0, {}

    def send(self, src, dst, peer):
        k = self.count
        self.count += 1
        assert k < self.send_sems.shape[0]
        copy = pltpu.make_async_remote_copy(
            src_ref=src, dst_ref=dst, send_sem=self.send_sems.at[k],
            recv_sem=self.recv_sems.at[k], device_id=peer.id, device_id_type=MESH,
        )
        copy.start()
        self.started.append(copy)
        size = 2 * math.prod(dst.shape)
        begin = max(self.now, self.free.get(peer.link, 0.0))
        self.free[peer.link] = begin + size / RATE.get(peer.link, LINK_RATE)
        copy.there = self.free[peer.link] + LATENCY
        return copy

    def drain(self):
        for copy in self.started:
            copy.wait_send()
        self.started = []

    def add(self, flow):
        self.flows.append([None, flow])
        self.go_on(self.flows[-1])

    def go_on(self, entry):
        try:
            entry[0] = next(entry[1])
        except StopIteration:
            self.flows.remove(entry)

    def run(self):
        while self.flows:
            times = [(entry[0](), k) for k, entry in enumerate(self.flows)]
            when, k = min((t, k) for t, k in times if t is not None)
            self.now = max(self.now, when)
            self.go_on(self.flows[k])

    def busy(self, us):
        self.now += us


def got(*copies):
    yield lambda: max(copy.there for copy in copies)
    for copy in copies:
        copy.wait_recv()


def until(condition):
    yield lambda: 0.0 if condition() else None


def ring(wire, place, axis, piece, spawn):
    me = place.x if axis == "x" else place.z
    before, after, far = place.step(axis, -1), place.step(axis, 1), place.step(axis, 2)
    r = wire.send(piece(me), piece(me), place.to(axis, 1))
    l = wire.send(piece(me), piece(me), place.to(axis, -1))
    last = []

    def right():
        yield from got(r)
        last.append(wire.send(piece(before, 0), piece(before, 0), place.to(axis, 1)))
        spawn(before)

    def left():
        yield from got(l)
        last.append(wire.send(piece(after, 1), piece(after, 1), place.to(axis, -1)))
        spawn(after)

    def rest():
        yield from until(lambda: len(last) == 2)
        yield from got(*last)
        spawn(far)

    for flow in (right(), left(), rest()):
        wire.add(flow)


def gather_yab(wire, place, slot, first, last, finished, clear=lambda: True):
    x, y, z = place.x, place.y, place.z
    cross = wire.send(slot(x, y, z), slot(x, y, z), place.across())
    yield from got(cross)
    mine = {"x": x, "z": z}
    count = []

    def piece(a, b, half=None):
        return slot(b, half, a) if first == "z" else slot(a, half, b)

    def arrived(b):
        count.append(b)
        if len(count) == 16:
            finished()

    def along_last(a):
        arrived(a)

        def go():
            yield from until(clear)
            ring(wire, place, last, lambda b, half=None: piece(a, b, half), arrived)

        wire.add(go())

    ring(wire, place, first, lambda a, half=None: piece(a, mine[last], half), along_last)
    along_last(mine[first])


def gather_down(wire, place, D, finished):
    x, y, z = place.x, place.y, place.z
    count = []

    def by_x(a, half=None):
        if half is None:
            return D.at[a, y, z]
        return D.at[a, y, z, pl.ds(0, 48) if half == 0 else pl.ds(48, 32)]

    def by_z(b, half=None):
        if half is None:
            return D.at[:, y, b]
        return D.at[pl.ds(2 * half, 2), y, b]

    def along_y(b):
        cross = wire.send(by_z(b), by_z(b), place.across())

        def arrival():
            yield from got(cross)
            count.append(b)
            if len(count) == 4:
                finished()

        wire.add(arrival())

    def x_done(a):
        seen.append(a)
        if len(seen) == 3:
            ring(wire, place, "z", by_z, along_y)
            along_y(z)

    seen = []
    ring(wire, place, "x", by_x, x_done)


BLOCK = dict(G=(32, 2560), U=(32, 2560), D=(80, 896), Q=(32, 1152), O=(32, 896))


CLEAR = {"Q", "O"}


def start_gather(wire, place, ins, bufs, local_sems, done, pack):
    x, y, z, c = place.x, place.y, place.z, place.c
    rows = pl.ds(pl.multiple_of(c * 16, 16), 16)
    G, U, D, Q, O = bufs
    g_in, u_in, d_in, q_in, o_in = ins
    own, filled = {}, set()

    def place_own(name, k, src, dst):
        pack(name)
        own[name] = pltpu.make_async_copy(src, dst, local_sems.at[k])
        own[name].start()

    def whole(buf):
        def slot(px, half, pz):
            if half is None:
                return buf.at[px, :, pz]
            return buf.at[px, half, pz]
        return slot

    def part(buf):
        def slot(px, half, pz):
            if half is None:
                return buf.at[px, :, pz, rows]
            return buf.at[px, half, pz, rows]
        return slot

    def attention(name, buf):
        own[name].wait()
        yield from gather_yab(wire, place, part(buf), "z", "x", lambda: filled.add(name))
        yield from until(lambda: name in filled)
        mine = buf.at[:, :, :, rows]
        swap = wire.send(mine, mine, place.mate())
        yield from got(swap)
        done.add(name)

    def hidden(name, buf, swap, first, last):
        yield from got(swap)
        own[name].wait()
        clear = (lambda: CLEAR <= filled) if name == "G" else lambda: True
        yield from gather_yab(wire, place, whole(buf), first, last, lambda: done.add(name), clear)

    place_own("Q", 0, q_in, Q.at[x, y, z, rows])
    wire.add(attention("Q", Q))
    place_own("O", 1, o_in, O.at[x, y, z, rows])
    wire.add(attention("O", O))
    place_own("D", 2, d_in, D.at[x, y, z])
    own["D"].wait()
    gather_down(wire, place, D, lambda: done.add("D"))
    for name, k, src, dst, first, last in (("G", 3, g_in, G, "z", "x"), ("U", 4, u_in, U, "x", "z")):
        place_own(name, k, src.at[c], dst.at[x, y, z, rows])
        swap = wire.send(src.at[1 - c], dst.at[x, y, z, rows], place.mate())
        wire.add(hidden(name, dst, swap, first, last))


def bufs_shapes():
    return [(4, 2, 4) + BLOCK[k] for k in "GUDQO"]


def add(dst, *srcs):
    total = dst[...]
    for src in srcs:
        total = total + src[...]
    dst[...] = total


def add_each(count, dst, *srcs):
    def body(i, carry):
        add(dst(i), *[src(i) for src in srcs])
        return carry
    lax.fori_loop(0, count, body, 0)


def scatter_ring(wire, place, axis, piece, land, halves, finished):
    me = place.x if axis == "x" else place.z
    before, after, far = place.step(axis, -1), place.step(axis, 1), place.step(axis, 2)
    l1a, l1b, l2a, l2b = land
    r = wire.send(piece(far, 0), l1a, place.to(axis, 1))
    l = wire.send(piece(far, 1), l1b, place.to(axis, -1))
    last = []

    def right():
        yield from got(r)
        add(piece(after, 0), l1a)
        last.append(wire.send(piece(after), l2a, place.to(axis, 1)))

    def left():
        yield from got(l)
        add(piece(before, 1), l1b)
        last.append(wire.send(piece(before), l2b, place.to(axis, -1)))

    def rest():
        yield from until(lambda: len(last) == 2)
        yield from got(*last)
        halves(lambda i: piece(me, i), l2a, l2b)
        finished()

    for flow in (right(), left(), rest()):
        wire.add(flow)


def two_halves(dst, a, b):
    for i in range(2):
        add(dst(i), a.at[i], b.at[i])


def far_first(place, axis):
    me = place.x if axis == "x" else place.z
    return [place.step(axis, k) for k in (2, 1, -1)] + [me]


def scatter_aby(wire, place, slot, R, first, last, have=lambda k: True):
    r1a, r1b, r2a, r2b, s1a, s1b, s2a, s2b, t_buf = R
    mine = {"x": place.x, "z": place.z}

    def piece(a, b, half=None):
        return slot(b, half, a) if first == "z" else slot(a, half, b)

    order = far_first(place, last)
    filled = []

    def start(k, b):
        yield from until(lambda: have(k))
        scatter_ring(
            wire, place, first, lambda a, half=None: piece(a, b, half),
            (r1a.at[k], r1b.at[k], r2a.at[k], r2b.at[k]), two_halves, lambda: filled.append(k),
        )

    for k, b in enumerate(order):
        wire.add(start(k, b))
    a0 = mine[first]
    bq, bp, bm, b0 = order
    sent = []

    def outer():
        yield from until(lambda: 0 in filled)
        d_r = wire.send(piece(a0, bq, 0), s1a, place.to(last, 1))
        d_l = wire.send(piece(a0, bq, 1), s1b, place.to(last, -1))

        def right():
            yield from until(lambda: 1 in filled)
            yield from got(d_r)
            add(piece(a0, bp, 0), s1a)
            sent.append(wire.send(piece(a0, bp), s2a, place.to(last, 1)))

        def left():
            yield from until(lambda: 2 in filled)
            yield from got(d_l)
            add(piece(a0, bm, 1), s1b)
            sent.append(wire.send(piece(a0, bm), s2b, place.to(last, -1)))

        wire.add(right())
        wire.add(left())

    wire.add(outer())
    yield from until(lambda: len(sent) == 2 and 3 in filled)
    yield from got(*sent)
    two_halves(lambda i: piece(a0, b0, i), s2a, s2b)
    cross = wire.send(slot(place.x, 1 - place.y, place.z), t_buf, place.across())
    yield from got(cross)
    add(slot(place.x, place.y, place.z), t_buf)


def scatter_down(wire, place, D, R):
    yb, z1a, z1b, z2a, z2b, xa, xb, x2a, x2b = R
    x, y, z = place.x, place.y, place.z
    zp, zm, zq = place.step("z", 1), place.step("z", -1), place.step("z", 2)
    order = (zq, zp, zm, z)
    crossing = [wire.send(D.at[:, 1 - y, b], yb.at[k], place.across()) for k, b in enumerate(order)]
    sent = []

    def settle(k):
        yield from got(crossing[k])
        add_each(4, lambda i: D.at[i, y, order[k]], lambda i: yb.at[k, i])

    yield from settle(0)
    d_r = wire.send(D.at[pl.ds(0, 2), y, zq], z1a, place.to("z", 1))
    d_l = wire.send(D.at[pl.ds(2, 2), y, zq], z1b, place.to("z", -1))

    def right():
        yield from settle(1)
        yield from got(d_r)
        add_each(2, lambda i: D.at[i, y, zp], lambda i: z1a.at[i])
        sent.append(wire.send(D.at[:, y, zp], z2a, place.to("z", 1)))

    def left():
        yield from settle(2)
        yield from got(d_l)
        add_each(2, lambda i: D.at[i + 2, y, zm], lambda i: z1b.at[i])
        sent.append(wire.send(D.at[:, y, zm], z2b, place.to("z", -1)))

    wire.add(right())
    wire.add(left())
    yield from settle(3)
    yield from until(lambda: len(sent) == 2)
    yield from got(*sent)
    add_each(4, lambda i: D.at[i, y, z], lambda i: z2a.at[i], lambda i: z2b.at[i])

    def by_x(a, half=None):
        if half is None:
            return D.at[a, y, z]
        return D.at[a, y, z, pl.ds(0, 48) if half == 0 else pl.ds(48, 32)]

    ended = []
    scatter_ring(
        wire, place, "x", by_x, (xa, xb, x2a, x2b),
        lambda dst, a, b: add(D.at[x, y, z], a, b), lambda: ended.append(1),
    )
    yield from until(lambda: ended)


def rs_scratch():
    def aby(rows, cols):
        shapes = [(4, rows, cols)] * 2 + [(4, 2, rows, cols)] * 2 + [(rows, cols)] * 2 + [(2, rows, cols)] * 2 + [(rows, cols)]
        return [pltpu.VMEM(s, BF) for s in shapes]
    out = []
    out += aby(32, 2560) + [pltpu.VMEM((16, 2560), BF)]
    out += aby(32, 2560) + [pltpu.VMEM((16, 2560), BF)]
    b = (80, 896)
    out += [pltpu.VMEM(s, BF) for s in (
        (4, 4) + b, (2,) + b, (2,) + b, (4,) + b, (4,) + b, (48, 896), (32, 896), b, b)]
    out += aby(16, 1152) + [pltpu.VMEM((4, 2, 4, 16, 1152), BF)]
    out += aby(16, 896) + [pltpu.VMEM((4, 2, 4, 16, 896), BF)]
    return out


N_RS_SCRATCH = 10 + 10 + 9 + 10 + 10


def start_scatter(wire, place, bufs, R, made, end):
    x, y, z, c = place.x, place.y, place.z, place.c
    G, U, D, Q, O = bufs
    rg, ru, rd, rq, ro = R[:10], R[10:20], R[20:29], R[29:39], R[39:49]
    rows = pl.ds(pl.multiple_of(c * 16, 16), 16)
    others = pl.ds(pl.multiple_of(16 - c * 16, 16), 16)

    def whole(buf):
        def slot(px, half, pz):
            return buf.at[px, :, pz] if half is None else buf.at[px, half, pz]
        return slot

    def part(buf):
        def slot(px, half, pz):
            return buf.at[px, :, pz, rows] if half is None else buf.at[px, half, pz, rows]
        return slot

    def hidden(name, buf, r, first, last):
        if name == "G":
            yield from until(lambda: name in made)
            have = lambda k: True
        else:
            have = lambda k: name + str(k) in made
        yield from scatter_aby(wire, place, whole(buf), r[:9], first, last, have)
        swap = wire.send(buf.at[x, y, z, others], r[9], place.mate())
        yield from got(swap)
        end(name, c, buf[x, y, z, rows], r[9][...])

    def attention(name, buf, r):
        yield from until(lambda: name in made)
        swap = wire.send(buf.at[:, :, :, others], r[9], place.mate())
        yield from got(swap)
        add_each(32, lambda i: buf.at[i // 8, lax.rem(i // 4, 2), lax.rem(i, 4), rows],
                 lambda i: r[9].at[i // 8, lax.rem(i // 4, 2), lax.rem(i, 4)])
        yield from scatter_aby(wire, place, part(buf), r[:9], "x", "z")
        end(name, c, buf[x, y, z, rows])

    def down():
        yield from until(lambda: "D" in made)
        yield from scatter_down(wire, place, D, rd)
        end("D", c, D[x, y, z])

    wire.add(down())
    wire.add(hidden("G", G, rg, "x", "z"))
    wire.add(hidden("U", U, ru, "z", "x"))
    wire.add(attention("O", O, ro))
    wire.add(attention("Q", Q, rq))


TOK = 256
FF = 2560


def mm(a, b):
    return jnp.dot(a, b, preferred_element_type=F32)


def mm_t(a, b):
    return lax.dot_general(a, b, (((1,), (1,)), ((), ())), preferred_element_type=F32)


def t_mm(a, b):
    return lax.dot_general(a, b, (((0,), (0,)), ((), ())), preferred_element_type=F32)


def constants():
    d = np.arange(D)
    spread = np.zeros((D, DP), np.float32)
    spread[d, 16 * (d // 14) + d % 14] = 1
    pick = np.zeros((64, DP), np.float32)
    pick[np.arange(64), 16 * np.arange(64) + 14] = 1
    own14 = (np.arange(64)[:, None] == d[None] // 14).astype(np.float32)
    j = np.arange(QKV)
    own18 = (np.arange(64)[:, None] == j[None] // 18).astype(np.float32)
    lane = np.arange(128)[:, None]
    e1 = (lane == d[None] % 14).astype(np.float32)
    eb = (lane == 64 + j[None] % 18).astype(np.float32)
    return [jnp.asarray(a, BF) for a in (spread, pick, own14, own18, e1, eb)]


CONST = ("spread", "pick", "own14", "own18", "e1", "eb")


def cols(buf, start, size):
    value = buf[:, :, :, :, pl.ds(start, size)]
    return value.reshape(-1, size)


def put(ref, value):
    ref[...] = value.reshape(ref.shape)


def rotate(x, lo32):
    return jnp.where(lo32, pltpu.roll(x, 96, 1), pltpu.roll(x, 32, 1))


def lane_is(shape, width, below):
    lane = lax.broadcasted_iota(jnp.int32, shape, 1)
    return lax.rem(lane, width) < below


def gains(R):
    q = cols(R.Q, 0, 128)
    s = mm(R.pick[...], q)
    s2 = pltpu.roll(s, 96, 1).astype(BF)
    s = s.astype(BF)
    R.g1[...] = jnp.sum(mm(s, R.e1[...]) * R.own14[...].astype(F32), axis=0, keepdims=True)
    R.g2[...] = jnp.sum(mm(s2, R.e1[...]) * R.own14[...].astype(F32), axis=0, keepdims=True)
    R.bias[...] = jnp.sum(mm(s, R.eb[...]) * R.own18[...].astype(F32), axis=0, keepdims=True)


def inverse_rms(h):
    return lax.rsqrt(jnp.sum(h * h, axis=-1, keepdims=True) * (1.0 / D) + norm_epsilon)


def project_qkv(R, source, tables, rows, size):
    h = source[rows].astype(F32)
    n1 = (h * inverse_rms(h) * R.g1[...]).astype(BF)
    R.N1[rows] = mm(n1, R.spread[...]).astype(BF)
    lo32 = lane_is((size, 128), 64, 32)
    lo = lane_is((size, 128), 128, 64)
    cos, sin = tables[0][rows], tables[1][rows]
    for start, width in ((0, 256), (256, 256), (512, 256), (768, 256), (1024, 128)):
        out = mm(R.N1[rows], cols(R.Q, start, width)) + R.bias[:, start:start + width]
        for k in range(width // 128):
            x = out[:, 128 * k:128 * k + 128]
            tile = (start + 128 * k) // 128
            if tile < 8:
                x = x * cos + rotate(x, lo32) * sin
            if tile < 7:
                R.QR[rows, 128 * tile:128 * tile + 128] = x.astype(BF)
            else:
                x = x.astype(BF).astype(F32)
                swapped = pltpu.roll(x, 64, 1)
                R.KV[tile - 7, 0, rows] = jnp.where(lo, x, swapped).astype(BF)
                R.KV[tile - 7, 1, rows] = x.astype(BF)
                R.KV[tile - 7, 2, rows] = jnp.where(lo, swapped, x).astype(BF)


def two_heads(R, tile):
    return jnp.concatenate([tile * R.lanes[0], tile * R.lanes[1]], axis=0)


def beside(x):
    return jnp.concatenate([x[:SEQ], x[SEQ:]], axis=1)


def variant_of(t):
    return 0 if t < 3 else (2 if t > 3 else 1)


def probs_of(R, mask, t, rows):
    q2 = two_heads(R, R.QR[rows, 128 * t:128 * t + 128])
    kk = R.KV[0, variant_of(t), rows]
    s = mm_t(q2, kk) * 0.125 + jnp.concatenate([mask, mask], axis=0)
    e = jnp.exp(s - jnp.max(s, axis=-1, keepdims=True))
    p = e * (1.0 / jnp.sum(e, axis=-1, keepdims=True))
    return q2, kk, p


def attend(R, tables, m):
    rows = own_rows(m)
    mask = tables[2][m]
    for t in range(7):
        _, _, p = probs_of(R, mask, t, rows)
        vv = two_heads(R, R.KV[1, variant_of(t), rows])
        R.DQKV[rows, 128 * t:128 * t + 128] = mm(beside(p.astype(BF)), vv).astype(BF)


def own_rows(m):
    return pl.ds(SEQ * m, SEQ)


def pair_own(m):
    return pl.ds(2 * SEQ * m, SEQ)


def pair_other(m):
    return pl.ds(2 * SEQ * m + SEQ, SEQ)


def pair(m):
    return pl.ds(2 * SEQ * m, 2 * SEQ)


def after_attention(R, source, m):
    rows = own_rows(m)
    R.CP[rows] = mm(R.DQKV[rows, :D], R.spread[...]).astype(BF)
    mid = source[rows].astype(F32) + mm(R.CP[rows], cols(R.O, 0, D))
    R.MID[rows] = mid
    n2 = (mid * inverse_rms(mid) * R.g2[...]).astype(BF)
    R.N2[pair_own(m)] = mm(n2, R.spread[...]).astype(BF)


def sigmoid(v):
    return 0.5 * jnp.tanh(0.5 * v) + 0.5


def hidden(R, rows):
    def body(j, carry):
        at = pl.ds(pl.multiple_of(j * 1280, 1280), 1280)
        n2 = R.N2[rows]
        gate = mm(n2, R.G[:, :, :, :, at].reshape(DP, 1280))
        up = mm(n2, R.U[:, :, :, :, at].reshape(DP, 1280))
        R.GA[rows, at] = gate.astype(BF)
        R.UP[rows, at] = up.astype(BF)
        R.ACT[rows, at] = (gate * sigmoid(gate) * up).astype(BF)
        return carry

    lax.fori_loop(0, FF // 1280, body, 0)


def hidden_other(R, swap, m):
    swap.n2(m).wait_recv()
    hidden(R, pair_other(m))


class Swap:
    def __init__(self, R, place):
        own = own_rows
        mate, across, beyond = place.mate(), place.across(), place.beyond()

        def table(k, refs, device):
            return lambda m: pltpu.make_async_remote_copy(
                src_ref=refs(m)[0], dst_ref=refs(m)[1], send_sem=R.xs.at[2 * k + m],
                recv_sem=R.xr.at[2 * k + m], device_id=device.id, device_id_type=MESH,
            )

        self.n2 = table(0, lambda m: (R.N2.at[pair_own(m)], R.N2.at[pair_other(m)]), mate)
        self.part = table(1, lambda m: (R.DB.at[own(m)], R.DC.at[own(m)]), mate)
        self.dy = table(2, lambda m: (R.DY.at[pair_own(m)], R.DY.at[pair_other(m)]), mate)
        self.dn = table(3, lambda m: (R.dn, R.dn_in.at[own(m)]), mate)
        self.hop_h = table(4, lambda m: (R.ys.at[own(m)], R.h.at[own(m)]), beyond)
        self.hop_dy = table(5, lambda m: (R.dhs.at[own(m)], R.DY.at[pair_own(m)]), beyond)
        self.og = table(6, lambda m: (R.og.at[own(m)], R.DY.at[pair_own(m)]), across)
        self.cos = table(7, lambda m: (R.cos.at[own(m)], R.tcos.at[own(m)]), across)
        self.sin = table(8, lambda m: (R.sin.at[own(m)], R.tsin.at[own(m)]), across)
        self.mask = table(9, lambda m: (R.mask.at[m], R.tmask.at[m]), across)
        self.y = table(10, lambda m: (R.ys.at[own(m)], R.y.at[own(m)]), across)
        self.dh = table(11, lambda m: (R.dhs.at[own(m)], R.dh.at[own(m)]), across)


N_SWAP = 24


def down_sent(R, swap, m):
    R.DB[own_rows(m)] = mm(R.ACT[pair_other(m)], R.D[...].reshape(FF, D)).astype(BF)
    swap.part(m).start()
    R.acc[SEQ:, 0:D] = R.MID[own_rows(m)] + mm(R.ACT[pair_own(m)], R.D[...].reshape(FF, D))


def down_done(R, swap, m):
    swap.part(m).wait_recv()
    R.ys[own_rows(m)] = (R.acc[SEQ:, 0:D] + R.DC[own_rows(m)].astype(F32)).astype(BF)
    swap.part(m).wait_send()


def hidden_back(R, m):
    rows = pair(m)

    def body(j, carry):
        down = R.D[j].reshape(640, D)
        for start, size in ((0, 256), (256, 256), (512, 128)):
            sub = pl.ds(pl.multiple_of(j * 640 + start, 128), size)
            dact = mm_t(R.DY[rows], down[start:start + size])
            gate = R.GA[rows, sub].astype(F32)
            up = R.UP[rows, sub].astype(F32)
            sig = sigmoid(gate)
            R.GA[rows, sub] = (dact * up * sig * (1.0 + gate * (1.0 - sig))).astype(BF)
            R.UP[rows, sub] = (dact * gate * sig).astype(BF)
        return carry

    lax.fori_loop(0, FF // 640, body, 0)


def normed_piece(R, m, x):
    rows = pair(m)
    at = pl.ds(pl.multiple_of(x * 256, 256), 256)
    R.acc[:, at] = mm_t(R.GA[rows], R.G[x].reshape(256, FF)) + mm_t(R.UP[rows], R.U[x].reshape(256, FF))


def normed_sent(R, swap, m):
    R.dn[...] = R.acc[SEQ:].astype(BF)
    swap.dn(m).start()


def normed_back(R, swap, m):
    def body(x, carry):
        normed_piece(R, m, x)
        return carry

    lax.fori_loop(0, 4, body, 0)
    normed_sent(R, swap, m)


def middle_back(R, swap, m):
    rows = own_rows(m)
    swap.dn(m).wait_recv()
    dn2p = (R.acc[:SEQ] + R.dn_in[rows].astype(F32)).astype(BF)
    dn2 = mm_t(dn2p, R.spread[...])
    mid = R.MID[rows]
    inv2 = inverse_rms(mid)
    R.dg2[m] = jnp.sum(dn2 * mid * inv2, axis=0, keepdims=True)
    scaled = dn2 * R.g2[...]
    mean = jnp.sum(scaled * mid, axis=-1, keepdims=True) * (1.0 / D)
    dmid = R.DY[pair_own(m)].astype(F32) + inv2 * scaled - mid * (inv2 * inv2 * inv2 * mean)
    R.MID[rows] = dmid
    R.DB[rows] = dmid.astype(BF)
    dctx = mm_t(R.DB[rows], cols(R.O, 0, D)).astype(BF)
    R.DC[rows] = mm_t(dctx, R.spread[...]).astype(BF)
    swap.dn(m).wait_send()


def attend_back(R, tables, m, tiles=range(7)):
    rows = own_rows(m)
    cos, sin, mask = tables[0][rows], tables[1][rows], tables[2][m]
    lo32 = lane_is((SEQ, 128), 64, 32)
    lo = lane_is((SEQ, 128), 128, 64)

    def spin_back(g):
        return g * cos + rotate(g * sin, lo32)

    for t in tiles:
        q2, kk, p = probs_of(R, mask, t, rows)
        var = variant_of(t)
        dc2 = two_heads(R, R.DC[rows, 128 * t:128 * t + 128])
        dp = mm_t(dc2, R.KV[1, var, rows])
        ds = (p * (dp - jnp.sum(p * dp, axis=-1, keepdims=True))).astype(BF)
        dk, dv = t_mm(ds, q2), t_mm(p.astype(BF), dc2)
        if t in (0, 3, 4):
            R.dkv[0, var] = dk
            R.dkv[1, var] = dv
        else:
            R.dkv[0, var] += dk
            R.dkv[1, var] += dv
        dq = mm(beside(ds), two_heads(R, kk)) * 0.125
        R.DQKV[rows, 128 * t:128 * t + 128] = spin_back(dq).astype(BF)

    if 6 not in tiles:
        return

    def joined(k):
        first, mixed, last = R.dkv[k, 0], R.dkv[k, 1], R.dkv[k, 2]
        return mixed + jnp.where(
            lo, first + pltpu.roll(first, 64, 1), last + pltpu.roll(last, 64, 1)
        )

    R.DQKV[rows, 896:1024] = spin_back(joined(0) * 0.125).astype(BF)
    R.DQKV[rows, 1024:1152] = joined(1).astype(BF)


def stream_back(R, m):
    rows = own_rows(m)
    dqkv = R.DQKV[rows]
    R.dbias[m] = jnp.sum(dqkv.astype(F32), axis=0, keepdims=True)
    dn1 = mm_t(mm_t(dqkv, cols(R.Q, 0, QKV)).astype(BF), R.spread[...])
    h = R.h[rows].astype(F32)
    inv1 = inverse_rms(h)
    R.dg1[m] = jnp.sum(dn1 * h * inv1, axis=0, keepdims=True)
    scaled = dn1 * R.g1[...]
    mean = jnp.sum(scaled * h, axis=-1, keepdims=True) * (1.0 / D)
    R.dhs[rows] = (R.MID[rows] + inv1 * scaled - h * (inv1 * inv1 * inv1 * mean)).astype(BF)


def pause(wire):
    now = wire.now
    yield lambda: now


ORDER = ("N", "U0", "G", "U1", "U2", "U3", "D", "M", "O", "R", "Q")


def weight_grads(R, wire, done, rest, slabs):
    def step(us, body):
        body()
        wire.busy(us)
        yield from pause(wire)

    def down(x):
        at = pl.ds(640 * x, 640)
        for start, size in ((0, 512), (512, 384)):
            grad = t_mm(R.ACT[:, at], R.DY[:, start:start + size])
            put(R.D.at[x, :, :, :, pl.ds(start, size)], grad.astype(BF))

    def wide(buf, grad, x):
        n2 = R.N2[:, pl.ds(pl.multiple_of(x * 256, 256), 256)]
        for start in range(0, FF, 512):
            at = pl.ds(start, 512)
            put(buf.at[x, :, :, :, at], t_mm(n2, grad[:, at]).astype(BF))

    def out_rows(x):
        rows = pl.ds(256 * x, 256)
        put(R.O.at[x], t_mm(R.CP[:, rows], R.DB[...]).astype(BF))

    def small_rows():
        small = (
            mm_t((R.own14[...].astype(F32) * (R.dg1[0] + R.dg1[1])).astype(BF), R.e1[...])
            + pltpu.roll(
                mm_t((R.own14[...].astype(F32) * (R.dg2[0] + R.dg2[1])).astype(BF), R.e1[...]), 32, 1
            )
            + mm_t((R.own18[...].astype(F32) * (R.dbias[0] + R.dbias[1])).astype(BF), R.eb[...])
        )
        R.small[...] = small.astype(BF)

    def qkv_rows(x):
        rows = pl.ds(256 * x, 256)
        n1 = R.N1[:, rows]
        for start in range(0, QKV, 384):
            g = t_mm(n1, R.DQKV[:, start:start + 384])
            if start == 0:
                g = jnp.concatenate([g[:, :128] + t_mm(R.pick[:, rows], R.small[...]), g[:, 128:]], axis=1)
            put(R.Q.at[x, :, :, :, pl.ds(start, 384)], g.astype(BF))

    early, middle, late = rest
    for name in ORDER:
        if name == "N":
            for piece in early:
                yield from step(0.9, piece)
        elif name == "M":
            for piece in middle:
                yield from step(2.3, piece)
        elif name == "R":
            for piece in late:
                yield from step(1.9, piece)
        elif name == "Q":
            yield from step(0.2, small_rows)
            for x in range(4):
                yield from step(0.4, lambda: qkv_rows(x))
        elif name == "O":
            for x in range(4):
                yield from step(0.3, lambda: out_rows(x))
        elif name == "D":
            for x in range(4):
                yield from step(0.75, lambda: down(x))
        elif name == "G":
            for x in range(4):
                yield from step(1.1, lambda: wide(R.G, R.GA, x))
        else:
            yield from step(1.1, lambda: wide(R.U, R.UP, slabs[int(name[1])]))
        done.add(name)


def pack(R, name):
    if name in "GU":
        src, dst = (R.g_in, R.g_st) if name == "G" else (R.u_in, R.u_st)
        R.g_s[...] = jnp.zeros_like(R.g_s)
        for f in range(64):
            piece = src[:, 76 * f:76 * f + 76].astype(F32)
            R.g_s[f % 2, 0:14, 80 * (f // 2):80 * (f // 2) + 76] = piece
        dst[...] = R.g_s[...].astype(BF)
    elif name == "D":
        R.acc[0:80, 0:D] = jnp.zeros((80, D), F32)
        R.acc[0:76, 0:D] = R.d_in[...].astype(F32)
        R.d_st[...] = R.acc[0:80, 0:D].astype(BF)
    elif name == "O":
        R.o_s[...] = jnp.zeros_like(R.o_s)
        R.o_s[0:14] = R.o_in[...].astype(F32)
        R.o_st[...] = R.o_s[...].astype(BF)
    else:
        R.q_s[...] = jnp.zeros_like(R.q_s)
        R.q_s[0:14] = R.q_in[...].astype(F32)
        R.q_s[14:15, 0:14] = R.a_in[...].astype(F32)
        R.q_s[14:15, 32:46] = R.c_in[...].astype(F32)
        R.q_s[14:15, 64:82] = R.b_in[...].astype(F32)
        R.q_st[...] = R.q_s[...].astype(BF)


def keep(R, name, c, mine, other=None):
    dst = getattr(R, name.lower() + "_o")
    if other is None:
        dst[...] = mine
    else:
        dst[c] = mine
        dst[1 - c] = other


def finish_kernel(
    y, dh, g_h, u_h, d_h, q_h, o_h, y_o, dh_o, a_o, q_o, b_o, o_o, c_o, g_o, u_o, d_o, g, u, d, q, o, wide, flat, sems
):
    moves = [
        pltpu.make_async_copy(src, dst, sems.at[k])
        for k, (src, dst) in enumerate(
            ((g_h, g), (u_h, u), (d_h, d), (q_h, q), (o_h, o), (y, y_o), (dh, dh_o))
        )
    ]
    for move in moves:
        move.start()
    for move in moves:
        move.wait()
    for src, dst in ((g, g_o), (u, u_o)):
        wide[...] = src[...].astype(F32)
        for f in range(64):
            at = 80 * (f // 2)
            flat[0:14, 76 * f:76 * f + 76] = wide[f % 2, 0:14, at:at + 76]
        for r in range(14):
            dst[r] = flat[r:r + 1, :]
    flat[0:80, 0:D] = d[...].astype(F32)
    for r in range(76):
        d_o[r] = flat[r:r + 1, 0:D]
    flat[0:16, 0:QKV] = q[...].astype(F32)
    for r in range(14):
        q_o[r] = flat[r:r + 1, 0:QKV]
    a_o[...] = flat[14:15, 0:14]
    c_o[...] = flat[14:15, 32:46]
    b_o[...] = flat[14:15, 64:82]
    flat[16:32, 0:D] = o[...].astype(F32)
    for r in range(14):
        o_o[r] = flat[16 + r:17 + r, 0:D]


def finish_grads(parts):
    shapes = [
        (TOK, D), (TOK, D), (1, 14), (14, 1, QKV), (1, 18), (14, 1, D), (1, 14),
        (14, 1, 4864), (14, 1, 4864), (76, 1, D),
    ]
    vmem = pl.BlockSpec(memory_space=pltpu.VMEM)
    return pl.pallas_call(
        finish_kernel,
        out_shape=[jax.ShapeDtypeStruct(s, BF if k < 2 else F32) for k, s in enumerate(shapes)],
        in_specs=[pl.BlockSpec(memory_space=pl.ANY)] * len(parts),
        out_specs=[vmem] * len(shapes),
        scratch_shapes=[pltpu.VMEM(part.shape, BF) for part in parts[2:]]
        + [pltpu.VMEM((2, 16, FF), F32), pltpu.VMEM((80, 4864), F32), pltpu.SemaphoreType.DMA((7,))],
        compiler_params=pltpu.CompilerParams(vmem_limit_bytes=127 * 2**19),
        name="finish_grads",
    )(*parts)


INS = ("g_in", "u_in", "d_in", "q_in", "o_in", "a_in", "b_in", "c_in", "tokens", "og", "cos", "sin", "mask") + CONST
IN_HBM = ("og", "tokens", "cos", "sin", "mask")
OUTS = ("y", "dh", "g_o", "u_o", "d_o", "q_o", "o_o")
LOCAL = (
    ("h", (TOK, D), BF), ("N1", (TOK, DP), BF), ("QR", (TOK, D), BF),
    ("KV", (2, 3, TOK, 128), BF), ("CP", (TOK, DP), BF),
    ("MID", (TOK, D), F32), ("N2", (2 * TOK, DP), BF), ("GA", (2 * TOK, FF), BF),
    ("UP", (2 * TOK, FF), BF), ("ACT", (2 * TOK, FF), BF), ("DY", (2 * TOK, D), BF), ("acc", (TOK, DP), F32), ("dn", (SEQ, DP), BF), ("dn_in", (TOK, DP), BF),
    ("DB", (TOK, D), BF), ("DC", (TOK, D), BF), ("DQKV", (TOK, QKV), BF),
    ("dkv", (2, 3, SEQ, 128), F32), ("lanes", (2, SEQ, 128), BF),
    ("small", (64, 128), BF),
    ("g1", (1, D), F32), ("g2", (1, D), F32), ("bias", (1, QKV), F32),
    ("dg1", (2, 1, D), F32), ("dg2", (2, 1, D), F32), ("dbias", (2, 1, QKV), F32),
    ("g_st", (2, 16, FF), BF), ("u_st", (2, 16, FF), BF), ("d_st", (80, D), BF),
    ("q_st", (16, QKV), BF), ("o_st", (16, D), BF), ("g_s", (2, 16, FF), F32),
    ("q_s", (16, QKV), F32), ("o_s", (16, D), F32),
    ("ys", (TOK, D), BF), ("dhs", (TOK, D), BF),
    ("tcos", (TOK, 128), F32), ("tsin", (TOK, 128), F32), ("tmask", (2, SEQ, SEQ), F32),
)


def layers_kernel(*refs):
    names = INS + OUTS + tuple("GUDQO") + tuple(name for name, _, _ in LOCAL)
    R = SimpleNamespace(**dict(zip(names, refs)))
    rest = refs[len(names):]
    R.ss, R.rs, R.ls, R.xs, R.xr = rest[N_RS_SCRATCH:]
    place = Place()
    greet(place)
    wire = Wire(R.ss, R.rs)
    swap = Swap(R, place)
    bufs = (R.G, R.U, R.D, R.Q, R.O)
    done = set()
    tables = (R.tcos, R.tsin, R.tmask)

    def only(section):
        return lambda body: pl.when(place.s == section)(body)

    own = [
        pltpu.make_async_copy(src, dst, R.ls.at[5 + k])
        for k, (src, dst) in enumerate(zip((R.tokens, R.cos, R.sin, R.mask), (R.h,) + tables))
    ]

    def early():
        yield from until(lambda: {"Q", "O"} <= done)

        @only(0)
        def _():
            for move in own:
                move.wait()

        gains(R)
        wire.busy(0.5)
        for m in range(MICRO):
            yield from pause(wire)
            only(0)(lambda: project_qkv(R, R.h, tables, own_rows(m), SEQ))
            wire.busy(1.2)
            yield from pause(wire)
            only(0)(lambda: attend(R, tables, m))
            wire.busy(1.3)
            yield from pause(wire)

            @only(0)
            def _():
                after_attention(R, R.h, m)
                swap.n2(m).start()

            wire.busy(1.5)

    start_gather(wire, place, (R.g_st, R.u_st, R.d_st, R.q_st, R.o_st), bufs, R.ls, done, lambda name: pack(R, name))
    @only(0)
    def _():
        for move in own:
            move.start()

    @only(1)
    def _():
        for m in range(MICRO):
            for move in (swap.og, swap.cos, swap.sin, swap.mask):
                move(m).start()

    lo = lane_is((SEQ, 128), 128, 64).astype(F32)
    R.lanes[0] = lo.astype(BF)
    R.lanes[1] = (1.0 - lo).astype(BF)
    wire.add(early())
    wire.run()

    @only(0)
    def _():
        hidden(R, pair_own(0))
        hidden_other(R, swap, 0)
        down_sent(R, swap, 0)
        hidden(R, pair_own(1))
        down_done(R, swap, 0)
        swap.hop_h(0).start()
        hidden_other(R, swap, 1)
        down_sent(R, swap, 1)
        down_done(R, swap, 1)
        swap.hop_h(1).start()
        R.y[...] = R.ys[...]
        swap.hop_dy(0).wait_recv()
        swap.dy(0).start()
        swap.dy(0).wait_recv()
        hidden_back(R, 0)
        normed_back(R, swap, 0)
        middle_back(R, swap, 0)
        attend_back(R, tables, 0)
        stream_back(R, 0)
        swap.hop_dy(1).wait_recv()
        swap.dy(1).start()
        swap.dy(1).wait_recv()
        hidden_back(R, 1)

    @only(1)
    def _():
        def start(m):
            swap.hop_h(m).wait_recv()
            rows = own_rows(m)
            project_qkv(R, R.h, tables, rows, SEQ)
            attend(R, tables, m)
            after_attention(R, R.h, m)
            swap.n2(m).start()

        def feed(m):
            hidden(R, pair_own(m))
            hidden_other(R, swap, m)
            down_sent(R, swap, m)

        def fed(m):
            down_done(R, swap, m)
            swap.y(m).start()

        def finish(m):
            middle_back(R, swap, m)
            attend_back(R, tables, m)
            stream_back(R, m)
            swap.hop_dy(m).start()
            swap.dh(m).start()

        for m in range(MICRO):
            for move in (swap.og, swap.cos, swap.sin, swap.mask):
                move(m).wait_recv()
            swap.dy(m).start()
        start(0)
        feed(0)
        start(1)
        fed(0)
        swap.dy(0).wait_recv()
        hidden_back(R, 0)
        normed_back(R, swap, 0)
        feed(1)
        finish(0)
        fed(1)
        swap.dy(1).wait_recv()
        hidden_back(R, 1)
        normed_back(R, swap, 1)
        finish(1)

    wire.drain()

    def last(body):
        return lambda: only(0)(body)

    rest_early = [last(lambda x=x: normed_piece(R, 1, x)) for x in range(4)]
    rest_early.append(last(lambda: normed_sent(R, swap, 1)))

    def dh_done():
        stream_back(R, 1)
        R.dh[...] = R.dhs[...]

    rest_middle = [last(lambda: middle_back(R, swap, 1))]
    rest_late = [
        last(lambda: attend_back(R, tables, 1, range(0, 4))),
        last(lambda: attend_back(R, tables, 1, range(4, 7))),
        last(dh_done),
    ]
    made = set()
    start_scatter(wire, place, bufs, rest[:N_RS_SCRATCH], made, lambda *a: keep(R, *a))
    wire.add(weight_grads(R, wire, made, (rest_early, rest_middle, rest_late), far_first(place, "x")))
    wire.run()
    wire.drain()
    for m in range(MICRO):
        swap.n2(m).wait_send()
        swap.dy(m).wait_send()

    @only(0)
    def _():
        for m in range(MICRO):
            swap.hop_h(m).wait_send()

    @only(1)
    def _():
        for m in range(MICRO):
            for move in (swap.og, swap.cos, swap.sin, swap.mask, swap.y, swap.dh, swap.hop_dy):
                move(m).wait_send()
            swap.y(m).wait_recv()
            swap.dh(m).wait_recv()


N_WIRE = 208


def run_layers(ins):
    outs = [(TOK, D)] * 2 + [(2, 16, FF)] * 2 + [(80, D), (16, QKV), (16, D)]
    kinds = [BF] * 7
    vmem = pl.BlockSpec(memory_space=pltpu.VMEM)
    dma = pltpu.SemaphoreType.DMA
    return pl.pallas_call(
        layers_kernel,
        out_shape=[jax.ShapeDtypeStruct(s, k) for s, k in zip(outs, kinds)],
        in_specs=[pl.BlockSpec(memory_space=pl.ANY) if n in IN_HBM else vmem for n in INS],
        out_specs=[vmem] * len(OUTS),
        scratch_shapes=[pltpu.VMEM(s, BF) for s in bufs_shapes()]
        + [pltpu.VMEM(s, k) for _, s, k in LOCAL]
        + rs_scratch()
        + [dma((N_WIRE,)), dma((N_WIRE,)), dma((9,)), dma((N_SWAP,)), dma((N_SWAP,))],
        compiler_params=pltpu.CompilerParams(
            collective_id=0, has_side_effects=True, vmem_limit_bytes=127 * 2**19
        ),
        name="two_layers",
    )(*ins)


def rope_tables(segment_row, head_size):
    length = segment_row.shape[0]
    places = jnp.arange(length, dtype=jnp.int32)
    changes = jnp.concatenate(
        [jnp.ones((1,), jnp.int32), (segment_row[1:] != segment_row[:-1]).astype(jnp.int32)]
    )
    starts = lax.cummax(places * changes, axis=0)
    offsets = (places - starts).astype(F32)
    ladder = jnp.arange(head_size // 2, dtype=F32) * (-2.0 * math.log(rope_base) / head_size)
    angles = offsets[:, None] * jnp.exp(ladder)[None, :]
    cos, sin = jnp.cos(angles), jnp.sin(angles)
    return (
        jnp.concatenate([cos, cos, cos, cos], axis=-1),
        jnp.concatenate([-sin, sin, -sin, sin], axis=-1),
    )


def mask_of(segment_row):
    places = jnp.arange(segment_row.shape[0], dtype=jnp.int32)
    seen = (segment_row[:, None] == segment_row[None, :]) & (places[None, :] <= places[:, None])
    return jnp.where(seen, 0.0, -1e30).astype(F32)


def shards(
    tokens_in, out_grad, segments, norm1_gain, qkv_weight, qkv_bias, out_weight, norm2_gain,
    gate_weight, up_weight, down_weight,
):
    half = MICRO * SEQ
    rows = segments[:, 0]
    cos, sin = jax.vmap(rope_tables, in_axes=(0, None))(rows, HEAD_DIM)
    parts = run_layers([
        gate_weight[0],
        up_weight[0],
        down_weight[0],
        qkv_weight[0],
        out_weight[0],
        norm1_gain,
        qkv_bias,
        norm2_gain,
        tokens_in.reshape(half, D),
        out_grad.reshape(half, D),
        cos.reshape(half, 128),
        sin.reshape(half, 128),
        jax.vmap(mask_of)(rows),
        *constants(),
    ])
    shape = (1, MICRO, 1, SEQ, D)
    y, dh, a, q, b, o, c, g, u, d = finish_grads(parts)
    q, o, g, u, d = [part.transpose(1, 0, 2) for part in (q, o, g, u, d)]
    return y.reshape(shape), dh.reshape(shape), a, q, b, o, c, g, u, d


def solution(mesh):
    in_specs = (
        P(None, "fsdp", None, None),
        P(None, "fsdp", None, None),
        P(None, "fsdp", None),
        P("section", "fsdp"),
        P("section", "fsdp", None),
        P("section", "fsdp"),
        P("section", "fsdp", None),
        P("section", "fsdp"),
        P("section", "fsdp", None),
        P("section", "fsdp", None),
        P("section", "fsdp", None),
    )
    out_specs = (
        P("section", None, "fsdp", None, None),
        P("section", None, "fsdp", None, None),
        P("section", "fsdp"),
        P("section", "fsdp", None),
        P("section", "fsdp"),
        P("section", "fsdp", None),
        P("section", "fsdp"),
        P("section", "fsdp", None),
        P("section", "fsdp", None),
        P("section", "fsdp", None),
    )
    return jax.shard_map(shards, mesh=mesh, in_specs=in_specs, out_specs=out_specs, check_vma=False)
```
